32 devices in a mesh: seq: 8 (over z, x), dp: 4 (over y, core).
Axes of the slice: x: 2, y: 2, z: 4, core: 2. Of those that a mesh axis runs over, the one named last changes fastest.
Arguments:
- inputs: bfloat16 [16, 1024, 768], P('dp', 'seq'), may hold values from -6 to 6
- lengths: int32 [16], P('dp'), may hold values from 1 to 1024, as said below
- norm_gain: float32 [768], replicated, may hold values from 0.25 to 1.75
- norm_bias: float32 [768], replicated, may hold values from -3 to 3
- mixer_in: bfloat16 [768, 2304], replicated, may hold values from -0.21875 to 0.21875
- filter_in: float32 [33, 64], replicated, may hold values from -64 to 64
- filter_in_bias: float32 [64], replicated, may hold values from -3.140625 to 3.140625
- filter_mid: float32 [64, 64], replicated, may hold values from -0.75 to 0.75
- filter_mid_bias: float32 [64], replicated, may hold values from -3.140625 to 3.140625
- filter_out: float32 [64, 768], replicated, may hold values from -0.03125 to 0.03125
- mixer_out: bfloat16 [768, 768], replicated, may hold values from -0.21875 to 0.21875
- second_gain: float32 [768], replicated, may hold values from 0.25 to 1.75
- second_bias: float32 [768], replicated, may hold values from -3 to 3
- up_weight: bfloat16 [768, 3072], replicated, may hold values from -0.21875 to 0.21875
- down_weight: bfloat16 [3072, 768], replicated, may hold values from -0.109375 to 0.109375
- cotangent: bfloat16 [16, 1024, 768], P('dp', 'seq'), may hold values from -6 to 6
Outputs:
- output: bfloat16 [16, 1024, 768], P('dp', 'seq')
- grad_inputs: float32 [16, 1024, 768], P('dp', 'seq')
- grad_norm_gain: float32 [768], replicated
- grad_norm_bias: float32 [768], replicated
- grad_mixer_in: float32 [768, 2304], replicated
- grad_filter_in: float32 [33, 64], replicated
- grad_filter_in_bias: float32 [64], replicated
- grad_filter_mid: float32 [64, 64], replicated
- grad_filter_mid_bias: float32 [64], replicated
- grad_filter_out: float32 [64, 768], replicated
- grad_mixer_out: float32 [768, 768], replicated
- grad_second_gain: float32 [768], replicated
- grad_second_bias: float32 [768], replicated
- grad_up_weight: float32 [768, 3072], replicated
- grad_down_weight: float32 [3072, 768], replicated
The draws below stay inside these ranges and needn't reach their ends.
Inputs may be any that keep to these rules, and one draw needn't show every extreme that they name: `lengths`: in every aligned block of 4 sequences (those of one index of dp) at least one sequence has length 1024.
All inputs are finite; a program needn't handle non-finite values.
Results may differ from the reference program's by a relative error of at most 0.012.
Values may be sent and summed in bfloat16 or wider, within the bound.
No kernel may reach another device: no remote copies, remote signals or barrier semaphores. Data moves between devices by JAX's collectives and lax.ppermute only.
A program may use at most 256 MiB of HBM per device.

```python
import math
import jax
import jax.numpy as jnp
from jax import lax

D = 768
FF = 3072
KL = 2048
FORDER = 64
BANDS = 16
EMB = 33
SEQ_DP = 4
SEQS = 16
LEN = 1024


def draw_lengths(key, part):
    key = jax.random.fold_in(key, 7)
    first_key, second_key = jax.random.split(key)
    drawn = jax.random.randint(first_key, (SEQS,), 1, LEN + 1)
    chosen = jax.random.randint(second_key, (SEQS // SEQ_DP, 1), 0, SEQ_DP)
    slots = jnp.arange(SEQ_DP, dtype=jnp.int32)[None, :]
    full_seq = (slots == chosen).reshape(SEQS)
    return jnp.where(full_seq, LEN, drawn).astype(jnp.int32)


def steps_of(stream_key, shape, shards, least, high):
    level = 1.0
    for dim, parts in shards:
        steps = jax.random.uniform(jax.random.fold_in(jax.random.fold_in(stream_key, 6), dim), (parts,), jnp.float32, least / len(shards), high / len(shards))
        level = level * jnp.repeat(jnp.exp(steps), shape[dim] // parts).reshape((-1,) + (1,) * (len(shape) - 1 - dim))
    return level


def normal_values(own_key, shape, scale, limit, shards=(), kind=jnp.bfloat16):
    values = scale * jax.random.normal(own_key, shape, jnp.float32)
    if shards:
        values = values * steps_of(own_key, shape, shards, -0.22, 0.18)
    return jnp.clip(values, -limit, limit).astype(kind)


def setup_inputs(seed: int = 0) -> dict:
    seeds = jax.random.split(jax.random.key(seed), 17)
    return {
        "inputs": normal_values(seeds[0], (SEQS, LEN, D), 1.0, 6.0, ((0, 4), (1, 8))),
        "lengths": draw_lengths(jax.random.fold_in(seeds[16], 71), 0),
        "norm_gain": jnp.clip(1.0 + 0.15 * jax.random.normal(seeds[2], (D,), jnp.float32), 0.25, 1.75),
        "norm_bias": normal_values(seeds[3], (D,), 0.3, 3.0, (), jnp.float32),
        "mixer_in": normal_values(seeds[4], (D, 3 * D), D ** -0.5, 0.21875),
        "filter_in": normal_values(seeds[5], (EMB, FORDER), 16.0, 64.0, (), jnp.float32),
        "filter_in_bias": jnp.clip(jax.random.uniform(seeds[6], (FORDER,), jnp.float32, -3.140625, 3.140625), -3.140625, 3.140625),
        "filter_mid": normal_values(seeds[7], (FORDER, FORDER), FORDER ** -0.5, 0.75, (), jnp.float32),
        "filter_mid_bias": jnp.clip(jax.random.uniform(seeds[8], (FORDER,), jnp.float32, -3.140625, 3.140625), -3.140625, 3.140625),
        "filter_out": normal_values(seeds[9], (FORDER, D), (FORDER * KL // 4) ** -0.5, 0.03125, (), jnp.float32),
        "mixer_out": normal_values(seeds[10], (D, D), D ** -0.5, 0.21875),
        "second_gain": jnp.clip(1.0 + 0.15 * jax.random.normal(seeds[11], (D,), jnp.float32), 0.25, 1.75),
        "second_bias": normal_values(seeds[12], (D,), 0.3, 3.0, (), jnp.float32),
        "up_weight": normal_values(seeds[13], (D, FF), D ** -0.5, 0.21875),
        "down_weight": normal_values(seeds[14], (FF, D), FF ** -0.5, 0.109375),
        "cotangent": normal_values(seeds[15], (SEQS, LEN, D), 1.0, 6.0, ((0, 4), (1, 8))),
    }


@jax.custom_vjp
def low(v):
    return lax.optimization_barrier(v.astype(jnp.bfloat16)).astype(jnp.float32)

@jax.custom_vjp
def low_back(v):
    return v

def low_keep(v):
    return (low(v), None)

def low_pass(kept, grad):
    return (grad,)

def back_keep(v):
    return (v, None)

def back_low(kept, grad):
    return (low(grad),)
low.defvjp(low_keep, low_pass)
low_back.defvjp(back_keep, back_low)

def matmul(left, right):
    return jnp.dot(left, right, precision=lax.Precision.HIGHEST, preferred_element_type=jnp.float32)

def layer_norm(values, gain, shift):
    center = values - lax.optimization_barrier(jnp.mean(values, axis=-1, keepdims=True))
    spread = lax.optimization_barrier(jnp.mean(center * center, axis=-1, keepdims=True))
    return center * lax.rsqrt(spread + 1e-05) * gain + shift

def feature_table():
    steps = jnp.arange(KL, dtype=jnp.float32) / KL
    freqs = jnp.arange(1, BANDS + 1, dtype=jnp.float32)
    phase = 2.0 * math.pi * steps[:, None] * freqs[None, :]
    return jnp.concatenate([steps[:, None], jnp.cos(phase), jnp.sin(phase)], axis=1)

def filter_kernel(filter_in, filter_in_bias, filter_mid, filter_mid_bias, filter_out):
    table = feature_table()
    first = jnp.sin(matmul(table, filter_in) + filter_in_bias)
    second = jnp.sin(matmul(first, filter_mid) + filter_mid_bias)
    return matmul(second, filter_out)

def long_conv(gated, kernel):
    total = LEN + KL
    spectrum = jnp.fft.rfft(gated, n=total, axis=0) * jnp.fft.rfft(kernel, n=total, axis=0)
    return jnp.fft.irfft(spectrum, n=total, axis=0)[:LEN]

def block(values, mask, norm_gain, norm_bias, mixer_in, kernel, mixer_out, second_gain, second_bias, up_weight, down_weight):
    normed = low(layer_norm(values, norm_gain, norm_bias))
    projected = low_back(matmul(normed, mixer_in))
    value = projected[:, :D]
    gate_a = projected[:, D:2 * D]
    gate_b = projected[:, 2 * D:]
    gated = low(value * gate_a) * mask
    mixed = low_back(long_conv(gated, kernel))
    gated_out = low(gate_b * mixed)
    middle = values + low_back(matmul(gated_out, mixer_out))
    second_normed = low(layer_norm(middle, second_gain, second_bias))
    pre = low_back(matmul(second_normed, up_weight))
    activated = low(jax.nn.gelu(pre, approximate=True))
    return middle + low_back(matmul(activated, down_weight))

def reference(inputs, lengths, norm_gain, norm_bias, mixer_in, filter_in, filter_in_bias, filter_mid, filter_mid_bias, filter_out, mixer_out, second_gain, second_bias, up_weight, down_weight, cotangent):
    valid = (jnp.arange(LEN, dtype=jnp.int32)[None, :] < lengths[:, None]).astype(jnp.float32)[:, :, None]

    def forward(values, ngain, nbias, minw, fin, fib, fmid, fmb, fout, moutw, sgain, sbias, upw, downw):
        kernel = filter_kernel(fin, fib, fmid, fmb, fout)

        def step(carry, item):
            return (carry, block(item[0], item[1], ngain, nbias, minw, kernel, moutw, sgain, sbias, upw, downw))
        _, outs = lax.scan(jax.checkpoint(step), None, (values, valid))
        return outs
    result, backward = jax.vjp(forward, inputs.astype(jnp.float32), norm_gain, norm_bias, mixer_in.astype(jnp.float32), filter_in, filter_in_bias, filter_mid, filter_mid_bias, filter_out, mixer_out.astype(jnp.float32), second_gain, second_bias, up_weight.astype(jnp.float32), down_weight.astype(jnp.float32))
    g_inputs, g_ngain, g_nbias, g_min, g_fin, g_fib, g_fmid, g_fmb, g_fout, g_mout, g_sgain, g_sbias, g_up, g_down = backward(cotangent.astype(jnp.float32))
    return (result.astype(jnp.bfloat16), g_inputs, g_ngain, g_nbias, g_min, g_fin, g_fib, g_fmid, g_fmb, g_fout, g_mout, g_sgain, g_sbias, g_up, g_down)
```

```python
import math

import jax
import jax.numpy as jnp
import numpy as np
from jax import lax
from jax.experimental import pallas as pl
from jax.experimental.pallas import tpu as pltpu
from jax.sharding import PartitionSpec as P

AX = ("seq", "dp")
HIGH = lax.Precision.HIGHEST
EPSILON = 1e-05
BANDS = 16
KL = 2048
F32 = jnp.float32
BF16 = jnp.bfloat16


def mm(a, b, ca=1, cb=0):
    return lax.dot_general(a, b, (((ca,), (cb,)), ((), ())), preferred_element_type=F32)


def perm_of(f):
    pairs = []
    for z in range(4):
        for x in range(2):
            for y in range(2):
                for c in range(2):
                    a, b, d, e = f(z, x, y, c)
                    pairs.append(((z * 2 + x) * 4 + y * 2 + c, (a * 2 + b) * 4 + d * 2 + e))
    return pairs


PC = perm_of(lambda z, x, y, c: (z, x, y, 1 - c))
PX = perm_of(lambda z, x, y, c: (z, 1 - x, y, c))
PY = perm_of(lambda z, x, y, c: (z, x, 1 - y, c))
PZ = [perm_of(lambda z, x, y, c, k=k: (z ^ k, x, y, c)) for k in range(4)]


def send(v, perm):
    return lax.ppermute(v, AX, perm)


def tie(*vals):
    return lax.optimization_barrier(tuple(vals))


def swap_in(v, c):
    v = v.reshape(4, 2, 64, v.shape[-1])
    keep = pick(v, c, 1)
    got = send(pick(v, 1 - c, 1), PC)
    return jnp.where(c == 0, jnp.concatenate([keep, got]), jnp.concatenate([got, keep]))


def exchange_seq(v):
    return lax.all_to_all(v, "seq", 0, 0)


def swap_out(v, c):
    v = v.reshape(2, 4, 64, v.shape[-1])
    keep = pick(v, c)
    got = send(pick(v, 1 - c), PC)
    m = jnp.stack([jnp.where(c == 0, keep, got), jnp.where(c == 0, got, keep)], axis=1)
    return m.reshape(4, 128, v.shape[-1])


def both(own, c):
    other = send(own, PC)
    return jnp.stack([jnp.where(c == 0, own, other), jnp.where(c == 0, other, own)], axis=1)


def feature_table(taps):
    steps = np.arange(taps, dtype=np.float64) / KL
    freqs = np.arange(1, BANDS + 1, dtype=np.float64)
    phase = 2.0 * math.pi * steps[:, None] * freqs[None, :]
    return np.concatenate([steps[:, None], np.cos(phase), np.sin(phase)], axis=1).astype(np.float32)


def dft_table(length):
    f = 2 * np.arange(length, dtype=np.int64)[:, None] + 1
    n = np.arange(length, dtype=np.int64)[None, :]
    angle = (f * n % (4 * length)) * (2.0 * math.pi / (4 * length))
    return np.concatenate([np.cos(angle), -np.sin(angle)], axis=0).astype(np.float32)


def norm_parts(v):
    center = v - jnp.mean(v, axis=-1, keepdims=True)
    spread_ = jnp.mean(center * center, axis=-1, keepdims=True)
    inv = lax.rsqrt(spread_ + EPSILON)
    return center * inv, inv


def norm_back(q, hat, inv):
    return (q - jnp.mean(q, -1, keepdims=True) - hat * jnp.mean(q * hat, -1, keepdims=True)) * inv


def lanes(a, at, size):
    return lax.dynamic_slice_in_dim(a, at, size, axis=1)


def in_order(bit, own, other, axis=0):
    first = jnp.where(bit == 0, own, other)
    second = jnp.where(bit == 0, other, own)
    return jnp.concatenate([first, second], axis=axis)


def pick(a, i, axis=0):
    return lax.dynamic_index_in_dim(a, i, axis, keepdims=False)


class Reducer:
    def __init__(self, sends, keeps, z, x, y):
        self.pos, self.z0, self.z1 = (x, y), z & 1, z >> 1
        self.sends, self.keeps = sends, keeps
        self.cols = keeps[0].shape[1]
        self.r = keeps[0].shape[0] // 8

    def start1(self):
        self.got = (send(self.sends[0], PX), send(self.sends[1], PY))

    def start2(self):
        pos = self.pos[::-1]
        sums = [k + g.astype(F32) for k, g in zip(self.keeps, self.got)]
        sums = [s.reshape(2, 4 * self.r, self.cols) for s in sums]
        self.keeps = [pick(s, p) for s, p in zip(sums, pos)]
        out = [pick(s, 1 - p).astype(BF16) for s, p in zip(sums, pos)]
        self.got = (send(out[0], PY), send(out[1], PX))

    def start3(self):
        sums = [k + g.astype(F32) for k, g in zip(self.keeps, self.got)]
        w = [s.reshape(2, 2 * self.r, self.cols) for s in sums]
        self.keeps = jnp.stack([pick(v, self.z0) for v in w])
        self.got = (send(jnp.stack([pick(v, 1 - self.z0).astype(BF16) for v in w]), PZ[1]),)

    def start4(self):
        w = self.keeps + self.got[0].astype(F32)
        w = w.reshape(2, 2, self.r, self.cols)
        self.keeps = pick(w, self.z1, 1)
        self.got = (send(pick(w, 1 - self.z1, 1).astype(BF16), PZ[2]),)

    def start5(self):
        self.total = (self.keeps + self.got[0].astype(F32)).astype(BF16)
        self.got = (send(self.total, PZ[2]),)

    def start6(self):
        self.total = in_order(self.z1, self.total, self.got[0], 1)
        self.got = (send(self.total, PZ[1]),)

    def start7(self):
        v = in_order(self.z0, self.total, self.got[0], 1)
        self.own = [v[0], v[1]]
        self.got = (send(v[0], PY), send(v[1], PX))

    def start8(self):
        pos = self.pos[::-1]
        self.near = [in_order(p, o, g) for p, o, g in zip(pos, self.own, self.got)]
        self.got = (send(self.near[0], PX), send(self.near[1], PY))
        self.pair_near = [send(v, PC) for v in self.near]

    def start9(self):
        self.far = list(self.got)
        self.pair_far = [send(v, PC) for v in self.far]


def write(bufs, sources, spots, moves):
    n, m = len(sources), len(bufs)
    rows, cols = sources[0].shape
    each = len(moves(0, [0] * spots.shape[1]))

    def body(*refs):
        spot = refs[0]
        src, out, wide, sem = refs[1 : 1 + n], refs[1 + n + m : 1 + n + 2 * m], refs[-2], refs[-1]
        copies = []
        for k in range(n):
            wide[k] = src[k][...].astype(F32)
            for q, (b, i, j, at, size) in enumerate(moves(k, [spot[k, e] for e in range(spots.shape[1])])):
                copy = pltpu.make_async_copy(
                    wide.at[k, :, pl.ds(at, size)],
                    out[b].at[pl.ds(pl.multiple_of(i, 8), rows), pl.ds(pl.multiple_of(j, 128), size)],
                    sem.at[k, q],
                )
                copy.start()
                copies.append(copy)
        for copy in copies:
            copy.wait()

    return pl.pallas_call(
        body,
        in_specs=[pl.BlockSpec(memory_space=pltpu.SMEM)]
        + [pl.BlockSpec(memory_space=pltpu.VMEM)] * n
        + [pl.BlockSpec(memory_space=pl.ANY)] * m,
        out_specs=[pl.BlockSpec(memory_space=pl.ANY)] * m,
        out_shape=[jax.ShapeDtypeStruct(b.shape, F32) for b in bufs],
        input_output_aliases={1 + n + b: b for b in range(m)},
        scratch_shapes=[pltpu.VMEM((n, rows, cols), F32), pltpu.SemaphoreType.DMA((n, each))],
        compiler_params=pltpu.CompilerParams(vmem_limit_bytes=32 * 2**20),
    )(spots, *sources, *bufs)


def fresh(*shapes):
    def body(*refs):
        pass

    return pl.pallas_call(
        body,
        out_specs=[pl.BlockSpec(memory_space=pl.ANY)] * len(shapes),
        out_shape=[jax.ShapeDtypeStruct(s, F32) for s in shapes],
    )()


def write_down(k, s):
    return [(0, s[0] * 1536 + s[1] * 768 + s[2] * 384, 0, 0, 768)]


def write_up(k, s):
    return [(0, s[1] * 384 + s[2] * 192, s[0] * 1536, 0, 1536)]


def write_mix(k, s):
    moves = [(0, s[1] * 384 + s[2] * 192, g * 768 + s[0] * 384, g * 384, 384) for g in range(3)]
    return moves + [(1, s[0] * 384 + s[2] * 192, s[1] * 384, 1152, 384)]


def hold(reducer, *vals):
    n = len(reducer.got)
    out = tie(*reducer.got, *vals)
    reducer.got = tuple(out[:n])
    return out[n] if len(vals) == 1 else out[n:]


GELU_A = math.sqrt(2.0 / math.pi)
GELU_B = 0.044715


def gelu_pair(v):
    sq = v * v
    t = jnp.tanh(GELU_A * v * (1.0 + GELU_B * sq))
    up = 0.5 * (1.0 + t)
    return v * up, up + 0.5 * v * (1.0 - t * t) * (GELU_A * (1.0 + 3.0 * GELU_B * sq))


def chip_local(
    inputs, lengths, norm_gain, norm_bias, mixer_in, filter_in, filter_in_bias, filter_mid, filter_mid_bias,
    filter_out, mixer_out, second_gain, second_bias, up_weight, down_weight, cotangent,
):
    s = lax.axis_index("seq")
    d = lax.axis_index("dp")
    z, x, y, c = s // 2, s % 2, d // 2, d % 2
    width = inputs.shape[-1]
    rows = 8 * inputs.shape[1]
    half = width // 2
    ff = up_weight.shape[1] // 2
    x_half = exchange_seq(swap_in(inputs, c))
    other_len = send(lengths, PC)
    length = pick(jnp.where(c == (z >> 1), lengths, other_len), (z & 1) * 2 + x)
    valid = (jnp.arange(rows, dtype=jnp.int32) < length).astype(F32)[:, None]
    cot_half = swap_in(cotangent, c)
    zero = 0 * c
    near = jnp.stack([jnp.stack(v) for v in ((c, zero, x), (c, zero + 1, y), (1 - c, zero, x), (1 - c, zero + 1, y))])
    far = jnp.stack(
        [jnp.stack(v) for v in ((c, zero, 1 - x), (c, zero + 1, 1 - y), (1 - c, zero, 1 - x), (1 - c, zero + 1, 1 - y))]
    )
    w_in = jnp.concatenate([lanes(mixer_in, g * width + c * half, half) for g in range(3)], axis=1)
    w_mo = lax.dynamic_slice_in_dim(mixer_out, c * half, half, 0)
    w_up = lanes(up_weight, c * ff, ff)
    w_dn = lax.dynamic_slice_in_dim(down_weight, c * ff, ff, 0)
    f_out = lanes(filter_out, c * half, half)
    table = jnp.asarray(dft_table(rows), BF16)
    feats = jnp.asarray(feature_table(rows))
    first_act = jnp.dot(feats, filter_in, precision=HIGH) + filter_in_bias
    h1 = jnp.sin(first_act)
    second_act = jnp.dot(h1, filter_mid, precision=HIGH) + filter_mid_bias
    h2 = jnp.sin(second_act)
    h2_hi = h2.astype(BF16)
    h2_lo = (h2 - h2_hi.astype(F32)).astype(BF16)
    hf = mm(table, jnp.concatenate([h2_hi, h2_lo], axis=1))
    hf = (hf[:, :64] + hf[:, 64:]) * (1.0 / rows)
    k = jnp.dot(hf, f_out, precision=HIGH)
    x_half, k, w_in, w_mo, w_up, w_dn, cot_half, valid, near, far = tie(
        x_half, k, w_in, w_mo, w_up, w_dn, cot_half, valid, near, far
    )
    cot_half = exchange_seq(cot_half)
    k_re, k_im = k[:rows], k[rows:]
    x_full = both(x_half, c).reshape(rows, width)
    xf = x_full.astype(F32)
    hat1, inv1 = norm_parts(xf)
    normed = (hat1 * norm_gain + norm_bias).astype(BF16)
    proj = mm(normed, w_in)
    value, gate_a, gate_b = proj[:, :half], proj[:, half : 2 * half], proj[:, 2 * half :]
    gated = (value * gate_a).astype(BF16) * valid.astype(BF16)
    zf = mm(table, gated)
    z_re, z_im = zf[:rows], zf[rows:]
    yf = jnp.concatenate([k_re * z_re - k_im * z_im, k_re * z_im + k_im * z_re]).astype(BF16)
    mixed = mm(table, yf, 0, 0)
    gated_out = (gate_b * mixed).astype(BF16)
    part = mm(gated_out, w_mo)
    middle = xf + part + send(part.astype(BF16), PC).astype(F32)
    hat2, inv2 = norm_parts(middle)
    second_normed = (hat2 * second_gain + second_bias).astype(BF16)
    activated, dgelu = gelu_pair(mm(second_normed, w_up))
    activated, dgelu = activated.astype(BF16), dgelu.astype(BF16)
    cot = both(cot_half, c).reshape(rows, width)
    g_down = mm(activated, cot, 0, 0).reshape(2, 2, ff // 4, width)
    down = Reducer(
        [pick(g_down[0], 1 - x).astype(BF16), pick(g_down[1], 1 - y).astype(BF16)],
        [pick(g_down[0], x), pick(g_down[1], y)], z, x, y,
    )
    down.start1()
    d_pre = (mm(cot, w_dn, 1, 1) * dgelu.astype(F32)).astype(BF16)
    g_up = mm(second_normed, d_pre, 0, 0).reshape(2, 2, half // 2, ff)
    up = Reducer(
        [pick(g_up[0], 1 - x).astype(BF16), pick(g_up[1], 1 - y).astype(BF16)],
        [pick(g_up[0], x), pick(g_up[1], y)], z, x, y,
    )
    up.start1()
    d_second_part = mm(d_pre, w_up, 1, 1)
    d_second_part = hold(down, d_second_part)
    down.start2()
    g_second_bias = jnp.sum(d_second_part, axis=0)
    g_second_gain = jnp.sum(d_second_part * hat2, axis=0)
    d_second = d_second_part + send(d_second_part.astype(BF16), PC).astype(F32)
    d_middle = cot.astype(F32) + norm_back(d_second * second_gain, hat2, inv2)
    d_middle_low = d_middle.astype(BF16)
    d_go = mm(d_middle_low, w_mo, 1, 1)
    d_gate_b = (d_go * mixed).astype(BF16)
    d_mixed = (d_go * gate_b).astype(BF16)
    d_mixed = hold(up, d_mixed)
    up.start2()
    df = mm(table, d_mixed)
    d_re, d_im = df[:rows], df[rows:]
    gf = jnp.concatenate([k_re * d_re + k_im * d_im, k_re * d_im - k_im * d_re]).astype(BF16)
    gf = hold(down, gf)
    down.start3()
    d_gated = mm(table, gf, 0, 0) * valid
    d_proj = jnp.concatenate([(d_gated * gate_a).astype(BF16), (d_gated * value).astype(BF16), d_gate_b], axis=1)
    g_in = mm(normed, d_proj, 0, 0).reshape(2, 2, half // 2, 3 * half)
    g_mo = mm(gated_out, d_middle_low, 0, 0)
    g_mo = [g_mo[:, :half].reshape(2, half // 2, half), g_mo[:, half:].reshape(2, half // 2, half)]

    def mix_part(n, i):
        return jnp.concatenate([pick(g_in[n], i), pick(g_mo[n], i)], axis=1)

    mix = Reducer(
        [mix_part(0, 1 - x).astype(BF16), mix_part(1, 1 - y).astype(BF16)],
        [mix_part(0, x), mix_part(1, y)], z, x, y,
    )
    mix.start1()
    d_proj = hold(up, d_proj)
    up.start3()
    d_proj = hold(down, d_proj)
    down.start4()
    d_normed_part = mm(d_proj, w_in, 1, 1)
    d_normed_part = hold(down, d_normed_part)
    down.start5()
    d_normed_part = hold(up, d_normed_part)
    up.start4()
    g_norm_bias = jnp.sum(d_normed_part, axis=0)
    g_norm_gain = jnp.sum(d_normed_part * hat1, axis=0)
    dn = d_normed_part.reshape(8, 2, 64, width)
    dn_own = pick(dn, c, 1) + send(pick(dn, 1 - c, 1).astype(BF16), PC).astype(F32)
    hat1_own = pick(hat1.reshape(8, 2, 64, width), c, 1)
    inv1_own = pick(inv1.reshape(8, 2, 64, 1), c, 1)
    dx = pick(d_middle.reshape(8, 2, 64, width), c, 1) + norm_back(dn_own * norm_gain, hat1_own, inv1_own)
    out_part = mm(activated, w_dn).reshape(8, 2, 64, width)
    middle_own = pick(middle.reshape(8, 2, 64, width), c, 1)
    out_own = middle_own + pick(out_part, c, 1) + send(pick(out_part, 1 - c, 1).astype(BF16), PC).astype(F32)
    back = jnp.concatenate([out_own.astype(BF16), dx.astype(BF16)], axis=2)
    back = swap_out(exchange_seq(back), c)
    output, grad_inputs = back[..., :width], back[..., width:].astype(F32)
    tf = jnp.concatenate([z_re * d_re + z_im * d_im, z_re * d_im - z_im * d_re]) * (1.0 / rows)
    tf_low = tf.astype(BF16)
    g_fo = mm(hf.astype(BF16), tf_low, 0, 0) * rows
    kf = mm(tf_low, f_out.astype(BF16), 1, 1)
    d_h2 = mm(table, kf.astype(BF16), 0, 0)
    d_s = jnp.cos(second_act) * d_h2
    g_fm = jnp.dot(h1.T, d_s, precision=HIGH)
    g_fmb = jnp.sum(d_s, axis=0)
    d_f = jnp.cos(first_act) * jnp.dot(d_s, filter_mid.T, precision=HIGH)
    g_fi = jnp.dot(feats.T, d_f, precision=HIGH)
    g_fib = jnp.sum(d_f, axis=0)
    zero = jnp.zeros_like(g_fo)
    g_fo_full = jnp.concatenate([jnp.where(c == 0, g_fo, zero), jnp.where(c == 0, zero, g_fo)], axis=1)
    misc = jnp.concatenate([g_fm, g_fi, g_fmb[None], g_fib[None]])
    misc = jnp.pad(misc, ((0, 104 - misc.shape[0]), (0, 0)))
    misc = jnp.concatenate([misc[i * 8 : (i + 1) * 8] for i in range(13)], axis=1)
    misc = jnp.concatenate([misc[:, :416], misc[:, 416:]])
    misc = jnp.pad(misc, ((0, 0), (0, width - 416)))
    vecs = jnp.stack([g_norm_gain, g_norm_bias, g_second_gain, g_second_bias])
    vecs = jnp.pad(vecs, ((0, 4), (0, 0)))
    small = jnp.concatenate([g_fo_full, misc, vecs])
    for perm in (PC, PX, PY, PZ[1], PZ[2]):
        small = small + send(small, perm)
    misc = jnp.concatenate([small[64:72, :416], small[72:80, :416]], axis=1)
    misc = jnp.concatenate([misc[:, i * 64 : (i + 1) * 64] for i in range(13)])
    vecs = small[80:84]
    bufs = fresh(down_weight.shape, up_weight.shape, mixer_in.shape, mixer_out.shape)
    outs = []
    for reducer, first, mine, moves in (
        (down, 6, bufs[:1], write_down), (up, 5, bufs[1:2], write_up), (mix, 2, bufs[2:], write_mix),
    ):
        for n in range(first, 10):
            getattr(reducer, f"start{n}")()
        mine = write(mine, reducer.near + reducer.pair_near, near, moves)
        outs += write(mine, reducer.far + reducer.pair_far, far, moves)
    grad_down, grad_up, grad_in, grad_mo = outs
    return (
        output, grad_inputs, vecs[0], vecs[1], grad_in, misc[64:97], misc[98], misc[:64], misc[97],
        small[:64], grad_mo, vecs[2], vecs[3], grad_up, grad_down,
    )


LAGS = 16


def shifted(value, axis, by):
    devices = lax.axis_size(axis)
    pairs = [(i, i + by) for i in range(devices) if 0 <= i + by < devices]
    return lax.ppermute(value, axis, pairs)


def plain_norm(values, gain, shift):
    center = values - jnp.mean(values, axis=-1, keepdims=True)
    spread = jnp.mean(center * center, axis=-1, keepdims=True)
    return center * lax.rsqrt(spread + EPSILON) * gain + shift


def features_of(taps, bands):
    steps = jnp.arange(taps, dtype=jnp.float32) / taps
    freqs = jnp.arange(1, bands + 1, dtype=jnp.float32)
    phase = 2.0 * math.pi * steps[:, None] * freqs[None, :]
    return jnp.concatenate([steps[:, None], jnp.cos(phase), jnp.sin(phase)], axis=1)


def taps_of(filter_in, filter_in_bias, filter_mid, filter_mid_bias, filter_out):
    table = features_of(KL, BANDS)
    first = jnp.sin(jnp.dot(table, filter_in, precision=HIGH) + filter_in_bias)
    second = jnp.sin(jnp.dot(first, filter_mid, precision=HIGH) + filter_mid_bias)
    return jnp.dot(second, filter_out, precision=HIGH)


def wave_tables(block_len):
    length = 2 * block_len
    index = jnp.arange(length, dtype=jnp.int32)
    angle = (index[:, None] * index[None, :] % length).astype(jnp.float32) * (
        2.0 * math.pi / length
    )
    return (jnp.cos(angle), jnp.sin(angle))


def split_table(table):
    leading = table.astype(jnp.bfloat16)
    remainder = (table - leading.astype(jnp.float32)).astype(jnp.bfloat16)
    return (leading, remainder)


def low_tables(cos_t, sin_t):
    length = cos_t.shape[0]
    half = length // 2
    return (
        split_table(cos_t[:, :half]),
        split_table(sin_t[:, :half]),
        split_table(cos_t[half:] / length),
        split_table(sin_t[half:] / length),
    )


def apply_split(pattern, halves, values):
    first = jnp.einsum(pattern, halves[0], values, preferred_element_type=jnp.float32)
    second = jnp.einsum(pattern, halves[1], values, preferred_element_type=jnp.float32)
    return first + second


def kernel_freq(kernel, cos_t, sin_t):
    block_len = cos_t.shape[0] // 2
    width = kernel.shape[1]
    count = kernel.shape[0] // block_len
    padded = jnp.concatenate(
        [
            jnp.zeros((block_len, width), jnp.float32),
            kernel,
            jnp.zeros((2 * block_len, width), jnp.float32),
        ],
        axis=0,
    )
    pieces = padded.reshape(count + 3, block_len, width)
    segments = jnp.concatenate([pieces[: count + 1], pieces[1 : count + 2]], axis=1)
    real = jnp.einsum("fn,mnd->mfd", cos_t, segments, precision=HIGH)
    imag = -jnp.einsum("fn,mnd->mfd", sin_t, segments, precision=HIGH)
    return (real, imag)


def to_freq(values, tables):
    real = apply_split("fc,scd->sfd", tables[0], values)
    imag = -apply_split("fc,scd->sfd", tables[1], values)
    return (real, imag)


def from_freq(real, imag, cos_t, sin_t):
    length = cos_t.shape[0]
    half = length // 2
    first = jnp.einsum("nf,sfd->snd", cos_t[half:], real, precision=HIGH)
    second = jnp.einsum("nf,sfd->snd", sin_t[half:], imag, precision=HIGH)
    return (first - second) / length


def grad_freq(values, tables):
    real = apply_split("nf,snd->sfd", tables[2], values)
    imag = -apply_split("nf,snd->sfd", tables[3], values)
    return (real, imag)


def grad_time(real, imag, cos_t, sin_t):
    half = cos_t.shape[0] // 2
    first = jnp.einsum("fc,sfd->scd", cos_t[:, :half], real, precision=HIGH)
    second = jnp.einsum("fc,sfd->scd", sin_t[:, :half], imag, precision=HIGH)
    return first - second


def add_forward(acc, k_real, k_imag, values, tables):
    z_real, z_imag = to_freq(values, tables)
    return (acc[0] + k_real * z_real - k_imag * z_imag, acc[1] + k_real * z_imag + k_imag * z_real)


def add_backward(acc, k_real, k_imag, grads, own_real, own_imag, tables):
    d_real, d_imag = grad_freq(grads, tables)
    new_real = acc[0] + k_real * d_real + k_imag * d_imag
    new_imag = acc[1] - k_imag * d_real + k_real * d_imag
    term_real = jnp.sum(own_real * d_real + own_imag * d_imag, axis=0)
    term_imag = jnp.sum(own_real * d_imag - own_imag * d_real, axis=0)
    return ((new_real, new_imag), (term_real, term_imag))


def forward_stack(stack, k_real, k_imag, acc, tables):

    def forward_step(carry, item):
        return (add_forward(carry, item[1], item[2], item[0], tables), None)

    result, _ = lax.scan(forward_step, acc, (stack, k_real, k_imag))
    return result


def backward_stack(stack, k_real, k_imag, acc, own_real, own_imag, tables):

    def backward_step(carry, item):
        return add_backward(carry, item[1], item[2], item[0], own_real, own_imag, tables)

    return lax.scan(backward_step, acc, (stack, k_real, k_imag))


def sum_everywhere(parts):
    flat_grads = jnp.concatenate([piece.reshape(-1) for piece in parts])
    portion = lax.psum_scatter(flat_grads, ("seq", "dp"), scatter_dimension=0, tiled=True)
    summed = lax.all_gather(portion.astype(jnp.bfloat16), ("seq", "dp"), axis=0, tiled=True).astype(
        portion.dtype
    )
    results = []
    offset = 0
    for piece in parts:
        results.append(summed[offset : offset + piece.size].reshape(piece.shape))
        offset = offset + piece.size
    return results


def block_local(
    inputs,
    lengths,
    norm_gain,
    norm_bias,
    mixer_in,
    filter_in,
    filter_in_bias,
    filter_mid,
    filter_mid_bias,
    filter_out,
    mixer_out,
    second_gain,
    second_bias,
    up_weight,
    down_weight,
    cotangent,
):
    seqs, block_len, width = inputs.shape
    row_count = seqs * block_len
    reach = min(LAGS, lax.axis_size("seq") - 1)
    rank = lax.axis_index("seq")
    position = rank * block_len + jnp.arange(block_len, dtype=jnp.int32)
    valid = (position[None, :] < lengths[:, None]).astype(jnp.float32)[:, :, None]
    cos_t, sin_t = wave_tables(block_len)
    tables = low_tables(cos_t, sin_t)
    kernel, filter_back = jax.vjp(
        taps_of, filter_in, filter_in_bias, filter_mid, filter_mid_bias, filter_out
    )
    k_real, k_imag = kernel_freq(kernel, cos_t, sin_t)
    x_full = inputs.astype(jnp.float32).reshape(row_count, width)
    normed = plain_norm(x_full, norm_gain, norm_bias).astype(jnp.bfloat16)
    projected = jnp.dot(normed, mixer_in, preferred_element_type=jnp.float32)
    value = projected[:, :width]
    gate_a = projected[:, width : 2 * width]
    gate_b = projected[:, 2 * width :]
    gated = (value * gate_a).astype(jnp.bfloat16).reshape(seqs, block_len, width) * valid.astype(
        jnp.bfloat16
    )
    own_real, own_imag = to_freq(gated, tables)
    initial = (
        k_real[0] * own_real - k_imag[0] * own_imag,
        k_real[0] * own_imag + k_imag[0] * own_real,
    )
    earlier = []
    for lag in range(1, reach + 1):
        earlier.append(shifted(gated, "seq", lag))
    y_real, y_imag = forward_stack(
        jnp.stack(earlier), k_real[1 : reach + 1], k_imag[1 : reach + 1], initial, tables
    )
    mixed = from_freq(y_real, y_imag, cos_t, sin_t).reshape(row_count, width)
    gated_out = (gate_b * mixed).astype(jnp.bfloat16)
    middle = x_full + jnp.dot(gated_out, mixer_out, preferred_element_type=jnp.float32)
    second_normed = plain_norm(middle, second_gain, second_bias).astype(jnp.bfloat16)
    pre = jnp.dot(second_normed, up_weight, preferred_element_type=jnp.float32)
    activated = jax.nn.gelu(pre, approximate=True).astype(jnp.bfloat16)
    result = middle + jnp.dot(activated, down_weight, preferred_element_type=jnp.float32)
    output = result.astype(jnp.bfloat16).reshape(seqs, block_len, width)
    upstream_low = cotangent.reshape(row_count, width)
    upstream = upstream_low.astype(jnp.float32)
    grad_down = jnp.einsum("rk,rd->kd", activated, upstream_low, preferred_element_type=jnp.float32)
    d_act = jnp.einsum("rd,kd->rk", upstream_low, down_weight, preferred_element_type=jnp.float32)
    _, gelu_back = jax.vjp(lambda arg: jax.nn.gelu(arg, approximate=True), pre)
    d_pre = gelu_back(d_act)[0].astype(jnp.bfloat16)
    grad_up = jnp.einsum("rd,rk->dk", second_normed, d_pre, preferred_element_type=jnp.float32)
    d_second = jnp.einsum("rk,dk->rd", d_pre, up_weight, preferred_element_type=jnp.float32)
    _, second_back = jax.vjp(plain_norm, middle, second_gain, second_bias)
    d_middle_norm, grad_second_gain, grad_second_bias = second_back(d_second)
    d_middle = upstream + d_middle_norm
    d_middle_low = d_middle.astype(jnp.bfloat16)
    grad_mixer_out = jnp.einsum(
        "rk,rd->kd", gated_out, d_middle_low, preferred_element_type=jnp.float32
    )
    d_gated_out = jnp.einsum(
        "rd,kd->rk", d_middle_low, mixer_out, preferred_element_type=jnp.float32
    )
    d_gate_b = d_gated_out * mixed
    d_mixed = (d_gated_out * gate_b).astype(jnp.bfloat16).reshape(seqs, block_len, width)
    empty_freq = jnp.zeros((seqs, 2 * block_len, width), jnp.float32)
    start_acc, own_terms = add_backward(
        (empty_freq, empty_freq), k_real[0], k_imag[0], d_mixed, own_real, own_imag, tables
    )
    unused = jnp.zeros((LAGS - reach, 2 * block_len, width), jnp.float32)
    later = []
    for lead in range(1, reach + 1):
        later.append(shifted(d_mixed, "seq", -lead))
    (z_real, z_imag), terms = backward_stack(
        jnp.stack(later),
        k_real[1 : reach + 1],
        k_imag[1 : reach + 1],
        start_acc,
        own_real,
        own_imag,
        tables,
    )
    dk_real = jnp.concatenate([own_terms[0][None], terms[0], unused], axis=0)
    dk_imag = jnp.concatenate([own_terms[1][None], terms[1], unused], axis=0)
    d_gated = (grad_time(z_real, z_imag, cos_t, sin_t) * valid).reshape(row_count, width)
    d_projected = jnp.concatenate([d_gated * gate_a, d_gated * value, d_gate_b], axis=1).astype(
        jnp.bfloat16
    )
    grad_mixer_in = jnp.einsum("rd,rk->dk", normed, d_projected, preferred_element_type=jnp.float32)
    d_normed = jnp.einsum("rk,dk->rd", d_projected, mixer_in, preferred_element_type=jnp.float32)
    _, first_back = jax.vjp(plain_norm, x_full, norm_gain, norm_bias)
    d_x_norm, grad_norm_gain, grad_norm_bias = first_back(d_normed)
    grad_inputs = (d_middle + d_x_norm).reshape(seqs, block_len, width)
    _, kernel_back = jax.vjp(lambda kern: kernel_freq(kern, cos_t, sin_t), kernel)
    d_kernel = kernel_back((dk_real, dk_imag))[0]
    dense = [
        grad_norm_gain,
        grad_norm_bias,
        grad_mixer_in,
        grad_mixer_out,
        grad_second_gain,
        grad_second_bias,
        grad_up,
        grad_down,
    ]
    summed = sum_everywhere([d_kernel] + dense)
    filter_grads = filter_back(summed[0])
    dense_sums = summed[1:]
    return (
        output,
        grad_inputs,
        dense_sums[0],
        dense_sums[1],
        dense_sums[2],
        filter_grads[0],
        filter_grads[1],
        filter_grads[2],
        filter_grads[3],
        filter_grads[4],
        dense_sums[3],
        dense_sums[4],
        dense_sums[5],
        dense_sums[6],
        dense_sums[7],
    )


SPECS_IN = (P("dp", "seq", None), P("dp")) + (P(),) * 13 + (P("dp", "seq", None),)
SPECS_OUT = (P("dp", "seq", None), P("dp", "seq", None)) + (P(),) * 13


def solution(mesh):
    local = chip_local if (mesh.shape["seq"], mesh.shape["dp"]) == (8, 4) else block_local
    return jax.shard_map(local, mesh=mesh, in_specs=SPECS_IN, out_specs=SPECS_OUT, check_vma=False)
```

```python
import math

import jax
import jax.numpy as jnp
import numpy as np
from jax import lax
from jax.experimental import pallas as pl
from jax.experimental.pallas import tpu as pltpu
from jax.sharding import PartitionSpec as P

AX = ("seq", "dp")
HIGH = lax.Precision.HIGHEST
EPSILON = 1e-05
BANDS = 16
KL = 2048
F32 = jnp.float32
BF16 = jnp.bfloat16


def mm(a, b, ca=1, cb=0):
    return lax.dot_general(a, b, (((ca,), (cb,)), ((), ())), preferred_element_type=F32)


def perm_of(f):
    pairs = []
    for z in range(4):
        for x in range(2):
            for y in range(2):
                for c in range(2):
                    a, b, d, e = f(z, x, y, c)
                    pairs.append(((z * 2 + x) * 4 + y * 2 + c, (a * 2 + b) * 4 + d * 2 + e))
    return pairs


PC = perm_of(lambda z, x, y, c: (z, x, y, 1 - c))
PX = perm_of(lambda z, x, y, c: (z, 1 - x, y, c))
PY = perm_of(lambda z, x, y, c: (z, x, 1 - y, c))
PZ = [perm_of(lambda z, x, y, c, k=k: (z ^ k, x, y, c)) for k in range(4)]


def send(v, perm):
    return lax.ppermute(v, AX, perm)


def tie(*vals):
    return lax.optimization_barrier(tuple(vals))


def swap_in(v, c):
    v = v.reshape(4, 2, 64, v.shape[-1])
    keep = pick(v, c, 1)
    got = send(pick(v, 1 - c, 1), PC)
    return jnp.where(c == 0, jnp.concatenate([keep, got]), jnp.concatenate([got, keep]))


def exchange_seq(v):
    return lax.all_to_all(v, "seq", 0, 0)


def swap_out(v, c):
    v = v.reshape(2, 4, 64, v.shape[-1])
    keep = pick(v, c)
    got = send(pick(v, 1 - c), PC)
    m = jnp.stack([jnp.where(c == 0, keep, got), jnp.where(c == 0, got, keep)], axis=1)
    return m.reshape(4, 128, v.shape[-1])


def both(own, c):
    other = send(own, PC)
    return jnp.stack([jnp.where(c == 0, own, other), jnp.where(c == 0, other, own)], axis=1)


def feature_table(taps):
    steps = np.arange(taps, dtype=np.float64) / KL
    freqs = np.arange(1, BANDS + 1, dtype=np.float64)
    phase = 2.0 * math.pi * steps[:, None] * freqs[None, :]
    return np.concatenate([steps[:, None], np.cos(phase), np.sin(phase)], axis=1).astype(np.float32)


def dft_table(length):
    f = 2 * np.arange(length, dtype=np.int64)[:, None] + 1
    n = np.arange(length, dtype=np.int64)[None, :]
    angle = (f * n % (4 * length)) * (2.0 * math.pi / (4 * length))
    return np.concatenate([np.cos(angle), -np.sin(angle)], axis=0).astype(np.float32)


def norm_parts(v):
    center = v - jnp.mean(v, axis=-1, keepdims=True)
    spread_ = jnp.mean(center * center, axis=-1, keepdims=True)
    inv = lax.rsqrt(spread_ + EPSILON)
    return center * inv, inv


def norm_back(q, hat, inv):
    return (q - jnp.mean(q, -1, keepdims=True) - hat * jnp.mean(q * hat, -1, keepdims=True)) * inv


def lanes(a, at, size):
    return lax.dynamic_slice_in_dim(a, at, size, axis=1)


def in_order(bit, own, other, axis=0):
    first = jnp.where(bit == 0, own, other)
    second = jnp.where(bit == 0, other, own)
    return jnp.concatenate([first, second], axis=axis)


def pick(a, i, axis=0):
    return lax.dynamic_index_in_dim(a, i, axis, keepdims=False)


GELU_A = math.sqrt(2.0 / math.pi)
GELU_B = 0.044715


def gelu_pair(v):
    sq = v * v
    t = jnp.tanh(GELU_A * v * (1.0 + GELU_B * sq))
    up = 0.5 * (1.0 + t)
    return v * up, up + 0.5 * v * (1.0 - t * t) * (GELU_A * (1.0 + 3.0 * GELU_B * sq))


def nn(a, b):
    return jnp.dot(a, b, preferred_element_type=F32)


def nt(a, b):
    return lax.dot_general(a, b, (((1,), (1,)), ((), ())), preferred_element_type=F32)


def tn(a, b):
    return lax.dot_general(a, b, (((0,), (0,)), ((), ())), preferred_element_type=F32)


def stats(v):
    center = v - jnp.mean(v, axis=-1, keepdims=True)
    inv = lax.rsqrt(jnp.mean(center * center, axis=-1, keepdims=True) + EPSILON)
    return center * inv, inv


def loop(n, body):
    def step(i, carry):
        body(i)
        return carry

    lax.fori_loop(0, n, step, 0)


def at(i, size, least=64):
    return pl.ds(pl.multiple_of(i * size, least), size)


CHUNKS = tuple(slice(256 * q, 256 * (q + 1)) for q in range(4))


def tokens(c, own, other, q):
    parts = []
    for p in (2 * q, 2 * q + 1):
        a, b = own[p].astype(F32), other[p].astype(F32)
        parts += [jnp.where(c == 0, a, b), jnp.where(c == 0, b, a)]
    return jnp.concatenate(parts, axis=0)


def set_own(ref, q, c, tile, mine=True):
    for n in range(2):
        first, second = tile[128 * n : 128 * n + 64], tile[128 * n + 64 : 128 * n + 128]
        ref[2 * q + n] = jnp.where((c == 0) == mine, first, second).astype(ref.dtype)


ANY = pl.BlockSpec(memory_space=pl.ANY)


def call(body, name, grid, scalars, ins, outs, scratch=(), vmem=60):
    def spec(block, index):
        return ANY if block is None else pl.BlockSpec(block, index)

    return pl.pallas_call(
        body,
        grid_spec=pltpu.PrefetchScalarGridSpec(
            num_scalar_prefetch=1,
            grid=(grid,),
            in_specs=[spec(b, i) for _, b, i in ins],
            out_specs=[spec(b, i) for _, _, b, i in outs],
            scratch_shapes=list(scratch),
        ),
        out_shape=[jax.ShapeDtypeStruct(s, t) for s, t, _, _ in outs],
        compiler_params=pltpu.CompilerParams(
            dimension_semantics=("arbitrary",), vmem_limit_bytes=vmem * 2**20
        ),
        name=name,
    )(scalars, *[a for a, _, _ in ins])


def whole(a):
    return (a, a.shape, lambda g, i, n=a.ndim: (0,) * n)


def step_from(first, count, lead=0, tail=1):
    def index(g, info):
        return (0,) * lead + (jnp.clip(g - first, 0, count - 1),) + (0,) * tail

    return index


class Copies:
    def __init__(self, sem):
        self.sem, self.count, self.out = sem, 0, []

    def load(self, src, dst):
        copy = pltpu.make_async_copy(src, dst, self.sem.at[self.count])
        self.count += 1
        copy.start()
        return copy

    def store(self, src, dst):
        self.out.append(self.load(src, dst))

    def finish(self):
        for copy in self.out:
            copy.wait()


def wait(*copies):
    for copy in copies:
        copy.wait()


def straight(body, name, scalars, rows_in, ins, outs, scratch, n_copies, vmem=60):
    return pl.pallas_call(
        body,
        in_specs=[pl.BlockSpec(memory_space=pltpu.SMEM)]
        + [pl.BlockSpec(memory_space=pltpu.VMEM)] * len(rows_in)
        + [ANY] * len(ins),
        out_specs=[ANY] * len(outs),
        out_shape=[jax.ShapeDtypeStruct(s, t) for s, t in outs],
        scratch_shapes=[pltpu.VMEM(s, t) for s, t in scratch] + [pltpu.SemaphoreType.DMA((n_copies,))],
        compiler_params=pltpu.CompilerParams(vmem_limit_bytes=vmem * 2**20),
        name=name,
    )(scalars, *rows_in, *ins)


def part_of(ref, axis, start, size):
    span = pl.ds(pl.multiple_of(start, 128), size)
    return ref.at[span, :] if axis == 0 else ref.at[:, span]


def front(info, x_own, x_other, gain, bias, mixer_in, wave, spec, back, mixer_out):
    width = mixer_in.shape[0]
    half = width // 2
    rows = wave.shape[1]

    def body(info, gain, bias, x_own, x_other, w_in, wave, spec, back, w_mo,
             normed_o, value_o, gate_a_o, gate_b_o, zf_o, mixed_o, gated_out_o, part_o,
             xo, xt, w3, wv, sp, bk, wm, normed, value, gate_a, gate_b, gated, prod, zf, mixed, gated_out, part, sem):
        c, length = info[0], info[1]
        io = Copies(sem)
        x_in = [(io.load(x_own.at[pl.ds(2 * q, 2)], xo.at[pl.ds(2 * q, 2)]),
                 io.load(x_other.at[pl.ds(2 * q, 2)], xt.at[pl.ds(2 * q, 2)])) for q in range(4)]
        w_got = [io.load(part_of(w_in, 1, n * width + c * half, half), w3.at[n]) for n in range(3)]
        f_got = []
        for q in range(2):
            span = pl.ds(512 * q, 512)
            f_got.append((io.load(wave.at[:, span], wv.at[:, span]), io.load(spec.at[:, span], sp.at[:, span])))
        b_got = [io.load(back.at[pl.ds(512 * q, 512)], bk.at[pl.ds(512 * q, 512)]) for q in range(2)]
        m_got = io.load(part_of(w_mo, 0, c * half, half), wm)
        for q, span in enumerate(CHUNKS):
            wait(*x_in[q])
            hat, _ = stats(tokens(c, xo, xt, q))
            normed[span, :] = (hat * gain[...] + bias[...]).astype(BF16)
        io.store(normed, normed_o)
        wait(w_got[0])
        v = nn(normed[...], w3[0])
        value[...] = v.astype(BF16)
        io.store(value, value_o)
        wait(w_got[1])
        a = nn(normed[...], w3[1])
        gate_a[...] = a.astype(BF16)
        io.store(gate_a, gate_a_o)
        at_row = lax.broadcasted_iota(jnp.int32, a.shape, 0)
        gated[...] = jnp.where(at_row < length, v * a, 0.0).astype(BF16)
        wait(w_got[2])
        gate_b[...] = nn(normed[...], w3[2]).astype(BF16)
        io.store(gate_b, gate_b_o)
        for q in range(2):
            span, low = slice(512 * q, 512 * q + 512), slice(rows + 512 * q, rows + 512 * q + 512)
            wait(*f_got[q])
            re = nn(wv[0, span], gated[...])
            im = nn(wv[1, span], gated[...])
            zf[0, span] = re.astype(BF16)
            zf[1, span] = im.astype(BF16)
            kr, ki = sp[0, span], sp[1, span]
            prod[span, :] = (kr * re - ki * im).astype(BF16)
            prod[low, :] = (kr * im + ki * re).astype(BF16)
        io.store(zf, zf_o)
        for q in range(2):
            span = slice(512 * q, 512 * q + 512)
            wait(b_got[q])
            m = nn(bk[span, :], prod[...])
            mixed[span, :] = m.astype(BF16)
            out = (gate_b[span, :].astype(F32) * m).astype(BF16)
            gated_out[span, :] = out
            if q == 0:
                wait(m_got)
            part[span, :] = nn(out, wm[...]).astype(BF16)
            here = pl.ds(512 * q, 512)
            io.store(part.at[here], part_o.at[here])
        io.store(mixed, mixed_o)
        io.store(gated_out, gated_out_o)
        io.finish()

    thin, wide = ((rows, half), BF16), ((rows, width), BF16)
    tok = ((8, 64, width), BF16)
    return straight(
        body, "front", info, [gain, bias], [x_own, x_other, mixer_in, wave, spec, back, mixer_out],
        [wide, thin, thin, thin, ((2, rows, half), BF16), thin, thin, wide],
        [tok, tok, ((3, width, half), BF16), (wave.shape, BF16), (spec.shape, F32), (back.shape, BF16),
         ((half, width), BF16), wide, thin, thin, thin, thin, ((2 * rows, half), BF16), ((2, rows, half), BF16), thin,
         thin, wide],
        8 + 3 + 4 + 2 + 1 + 9,
    )


def grad_shapes(rows, width):
    one = ((rows, width), BF16)
    return [one, one, ((2, rows, width), BF16)]


def make_grads(io, info, left, right, grad, send_a_o, send_b_o, keeps_o):
    for g, out in enumerate((send_a_o, send_b_o, keeps_o.at[0], keeps_o.at[1])):
        n = info[2 + g]
        grad[g] = tn(left(n), right(n)).astype(BF16)
        io.store(grad.at[g], out)


def up_grads(info, d_pre, normed):
    rows, ff = d_pre.shape
    width = normed.shape[1]

    def body(info, d_pre, normed, send_a_o, send_b_o, keeps_o, left, right, grad, sem):
        io = Copies(sem)
        l_in = []
        for g in range(4):
            l_in.append(io.load(part_of(d_pre, 1, info[2 + g] * (ff // 4), ff // 4), left.at[g]))
            if g == 0:
                r_in = io.load(normed, right)
        wait(r_in)
        for g, out in enumerate((send_a_o, send_b_o, keeps_o.at[0], keeps_o.at[1])):
            wait(l_in[g])
            grad[g] = tn(left[g], right[...]).astype(BF16)
            io.store(grad.at[g], out)
        io.finish()

    return straight(
        body, "up_grads", info, [], [d_pre, normed], grad_shapes(ff // 4, width),
        [((4, rows, ff // 4), BF16), ((rows, width), BF16), ((4, ff // 4, width), BF16)], 9,
    )


def set_sums(sums, gains, biases):
    sums[...] = jnp.zeros_like(sums)
    sums[0:1, :] = gains
    sums[1:2, :] = biases


def block_of(ref, n, size):
    return ref[:, pl.ds(pl.multiple_of(n * size, 128), size)]


def feed_forward(info, x_own, x_other, cot_own, cot_other, part, got, gain, bias, up_weight, down_weight):
    rows, width = part.shape
    ff = up_weight.shape[1] // 2
    cols = ff // 3

    def body(info, gain, bias, x_own, x_other, cot_own, cot_other, part, got, w_up, w_dn,
             middle_o, normed_o, cot_o, act_o, d_pre_o, d_sec_o, sums_o, send_a_o, send_b_o, keeps_o,
             xo, xt, co, ct, pt, gt, up, dn, middle, normed, cot, act, d_pre, d_sec, acc, sums, grad, sem):
        c = info[0]
        io = Copies(sem)
        x_in, c_in = [], []
        for q, span in enumerate(CHUNKS):
            two, here = pl.ds(2 * q, 2), pl.ds(256 * q, 256)
            x_in.append([io.load(x_own.at[two], xo.at[two]), io.load(x_other.at[two], xt.at[two]),
                         io.load(part.at[here], pt.at[here]), io.load(got.at[here], gt.at[here])])
        u_in = [io.load(part_of(w_up, 1, c * ff, cols), up.at[0])]
        c_in = [io.load(cot_own, co), io.load(cot_other, ct)]
        d_in = [io.load(part_of(w_dn, 0, c * ff, cols), dn.at[0])]
        for n in range(1, 3):
            u_in.append(io.load(part_of(w_up, 1, c * ff + n * cols, cols), up.at[n]))
            d_in.append(io.load(part_of(w_dn, 0, c * ff + n * cols, cols), dn.at[n]))
        for q, span in enumerate(CHUNKS):
            wait(*x_in[q])
            mid = tokens(c, xo, xt, q) + pt[span, :].astype(F32) + gt[span, :].astype(F32)
            middle[span, :] = mid
            hat, _ = stats(mid)
            normed[span, :] = (hat * gain[...] + bias[...]).astype(BF16)
        io.store(middle, middle_o)
        io.store(normed, normed_o)
        wait(*c_in)
        for q, span in enumerate(CHUNKS):
            cot[span, :] = tokens(c, co, ct, q).astype(BF16)
        io.store(cot, cot_o)
        for n in range(3):
            wait(u_in[n], d_in[n])
            v, slope = gelu_pair(nn(normed[...], up[n]))
            here = pl.ds(n * cols, cols)
            act[:, n * cols : (n + 1) * cols] = v.astype(BF16)
            io.store(act.at[:, here], act_o.at[:, here])
            d_pre[n] = (nt(cot[...], dn[n]) * slope).astype(BF16)
            io.store(d_pre.at[n], d_pre_o.at[:, here])
            more = nt(d_pre[n], up[n])
            if n == 0:
                acc[...] = more
            else:
                acc[...] += more
        gains, biases = 0.0, 0.0
        for q, span in enumerate(CHUNKS):
            ds = acc[span, :]
            d_sec[span, :] = ds.astype(BF16)
            here = pl.ds(256 * q, 256)
            io.store(d_sec.at[here], d_sec_o.at[here])
            hat, _ = stats(middle[span, :])
            gains += jnp.sum(ds * hat, axis=0, keepdims=True)
            biases += jnp.sum(ds, axis=0, keepdims=True)
        set_sums(sums, gains, biases)
        io.store(sums, sums_o)
        make_grads(io, info, lambda n: block_of(act, n, ff // 4), lambda n: cot[...], grad, send_a_o, send_b_o, keeps_o)
        io.finish()

    tok, wide, long = ((8, 64, width), BF16), ((rows, width), BF16), ((rows, ff), BF16)
    full = ((rows, width), F32)
    slab = ((3, rows, cols), BF16)
    return straight(
        body, "feed_forward", info, [gain, bias],
        [x_own, x_other, cot_own, cot_other, part, got, up_weight, down_weight],
        [full, wide, wide, long, long, wide, ((8, width), F32)] + grad_shapes(ff // 4, width),
        [tok, tok, tok, tok, wide, wide, ((3, width, cols), BF16), ((3, cols, width), BF16), full, wide, wide, long, slab,
         wide, full, ((8, width), F32), ((4, ff // 4, width), BF16)],
        16 + 2 + 6 + 3 + 6 + 5 + 4,
    )


def backward(
    info, d_sec, got, middle, cot, gain, mixer_out, mixed, gate_b, value, gate_a, wave, spec, zf, back, normed, gated_out
):
    rows, width = middle.shape
    half = width // 2

    def body(info, gain, d_sec, got, middle, cot, w_mo, mixed, gate_b, value, gate_a, wave, spec, zf, back,
             normed, gated_out, d_own_o, tf_o, d_proj_o, send_a_o, send_b_o, keeps_o,
             ds, gt, md, cs, wm, mx, gb, vl, ga, wv, sp, zs, bk, right, d_own, d_gb, d_mixed, prod, tf, left, grad, sem):
        c, length = info[0], info[1]
        io = Copies(sem)
        first = []
        for q in range(4):
            here = pl.ds(256 * q, 256)
            first.append([io.load(s.at[here], t.at[here]) for s, t in ((middle, md), (d_sec, ds), (got, gt), (cot, cs))])
        go_in = [io.load(part_of(w_mo, 0, c * half, half), wm), io.load(mixed, mx), io.load(gate_b, gb)]
        f_in = []
        for q in range(2):
            span = pl.ds(512 * q, 512)
            f_in.append([io.load(s.at[:, span], t.at[:, span]) for s, t in ((wave, wv), (spec, sp), (zf, zs))])
        b_in = [io.load(back.at[pl.ds(512 * q, 512)], bk.at[pl.ds(512 * q, 512)]) for q in range(2)]
        v_in = [io.load(value, vl), io.load(gate_a, ga)]
        g_in = [io.load(normed, right.at[0]), io.load(gated_out, left.at[:, pl.ds(3 * half, half)])]
        d_mid = right.at[1]
        for q, span in enumerate(CHUNKS):
            wait(*first[q])
            hat, inv = stats(md[span, :])
            t = (ds[span, :].astype(F32) + gt[span, :].astype(F32)) * gain[...]
            v = cs[span, :].astype(F32) + norm_back(t, hat, inv)
            d_mid[span, :] = v.astype(BF16)
            set_own(d_own, q, c, v)
        io.store(d_own, d_own_o)
        wait(*go_in)
        d_go = nt(d_mid[...], wm[...])
        d_gb[...] = (d_go * mx[...].astype(F32)).astype(BF16)
        d_mixed[...] = (d_go * gb[...].astype(F32)).astype(BF16)
        for q in range(2):
            span, low = slice(512 * q, 512 * q + 512), slice(rows + 512 * q, rows + 512 * q + 512)
            wait(*f_in[q])
            re = nn(wv[0, span], d_mixed[...])
            im = nn(wv[1, span], d_mixed[...])
            kr, ki = sp[0, span], sp[1, span]
            prod[span, :] = (kr * re + ki * im).astype(BF16)
            prod[low, :] = (kr * im - ki * re).astype(BF16)
            zr, zi = zs[0, span].astype(F32), zs[1, span].astype(F32)
            tf[0, span] = ((zr * re + zi * im) * (1.0 / rows)).astype(BF16)
            tf[1, span] = ((zr * im - zi * re) * (1.0 / rows)).astype(BF16)
        io.store(tf, tf_o)
        wait(*v_in)
        for q in range(2):
            span = slice(512 * q, 512 * q + 512)
            wait(b_in[q])
            m = nn(bk[span, :], prod[...])
            at_row = 512 * q + lax.broadcasted_iota(jnp.int32, m.shape, 0)
            m = jnp.where(at_row < length, m, 0.0)
            left[span, 0:half] = (m * ga[span, :].astype(F32)).astype(BF16)
            left[span, half : 2 * half] = (m * vl[span, :].astype(F32)).astype(BF16)
            left[span, 2 * half : 3 * half] = d_gb[span, :]
            here = pl.ds(512 * q, 512)
            io.store(left.at[here, pl.ds(0, 3 * half)], d_proj_o.at[here])
        wait(*g_in)
        make_grads(
            io, info, lambda n: block_of(left, n, half), lambda n: right[n // 3], grad, send_a_o, send_b_o, keeps_o
        )
        io.finish()

    wide, thin, full = ((rows, width), BF16), ((rows, half), BF16), ((rows, width), F32)
    own, freq, proj = ((8, 64, width), F32), ((2, rows, half), BF16), ((rows, 3 * half), BF16)
    return straight(
        body, "backward", info, [gain],
        [d_sec, got, middle, cot, mixer_out, mixed, gate_b, value, gate_a, wave, spec, zf, back, normed, gated_out],
        [own, freq, proj] + grad_shapes(half, width),
        [wide, wide, full, wide, ((half, width), BF16), thin, thin, thin, thin, (wave.shape, BF16), (spec.shape, F32),
         freq, (back.shape, BF16), ((2, rows, width), BF16), own, thin, thin, ((2 * rows, half), BF16), freq,
         ((rows, 4 * half), BF16), ((4, half, width), BF16)],
        16 + 3 + 6 + 2 + 2 + 2 + 4 + 4,
    )


def accumulate(acc, more):
    g = pl.program_id(0)

    @pl.when(g == 0)
    def _():
        acc[...] = more

    @pl.when(g > 0)
    def _():
        acc[...] += more


def norm_in_kernel(info, d_proj, w, x_own, x_other, keep, give, sums, acc):
    c = info[0]
    accumulate(acc, nt(d_proj[...], w[...]))

    @pl.when(pl.program_id(0) == 2)
    def _():
        gains, biases = 0.0, 0.0
        for q, rows in enumerate(CHUNKS):
            dn = acc[rows, :]
            hat, _ = stats(tokens(c, x_own, x_other, q))
            gains += jnp.sum(dn * hat, axis=0, keepdims=True)
            biases += jnp.sum(dn, axis=0, keepdims=True)
            set_own(keep, q, c, dn)
            set_own(give, q, c, dn, False)
        set_sums(sums, gains, biases)


def norm_in_back(info, d_proj, mixer_in, x_own, x_other):
    rows = d_proj.shape[0]
    width = mixer_in.shape[0]
    half = width // 2
    shape = (8, 64, width)
    return call(
        norm_in_kernel, "norm_in_back", 3, info,
        [(d_proj, (rows, half), lambda g, i: (0, g)), (mixer_in, (width, half), lambda g, i: (0, 2 * g + i[0])),
         whole(x_own), whole(x_other)],
        [(shape, F32, shape, lambda g, i: (0, 0, 0)), (shape, BF16, shape, lambda g, i: (0, 0, 0)),
         ((8, width), F32, (8, width), lambda g, i: (0, 0))],
        [pltpu.VMEM((rows, width), F32)],
        vmem=36,
    )


def out_kernel(info, act, w, middle, keep, give, acc):
    c = info[0]
    accumulate(acc, nn(act[...], w[...]))

    @pl.when(pl.program_id(0) == 2)
    def _():
        for q, rows in enumerate(CHUNKS):
            out = acc[rows, :]
            set_own(keep, q, c, out + middle[rows, :])
            set_own(give, q, c, out, False)


def out_part(info, act, down_weight, middle):
    rows, width = middle.shape
    cols = act.shape[1] // 3
    shape = (8, 64, width)
    return call(
        out_kernel, "out_part", 3, info,
        [(act, (rows, cols), lambda g, i: (0, g)), (down_weight, (cols, width), lambda g, i: (3 * i[0] + g, 0)),
         whole(middle)],
        [(shape, F32, shape, lambda g, i: (0, 0, 0)), (shape, BF16, shape, lambda g, i: (0, 0, 0))],
        [pltpu.VMEM((rows, width), F32)],
        vmem=36,
    )


def filter_back(info, tf, spread, f_out, slope2, slope1, turn, sides, back, norm_sums, second_sums):
    rows, half = tf.shape[1:]
    width = 2 * half

    def body(info, spread, f_out, slope2, slope1, turn, sides, norm_s, second_s, tf, back, out_o,
             tv, bk, out, sem):
        io = Copies(sem)
        t_in = [io.load(tf.at[n], tv.at[pl.ds(n * rows, rows)]) for n in range(2)]
        b_in = [io.load(back.at[pl.ds(512 * q, 512)], bk.at[pl.ds(512 * q, 512)]) for q in range(2)]
        wait(*t_in)
        g_fo = tn(spread[...], tv[...])[0:64] * float(rows)
        kf = nt(tv[...], f_out[...]).astype(BF16)
        wait(*b_in)
        d_s = slope2[...] * nn(bk[...], kf)
        high = lax.Precision.HIGHEST
        both = d_s + slope1[...] * jnp.dot(d_s, turn[...], precision=high, preferred_element_type=F32)
        g = tn(sides[...].astype(BF16), both.astype(BF16))
        lane = lax.broadcasted_iota(jnp.int32, (64, 128), 1)
        g = jnp.where(lane < 64, g[0:64], g[64:128])
        out[...] = jnp.zeros_like(out)
        out[0:32, 0:half] = g_fo[0:32].astype(BF16)
        out[0:32, half:] = g_fo[32:64].astype(BF16)
        for n in range(6):
            pair = [g[8 * n : 8 * n + 8]]
            if n < 2:
                pair.append(g[48 + 8 * n : 56 + 8 * n])
            elif n == 2:
                pair.append(jnp.broadcast_to(jnp.sum(both, axis=0, keepdims=True), (8, 128)))
            else:
                pair.append(jnp.zeros((8, 128), F32))
            out[32:48, 128 * n : 128 * n + 128] = jnp.concatenate(pair, axis=0).astype(BF16)
        out[48:64, :] = jnp.concatenate([norm_s[...], second_s[...]], axis=0).astype(BF16)
        io.store(out, out_o)
        io.finish()

    return straight(
        body, "filter_back", info, [spread, f_out, slope2, slope1, turn, sides, norm_sums, second_sums], [tf, back],
        [((64, width), BF16)],
        [((2 * rows, half), BF16), (back.shape, BF16), ((64, width), BF16)], 5, vmem=44,
    )[0]


def unpack_small(info, own, got):
    width = own.shape[1]
    half = width // 2

    def body(info, own, got, g_fo, g_fm, g_fi, b_m, b_f, norms, seconds):
        a, b = own[0:64, :].astype(F32), got[0:64, :].astype(F32)
        lo = jnp.where(info[0] == 0, a[0:32], b[0:32])
        hi = jnp.where(info[0] == 0, b[0:32], a[0:32])
        g_fo[0:32, 0:half], g_fo[32:64, 0:half] = lo[:, 0:half], lo[:, half:]
        g_fo[0:32, half:], g_fo[32:64, half:] = hi[:, 0:half], hi[:, half:]
        s = a[32:64] + b[32:64]
        tiles = [s[0:8, 128 * n : 128 * n + 128] for n in range(6)] + [s[8:16, 128 * n : 128 * n + 128] for n in range(3)]
        g = jnp.concatenate(tiles[:8], axis=0)
        g_fm[...] = g[:, 0:64]
        g_fi[...] = g[0:33, 64:128]
        b_m[...] = tiles[8][0:1, 0:64]
        b_f[...] = tiles[8][0:1, 64:128]
        norms[...] = s[16:24]
        seconds[...] = s[24:32]

    shapes = [(64, width), (64, 64), (33, 64), (1, 64), (1, 64), (8, width), (8, width)]
    return pl.pallas_call(
        body,
        in_specs=[pl.BlockSpec(memory_space=pltpu.SMEM)] + [pl.BlockSpec(memory_space=pltpu.VMEM)] * 2,
        out_specs=[pl.BlockSpec(memory_space=pltpu.VMEM)] * len(shapes),
        out_shape=[jax.ShapeDtypeStruct(s, F32) for s in shapes],
        compiler_params=pltpu.CompilerParams(vmem_limit_bytes=16 * 2**20),
        name="unpack_small",
    )(info, own, got)


def ends_of(gain, out_keep, out_got, d_norm_keep, d_norm_got, d_mid_own, x_half):
    blocks, n, width = x_half.shape

    def body(gain, out_keep, out_got, d_norm_keep, d_norm_got, d_mid_own, x_half, out):
        for p in range(blocks):
            hat, inv = stats(x_half[p].astype(F32))
            q = (d_norm_keep[p] + d_norm_got[p].astype(F32)) * gain[...]
            out[p, :, width:] = (d_mid_own[p] + norm_back(q, hat, inv)).astype(BF16)
            out[p, :, 0:width] = (out_keep[p] + out_got[p].astype(F32)).astype(BF16)

    return pl.pallas_call(
        body,
        in_specs=[pl.BlockSpec(memory_space=pltpu.VMEM)] * 7,
        out_specs=pl.BlockSpec(memory_space=pltpu.VMEM),
        out_shape=jax.ShapeDtypeStruct((blocks, n, 2 * width), BF16),
        compiler_params=pltpu.CompilerParams(vmem_limit_bytes=32 * 2**20),
        name="ends_of",
    )(gain, out_keep, out_got, d_norm_keep, d_norm_got, d_mid_own, x_half)


class Line:
    def __init__(self):
        self.token = None

    def __call__(self, fn, *args):
        if self.token is not None:
            self.token, *args = tie(self.token, *args)
        outs = fn(*args)
        self.token = jax.tree_util.tree_leaves(outs)[0]
        return outs


def small(line, body, name, outs, *ins):
    specs = [pl.BlockSpec(memory_space=pltpu.SMEM)] + [pl.BlockSpec(memory_space=pltpu.VMEM)] * (len(ins) - 1)
    return line(
        pl.pallas_call(
            body,
            in_specs=specs,
            out_specs=[pl.BlockSpec(memory_space=pltpu.VMEM)] * len(outs),
            out_shape=[jax.ShapeDtypeStruct(s, t) for s, t in outs],
            compiler_params=pltpu.CompilerParams(vmem_limit_bytes=16 * 2**20),
            name=name,
        ),
        *ins,
    )


def plus(a, b):
    return (a.astype(F32) + b.astype(F32)).astype(BF16)


class Reducer:
    def __init__(self, line, pos, send_a, send_b, keeps):
        self.line, self.pos, self.keeps = line, pos, keeps
        self.rows, self.cols = send_a.shape
        self.got = (send(send_a, PX), send(send_b, PY))

    def step2(self):
        n = self.rows // 2

        def body(pos, keeps, got_a, got_b, out_a, out_b, keep):
            for k, (got, out) in enumerate(((got_a, out_a), (got_b, out_b))):
                p = pos[1 - k]
                mine, others = at(p, n), at(1 - p, n)
                out[...] = plus(keeps[k, others, :], got[others, :])
                keep[k] = plus(keeps[k, mine, :], got[mine, :])

        a, b, self.keeps = small(
            self.line, body, "step2", [((n, self.cols), BF16)] * 2 + [((2, n, self.cols), BF16)], self.pos, self.keeps, *self.got
        )
        self.got = (send(a, PY), send(b, PX))

    def step3(self):
        n = self.rows // 4

        def body(pos, keeps, got_a, got_b, out, keep):
            mine, others = at(pos[2], n, 32), at(1 - pos[2], n, 32)
            for k, got in enumerate((got_a, got_b)):
                out[k] = plus(keeps[k, others, :], got[others, :])
                keep[k] = plus(keeps[k, mine, :], got[mine, :])

        shape = (2, n, self.cols)
        out, self.keeps = small(self.line, body, "step3", [(shape, BF16), (shape, BF16)], self.pos, self.keeps, *self.got)
        self.got = (send(out, PZ[1]),)

    def step4(self, extra=None):
        n = self.rows // 2
        self.extra = 0 if extra is None else extra.shape[0]

        def body(pos, keeps, got, *refs):
            out = refs[-1]
            for k in range(2):
                out[k * n // 2 : (k + 1) * n // 2, :] = plus(keeps[k], got[k])
            if extra is not None:
                out[n:, :] = refs[0][...]

        ins = [self.keeps, *self.got] + ([] if extra is None else [extra])
        (self.total,) = small(self.line, body, "step4", [((n + self.extra, self.cols), BF16)], self.pos, *ins)
        self.got = (send(self.total, PZ[2]),)

    def step5(self):
        def body(pos, total, got, out):
            out[...] = plus(total[...], got[...])

        (self.total,) = small(self.line, body, "step5", [(self.total.shape, BF16)], self.pos, self.total, *self.got)
        self.got = (send(self.total, PZ[1]),)

    def step6(self):
        n, more = self.rows // 4, self.extra

        def body(pos, total, got, out_a, out_b):
            mine, others = at(pos[2], n, 32), at(1 - pos[2], n, 32)
            for k, out in enumerate((out_a, out_b)):
                out[mine, :] = total[k * n : (k + 1) * n, :]
                out[others, :] = got[k * n : (k + 1) * n, :]
            if more:
                out_a[2 * n :, :] = plus(total[2 * n :, :], got[2 * n :, :])

        shapes = [((2 * n + more, self.cols), BF16), ((2 * n, self.cols), BF16)]
        self.own = small(self.line, body, "step6", shapes, self.pos, self.total, *self.got)
        self.got = (send(self.own[0], PY), send(self.own[1], PX))

    def step7(self):
        n, more = self.rows // 2, self.extra

        def body(pos, own_a, own_b, got_a, got_b, out_a, out_b):
            for k, (own, got, out) in enumerate(((own_a, got_a, out_a), (own_b, got_b, out_b))):
                p = pos[1 - k]
                out[at(p, n), :] = own[0:n, :]
                out[at(1 - p, n), :] = got[0:n, :]
            if more:
                out_a[2 * n :, :] = plus(own_a[n:, :], got_a[n:, :])

        shapes = [((2 * n + more, self.cols), BF16), ((2 * n, self.cols), BF16)]
        self.near = small(self.line, body, "step7", shapes, self.pos, *self.own, *self.got)
        self.got = (send(self.near[0], PX), send(self.near[1], PY))
        self.pair_near = [send(v, PC) for v in self.near]

    def step8(self):
        self.far = list(self.got)
        if self.extra:
            n = self.rows

            def body(pos, near, far, out):
                out[...] = plus(near[n:, :], far[n:, :])

            shape = (self.extra, self.cols)
            (self.sum,) = small(self.line, body, "step8", [(shape, BF16)], self.pos, self.near[0], self.far[0])
        self.pair_far = [send(v, PC) for v in self.far]


def write(line, bufs, sources, spots, moves):
    n, m = len(sources), len(bufs)
    rows, cols = sources[1].shape
    turned = any(t for _, _, _, _, t in moves([0, 0, 0]))
    straight = any(not t for _, _, _, _, t in moves([0, 0, 0]))

    def body(*refs):
        spot = refs[0]
        src, out = refs[1 : 1 + n], refs[1 + n + m : 1 + n + 2 * m]
        wide, tall, sem = refs[1 + n + 2 * m :]

        def each(act):
            for k in range(n):
                for when, b, i, j, t in moves([spot[k, e] for e in range(3)]):
                    size = (cols, rows) if t else (rows, cols)
                    src_ref = tall.at[k] if t else wide.at[k]
                    copy = pltpu.make_async_copy(
                        src_ref,
                        out[b].at[pl.ds(pl.multiple_of(i, 128), size[0]), pl.ds(pl.multiple_of(j, 128), size[1])],
                        sem.at[k],
                    )
                    act(k, when, t, copy)

        def begin(k, when, t, copy):
            @pl.when(when)
            def _():
                if t:
                    tall[k] = src[k][0:rows, :].astype(F32).T
                else:
                    wide[k] = src[k][0:rows, :].astype(F32)
                copy.start()

        def finish(k, when, t, copy):
            @pl.when(when)
            def _():
                copy.wait()

        each(begin)
        each(finish)

    return line(
        pl.pallas_call(
            body,
            in_specs=[pl.BlockSpec(memory_space=pltpu.SMEM)] + [pl.BlockSpec(memory_space=pltpu.VMEM)] * n + [ANY] * m,
            out_specs=[ANY] * m,
            out_shape=[jax.ShapeDtypeStruct(b.shape, F32) for b in bufs],
            input_output_aliases={1 + n + b: b for b in range(m)},
            scratch_shapes=[
                pltpu.VMEM((n, rows, cols) if straight else (n, 8, 128), F32),
                pltpu.VMEM((n, cols, rows) if turned else (n, 8, 128), F32),
                pltpu.SemaphoreType.DMA((n,)),
            ],
            compiler_params=pltpu.CompilerParams(vmem_limit_bytes=32 * 2**20),
            name="write",
        ),
        spots, *sources, *bufs,
    )


def fresh(*shapes):
    def body(*refs):
        pass

    return pl.pallas_call(
        body, out_specs=[ANY] * len(shapes), out_shape=[jax.ShapeDtypeStruct(s, F32) for s in shapes], name="fresh"
    )()


def write_down(s):
    return [(s[0] >= 0, 0, s[0] * 1536 + s[1] * 768 + s[2] * 384, 0, False)]


def write_up(s):
    return [(s[0] >= 0, 0, 0, s[0] * 1536 + s[1] * 768 + s[2] * 384, True)]


def write_mix(s):
    n = s[1] * 2 + s[2]
    return [(n < 3, 0, 0, n * 768 + s[0] * 384, True), (n == 3, 1, s[0] * 384, 0, False)]


def chip_local(
    inputs, lengths, norm_gain, norm_bias, mixer_in, filter_in, filter_in_bias, filter_mid, filter_mid_bias,
    filter_out, mixer_out, second_gain, second_bias, up_weight, down_weight, cotangent,
):
    s = lax.axis_index("seq")
    d = lax.axis_index("dp")
    z, x, y, c = s // 2, s % 2, d // 2, d % 2
    width = inputs.shape[-1]
    rows = 8 * inputs.shape[1]
    half = width // 2
    x_swapped = swap_in(inputs, c)
    cot_half = swap_in(cotangent, c)
    x_half = exchange_seq(x_swapped)
    other_len = send(lengths, PC)
    length = pick(jnp.where(c == (z >> 1), lengths, other_len), (z & 1) * 2 + x)
    tab = [1 - x, 3 - y, x, 2 + y]
    info = jnp.stack([c, length, *tab])
    zero = 0 * c
    pos = jnp.stack([x, y, z & 1, z >> 1])
    near = jnp.stack([jnp.stack(v) for v in ((c, zero, x), (c, zero + 1, y), (1 - c, zero, x), (1 - c, zero + 1, y))])
    far = jnp.stack(
        [jnp.stack(v) for v in ((c, zero, 1 - x), (c, zero + 1, 1 - y), (1 - c, zero, 1 - x), (1 - c, zero + 1, 1 - y))]
    )
    norm_gain, norm_bias = norm_gain[None], norm_bias[None]
    second_gain, second_bias = second_gain[None], second_bias[None]
    filter_in, filter_out, x_swapped = tie(filter_in, filter_out, x_swapped)
    f_out = lanes(filter_out, c * half, half)
    waves = dft_table(rows)
    table = jnp.asarray(waves, BF16)
    wave = table.reshape(2, rows, rows)
    back = jnp.asarray(waves.T, BF16)
    feats = jnp.asarray(feature_table(rows))
    first_act = jnp.dot(feats, filter_in, precision=HIGH) + filter_in_bias
    h1 = jnp.sin(first_act)
    second_act = jnp.dot(h1, filter_mid, precision=HIGH) + filter_mid_bias
    h2 = jnp.sin(second_act)
    h2_hi = h2.astype(BF16)
    h2_lo = (h2 - h2_hi.astype(F32)).astype(BF16)
    hf = mm(table, jnp.concatenate([h2_hi, h2_lo], axis=1))
    hf = (hf[:, :64] + hf[:, 64:]) * (1.0 / rows)
    spec = jnp.dot(hf, f_out, precision=lax.Precision.HIGH).reshape(2, rows, half)
    spread = jnp.pad(hf, ((0, 0), (0, 64))).astype(BF16)
    f_low = jnp.pad(f_out, ((0, 64), (0, 0))).astype(BF16)
    slope2 = jnp.pad(jnp.cos(second_act), ((0, 0), (0, 64)))
    slope1 = jnp.pad(jnp.cos(first_act), ((0, 0), (64, 0)))
    turn = jnp.pad(filter_mid.T, ((0, 64), (64, 0)))
    sides = jnp.concatenate([h1, jnp.pad(feats, ((0, 0), (0, 31)))], axis=1)
    x_half, spec, cot_half, info, near, far, pos, spread, f_low, slope2, slope1, turn, sides = tie(
        x_half, spec, cot_half, info, near, far, pos, spread, f_low, slope2, slope1, turn, sides
    )
    cot_half = exchange_seq(cot_half)
    x_pair = send(x_half, PC)
    normed, value, gate_a, gate_b, zf, mixed, gated_out, part = front(
        info, x_half, x_pair, norm_gain, norm_bias, mixer_in, wave, spec, back, mixer_out
    )
    cot_pair = send(cot_half, PC)
    middle, second_normed, cot, activated, d_pre, d_second, second_sums, *g_down = feed_forward(
        info, x_half, x_pair, cot_half, cot_pair, part, send(part, PC), second_gain, second_bias, up_weight, down_weight
    )
    d_second_pair = send(d_second, PC)
    line = Line()
    line.token = g_down[2]
    down = Reducer(line, pos, *g_down)
    up = Reducer(line, pos, *line(up_grads, info, d_pre, second_normed))
    d_mid_own, tf, d_proj, *g_mix = line(
        backward, info, d_second, d_second_pair, middle, cot, second_gain, mixer_out, mixed, gate_b, value, gate_a, wave,
        spec, zf, back, normed, gated_out,
    )
    mix = Reducer(line, pos, *g_mix)
    down.step2()
    up.step2()
    d_norm_keep, d_norm_give, norm_sums = line(norm_in_back, info, d_proj, mixer_in, x_half, x_pair)
    d_norm_got = send(d_norm_give, PC)
    down.step3()
    out_keep, out_give = line(out_part, info, activated, down_weight, middle)
    out_got = send(out_give, PC)
    up.step3()
    down.step4()
    mix.step2()
    tiny = line(
        filter_back, info, tf, spread, f_low, slope2, slope1, turn, sides, back, norm_sums, second_sums
    )
    up.step4(tiny)
    down.step5()
    mix.step3()
    ends = line(ends_of, norm_gain, out_keep, out_got, d_norm_keep, d_norm_got, d_mid_own, x_half)
    up.step5()
    down.step6()
    mix.step4()
    up.step6()
    down.step7()
    mix.step5()
    ends, line.token = tie(ends, line.token)
    ends = exchange_seq(ends)
    up.step7()
    bufs = fresh(down_weight.shape, up_weight.shape, mixer_in.shape, mixer_out.shape)
    grad_down = write(line, bufs[:1], [*down.near, *down.pair_near], near, write_down)
    mix.step6()
    down.step8()
    (grad_down,) = write(line, grad_down, [*down.far, *down.pair_far], far, write_down)
    grad_up = write(line, bufs[1:2], [*up.near, *up.pair_near], near, write_up)
    mix.step7()
    up.step8()
    tiny_got = send(up.sum, PC)
    (grad_up,) = write(line, grad_up, [*up.far, *up.pair_far], far, write_up)
    g_fo, g_fm, g_fi, b_m, b_f, norms, seconds = line(unpack_small, info, up.sum, tiny_got)
    grads_two = write(line, bufs[2:], [*mix.near, *mix.pair_near], near, write_mix)
    back_out = line(swap_out, ends, c)
    output, grad_inputs = back_out[..., :width], back_out[..., width:].astype(F32)
    mix.step8()
    grad_in, grad_mo = write(line, grads_two, [*mix.far, *mix.pair_far], far, write_mix)
    return (
        output, grad_inputs, norms[0], norms[1], grad_in, g_fi, b_f[0], g_fm, b_m[0],
        g_fo, grad_mo, seconds[0], seconds[1], grad_up, grad_down,
    )


LAGS = 16


def shifted(value, axis, by):
    devices = lax.axis_size(axis)
    pairs = [(i, i + by) for i in range(devices) if 0 <= i + by < devices]
    return lax.ppermute(value, axis, pairs)


def plain_norm(values, gain, shift):
    center = values - jnp.mean(values, axis=-1, keepdims=True)
    spread = jnp.mean(center * center, axis=-1, keepdims=True)
    return center * lax.rsqrt(spread + EPSILON) * gain + shift


def features_of(taps, bands):
    steps = jnp.arange(taps, dtype=jnp.float32) / taps
    freqs = jnp.arange(1, bands + 1, dtype=jnp.float32)
    phase = 2.0 * math.pi * steps[:, None] * freqs[None, :]
    return jnp.concatenate([steps[:, None], jnp.cos(phase), jnp.sin(phase)], axis=1)


def taps_of(filter_in, filter_in_bias, filter_mid, filter_mid_bias, filter_out):
    table = features_of(KL, BANDS)
    first = jnp.sin(jnp.dot(table, filter_in, precision=HIGH) + filter_in_bias)
    second = jnp.sin(jnp.dot(first, filter_mid, precision=HIGH) + filter_mid_bias)
    return jnp.dot(second, filter_out, precision=HIGH)


def wave_tables(block_len):
    length = 2 * block_len
    index = jnp.arange(length, dtype=jnp.int32)
    angle = (index[:, None] * index[None, :] % length).astype(jnp.float32) * (
        2.0 * math.pi / length
    )
    return (jnp.cos(angle), jnp.sin(angle))


def split_table(table):
    leading = table.astype(jnp.bfloat16)
    remainder = (table - leading.astype(jnp.float32)).astype(jnp.bfloat16)
    return (leading, remainder)


def low_tables(cos_t, sin_t):
    length = cos_t.shape[0]
    half = length // 2
    return (
        split_table(cos_t[:, :half]),
        split_table(sin_t[:, :half]),
        split_table(cos_t[half:] / length),
        split_table(sin_t[half:] / length),
    )


def apply_split(pattern, halves, values):
    first = jnp.einsum(pattern, halves[0], values, preferred_element_type=jnp.float32)
    second = jnp.einsum(pattern, halves[1], values, preferred_element_type=jnp.float32)
    return first + second


def kernel_freq(kernel, cos_t, sin_t):
    block_len = cos_t.shape[0] // 2
    width = kernel.shape[1]
    count = kernel.shape[0] // block_len
    padded = jnp.concatenate(
        [
            jnp.zeros((block_len, width), jnp.float32),
            kernel,
            jnp.zeros((2 * block_len, width), jnp.float32),
        ],
        axis=0,
    )
    pieces = padded.reshape(count + 3, block_len, width)
    segments = jnp.concatenate([pieces[: count + 1], pieces[1 : count + 2]], axis=1)
    real = jnp.einsum("fn,mnd->mfd", cos_t, segments, precision=HIGH)
    imag = -jnp.einsum("fn,mnd->mfd", sin_t, segments, precision=HIGH)
    return (real, imag)


def to_freq(values, tables):
    real = apply_split("fc,scd->sfd", tables[0], values)
    imag = -apply_split("fc,scd->sfd", tables[1], values)
    return (real, imag)


def from_freq(real, imag, cos_t, sin_t):
    length = cos_t.shape[0]
    half = length // 2
    first = jnp.einsum("nf,sfd->snd", cos_t[half:], real, precision=HIGH)
    second = jnp.einsum("nf,sfd->snd", sin_t[half:], imag, precision=HIGH)
    return (first - second) / length


def grad_freq(values, tables):
    real = apply_split("nf,snd->sfd", tables[2], values)
    imag = -apply_split("nf,snd->sfd", tables[3], values)
    return (real, imag)


def grad_time(real, imag, cos_t, sin_t):
    half = cos_t.shape[0] // 2
    first = jnp.einsum("fc,sfd->scd", cos_t[:, :half], real, precision=HIGH)
    second = jnp.einsum("fc,sfd->scd", sin_t[:, :half], imag, precision=HIGH)
    return first - second


def add_forward(acc, k_real, k_imag, values, tables):
    z_real, z_imag = to_freq(values, tables)
    return (acc[0] + k_real * z_real - k_imag * z_imag, acc[1] + k_real * z_imag + k_imag * z_real)


def add_backward(acc, k_real, k_imag, grads, own_real, own_imag, tables):
    d_real, d_imag = grad_freq(grads, tables)
    new_real = acc[0] + k_real * d_real + k_imag * d_imag
    new_imag = acc[1] - k_imag * d_real + k_real * d_imag
    term_real = jnp.sum(own_real * d_real + own_imag * d_imag, axis=0)
    term_imag = jnp.sum(own_real * d_imag - own_imag * d_real, axis=0)
    return ((new_real, new_imag), (term_real, term_imag))


def forward_stack(stack, k_real, k_imag, acc, tables):

    def forward_step(carry, item):
        return (add_forward(carry, item[1], item[2], item[0], tables), None)

    result, _ = lax.scan(forward_step, acc, (stack, k_real, k_imag))
    return result


def backward_stack(stack, k_real, k_imag, acc, own_real, own_imag, tables):

    def backward_step(carry, item):
        return add_backward(carry, item[1], item[2], item[0], own_real, own_imag, tables)

    return lax.scan(backward_step, acc, (stack, k_real, k_imag))


def sum_everywhere(parts):
    flat_grads = jnp.concatenate([piece.reshape(-1) for piece in parts])
    portion = lax.psum_scatter(flat_grads, ("seq", "dp"), scatter_dimension=0, tiled=True)
    summed = lax.all_gather(portion.astype(jnp.bfloat16), ("seq", "dp"), axis=0, tiled=True).astype(
        portion.dtype
    )
    results = []
    offset = 0
    for piece in parts:
        results.append(summed[offset : offset + piece.size].reshape(piece.shape))
        offset = offset + piece.size
    return results


def block_local(
    inputs,
    lengths,
    norm_gain,
    norm_bias,
    mixer_in,
    filter_in,
    filter_in_bias,
    filter_mid,
    filter_mid_bias,
    filter_out,
    mixer_out,
    second_gain,
    second_bias,
    up_weight,
    down_weight,
    cotangent,
):
    seqs, block_len, width = inputs.shape
    row_count = seqs * block_len
    reach = min(LAGS, lax.axis_size("seq") - 1)
    rank = lax.axis_index("seq")
    position = rank * block_len + jnp.arange(block_len, dtype=jnp.int32)
    valid = (position[None, :] < lengths[:, None]).astype(jnp.float32)[:, :, None]
    cos_t, sin_t = wave_tables(block_len)
    tables = low_tables(cos_t, sin_t)
    kernel, filter_back = jax.vjp(
        taps_of, filter_in, filter_in_bias, filter_mid, filter_mid_bias, filter_out
    )
    k_real, k_imag = kernel_freq(kernel, cos_t, sin_t)
    x_full = inputs.astype(jnp.float32).reshape(row_count, width)
    normed = plain_norm(x_full, norm_gain, norm_bias).astype(jnp.bfloat16)
    projected = jnp.dot(normed, mixer_in, preferred_element_type=jnp.float32)
    value = projected[:, :width]
    gate_a = projected[:, width : 2 * width]
    gate_b = projected[:, 2 * width :]
    gated = (value * gate_a).astype(jnp.bfloat16).reshape(seqs, block_len, width) * valid.astype(
        jnp.bfloat16
    )
    own_real, own_imag = to_freq(gated, tables)
    initial = (
        k_real[0] * own_real - k_imag[0] * own_imag,
        k_real[0] * own_imag + k_imag[0] * own_real,
    )
    earlier = []
    for lag in range(1, reach + 1):
        earlier.append(shifted(gated, "seq", lag))
    y_real, y_imag = forward_stack(
        jnp.stack(earlier), k_real[1 : reach + 1], k_imag[1 : reach + 1], initial, tables
    )
    mixed = from_freq(y_real, y_imag, cos_t, sin_t).reshape(row_count, width)
    gated_out = (gate_b * mixed).astype(jnp.bfloat16)
    middle = x_full + jnp.dot(gated_out, mixer_out, preferred_element_type=jnp.float32)
    second_normed = plain_norm(middle, second_gain, second_bias).astype(jnp.bfloat16)
    pre = jnp.dot(second_normed, up_weight, preferred_element_type=jnp.float32)
    activated = jax.nn.gelu(pre, approximate=True).astype(jnp.bfloat16)
    result = middle + jnp.dot(activated, down_weight, preferred_element_type=jnp.float32)
    output = result.astype(jnp.bfloat16).reshape(seqs, block_len, width)
    upstream_low = cotangent.reshape(row_count, width)
    upstream = upstream_low.astype(jnp.float32)
    grad_down = jnp.einsum("rk,rd->kd", activated, upstream_low, preferred_element_type=jnp.float32)
    d_act = jnp.einsum("rd,kd->rk", upstream_low, down_weight, preferred_element_type=jnp.float32)
    _, gelu_back = jax.vjp(lambda arg: jax.nn.gelu(arg, approximate=True), pre)
    d_pre = gelu_back(d_act)[0].astype(jnp.bfloat16)
    grad_up = jnp.einsum("rd,rk->dk", second_normed, d_pre, preferred_element_type=jnp.float32)
    d_second = jnp.einsum("rk,dk->rd", d_pre, up_weight, preferred_element_type=jnp.float32)
    _, second_back = jax.vjp(plain_norm, middle, second_gain, second_bias)
    d_middle_norm, grad_second_gain, grad_second_bias = second_back(d_second)
    d_middle = upstream + d_middle_norm
    d_middle_low = d_middle.astype(jnp.bfloat16)
    grad_mixer_out = jnp.einsum(
        "rk,rd->kd", gated_out, d_middle_low, preferred_element_type=jnp.float32
    )
    d_gated_out = jnp.einsum(
        "rd,kd->rk", d_middle_low, mixer_out, preferred_element_type=jnp.float32
    )
    d_gate_b = d_gated_out * mixed
    d_mixed = (d_gated_out * gate_b).astype(jnp.bfloat16).reshape(seqs, block_len, width)
    empty_freq = jnp.zeros((seqs, 2 * block_len, width), jnp.float32)
    start_acc, own_terms = add_backward(
        (empty_freq, empty_freq), k_real[0], k_imag[0], d_mixed, own_real, own_imag, tables
    )
    unused = jnp.zeros((LAGS - reach, 2 * block_len, width), jnp.float32)
    later = []
    for lead in range(1, reach + 1):
        later.append(shifted(d_mixed, "seq", -lead))
    (z_real, z_imag), terms = backward_stack(
        jnp.stack(later),
        k_real[1 : reach + 1],
        k_imag[1 : reach + 1],
        start_acc,
        own_real,
        own_imag,
        tables,
    )
    dk_real = jnp.concatenate([own_terms[0][None], terms[0], unused], axis=0)
    dk_imag = jnp.concatenate([own_terms[1][None], terms[1], unused], axis=0)
    d_gated = (grad_time(z_real, z_imag, cos_t, sin_t) * valid).reshape(row_count, width)
    d_projected = jnp.concatenate([d_gated * gate_a, d_gated * value, d_gate_b], axis=1).astype(
        jnp.bfloat16
    )
    grad_mixer_in = jnp.einsum("rd,rk->dk", normed, d_projected, preferred_element_type=jnp.float32)
    d_normed = jnp.einsum("rk,dk->rd", d_projected, mixer_in, preferred_element_type=jnp.float32)
    _, first_back = jax.vjp(plain_norm, x_full, norm_gain, norm_bias)
    d_x_norm, grad_norm_gain, grad_norm_bias = first_back(d_normed)
    grad_inputs = (d_middle + d_x_norm).reshape(seqs, block_len, width)
    _, kernel_back = jax.vjp(lambda kern: kernel_freq(kern, cos_t, sin_t), kernel)
    d_kernel = kernel_back((dk_real, dk_imag))[0]
    dense = [
        grad_norm_gain,
        grad_norm_bias,
        grad_mixer_in,
        grad_mixer_out,
        grad_second_gain,
        grad_second_bias,
        grad_up,
        grad_down,
    ]
    summed = sum_everywhere([d_kernel] + dense)
    filter_grads = filter_back(summed[0])
    dense_sums = summed[1:]
    return (
        output,
        grad_inputs,
        dense_sums[0],
        dense_sums[1],
        dense_sums[2],
        filter_grads[0],
        filter_grads[1],
        filter_grads[2],
        filter_grads[3],
        filter_grads[4],
        dense_sums[3],
        dense_sums[4],
        dense_sums[5],
        dense_sums[6],
        dense_sums[7],
    )


SPECS_IN = (P("dp", "seq", None), P("dp")) + (P(),) * 13 + (P("dp", "seq", None),)
SPECS_OUT = (P("dp", "seq", None), P("dp", "seq", None)) + (P(),) * 13


def solution(mesh):
    local = chip_local if (mesh.shape["seq"], mesh.shape["dp"]) == (8, 4) else block_local
    return jax.shard_map(local, mesh=mesh, in_specs=SPECS_IN, out_specs=SPECS_OUT, check_vma=False)
```

```python
import math

import jax
import jax.numpy as jnp
import numpy as np
from jax import lax
from jax.experimental import pallas as pl
from jax.experimental.pallas import tpu as pltpu
from jax.sharding import PartitionSpec as P

AX = ("seq", "dp")
HIGH = lax.Precision.HIGHEST
EPSILON = 1e-05
BANDS = 16
KL = 2048
F32 = jnp.float32
BF16 = jnp.bfloat16


def mm(a, b, ca=1, cb=0):
    return lax.dot_general(a, b, (((ca,), (cb,)), ((), ())), preferred_element_type=F32)


def perm_of(f):
    pairs = []
    for z in range(4):
        for x in range(2):
            for y in range(2):
                for c in range(2):
                    a, b, d, e = f(z, x, y, c)
                    pairs.append(((z * 2 + x) * 4 + y * 2 + c, (a * 2 + b) * 4 + d * 2 + e))
    return pairs


PC = perm_of(lambda z, x, y, c: (z, x, y, 1 - c))
PX = perm_of(lambda z, x, y, c: (z, 1 - x, y, c))
PY = perm_of(lambda z, x, y, c: (z, x, 1 - y, c))
PZ = [perm_of(lambda z, x, y, c, k=k: (z ^ k, x, y, c)) for k in range(4)]


def send(v, perm):
    return lax.ppermute(v, AX, perm)


def tie(*vals):
    return lax.optimization_barrier(tuple(vals))


def swap_in(v, c):
    v = v.reshape(4, 2, 64, v.shape[-1])
    keep = pick(v, c, 1)
    got = send(pick(v, 1 - c, 1), PC)
    return jnp.where(c == 0, jnp.concatenate([keep, got]), jnp.concatenate([got, keep]))


def exchange_seq(v):
    return lax.all_to_all(v, "seq", 0, 0)


def swap_out(v, c):
    v = v.reshape(2, 4, 64, v.shape[-1])
    keep = pick(v, c)
    got = send(pick(v, 1 - c), PC)
    m = jnp.stack([jnp.where(c == 0, keep, got), jnp.where(c == 0, got, keep)], axis=1)
    return m.reshape(4, 128, v.shape[-1])


def both(own, c):
    other = send(own, PC)
    return jnp.stack([jnp.where(c == 0, own, other), jnp.where(c == 0, other, own)], axis=1)


def feature_table(taps):
    steps = np.arange(taps, dtype=np.float64) / KL
    freqs = np.arange(1, BANDS + 1, dtype=np.float64)
    phase = 2.0 * math.pi * steps[:, None] * freqs[None, :]
    return np.concatenate([steps[:, None], np.cos(phase), np.sin(phase)], axis=1).astype(np.float32)


def dft_table(length):
    f = 2 * np.arange(length, dtype=np.int64)[:, None] + 1
    n = np.arange(length, dtype=np.int64)[None, :]
    angle = (f * n % (4 * length)) * (2.0 * math.pi / (4 * length))
    return np.concatenate([np.cos(angle), -np.sin(angle)], axis=0).astype(np.float32)


def norm_parts(v):
    center = v - jnp.mean(v, axis=-1, keepdims=True)
    spread_ = jnp.mean(center * center, axis=-1, keepdims=True)
    inv = lax.rsqrt(spread_ + EPSILON)
    return center * inv, inv


def norm_back(q, hat, inv):
    return (q - jnp.mean(q, -1, keepdims=True) - hat * jnp.mean(q * hat, -1, keepdims=True)) * inv


def lanes(a, at, size):
    return lax.dynamic_slice_in_dim(a, at, size, axis=1)


def in_order(bit, own, other, axis=0):
    first = jnp.where(bit == 0, own, other)
    second = jnp.where(bit == 0, other, own)
    return jnp.concatenate([first, second], axis=axis)


def pick(a, i, axis=0):
    return lax.dynamic_index_in_dim(a, i, axis, keepdims=False)


GELU_A = math.sqrt(2.0 / math.pi)
GELU_B = 0.044715


def gelu_pair(v):
    sq = v * v
    t = jnp.tanh(GELU_A * v * (1.0 + GELU_B * sq))
    up = 0.5 * (1.0 + t)
    return v * up, up + 0.5 * v * (1.0 - t * t) * (GELU_A * (1.0 + 3.0 * GELU_B * sq))


def nn(a, b):
    return jnp.dot(a, b, preferred_element_type=F32)


def nt(a, b):
    return lax.dot_general(a, b, (((1,), (1,)), ((), ())), preferred_element_type=F32)


def tn(a, b):
    return lax.dot_general(a, b, (((0,), (0,)), ((), ())), preferred_element_type=F32)


def stats(v):
    center = v - jnp.mean(v, axis=-1, keepdims=True)
    inv = lax.rsqrt(jnp.mean(center * center, axis=-1, keepdims=True) + EPSILON)
    return center * inv, inv


def loop(n, body):
    def step(i, carry):
        body(i)
        return carry

    lax.fori_loop(0, n, step, 0)


def at(i, size, least=64):
    return pl.ds(pl.multiple_of(i * size, least), size)


CHUNKS = tuple(slice(256 * q, 256 * (q + 1)) for q in range(4))


def tokens(c, own, other, q):
    parts = []
    for p in (2 * q, 2 * q + 1):
        a, b = own[p].astype(F32), other[p].astype(F32)
        parts += [jnp.where(c == 0, a, b), jnp.where(c == 0, b, a)]
    return jnp.concatenate(parts, axis=0)


def set_own(ref, q, c, tile, mine=True):
    for n in range(2):
        first, second = tile[128 * n : 128 * n + 64], tile[128 * n + 64 : 128 * n + 128]
        ref[2 * q + n] = jnp.where((c == 0) == mine, first, second).astype(ref.dtype)


ANY = pl.BlockSpec(memory_space=pl.ANY)


NO_COST = pl.CostEstimate(flops=3 * 10**8, bytes_accessed=0, transcendentals=0)


class Chain:
    last = None

    def note(self, outs):
        self.last = min(jax.tree_util.tree_leaves(outs), key=lambda v: v.size * v.dtype.itemsize)

    def __call__(self, body, at, **kwargs):
        def run(*args):
            if self.last is not None:
                inner = body
                kwargs["in_specs"] = kwargs["in_specs"][:at] + [ANY] + kwargs["in_specs"][at:]
                alias = kwargs.get("input_output_aliases", {})
                kwargs["input_output_aliases"] = {i + (i >= at): o for i, o in alias.items()}

                def outer(*refs):
                    inner(*refs[:at], *refs[at + 1 :])

                args = args[:at] + (self.last,) + args[at:]
            else:
                outer = body
            outs = pl.pallas_call(outer, cost_estimate=NO_COST, **kwargs)(*args)
            self.note(outs)
            return outs

        return run


CHAIN = Chain()


def call(body, name, grid, scalars, ins, outs, scratch=(), vmem=60):
    def spec(block, index):
        return ANY if block is None else pl.BlockSpec(block, index)

    specs = [spec(b, i) for _, b, i in ins]
    arrays = [a for a, _, _ in ins]
    inner = body
    if CHAIN.last is not None:
        specs, arrays = [ANY] + specs, [CHAIN.last] + arrays

        def inner(scalar, extra, *refs):
            body(scalar, *refs)

    got = pl.pallas_call(
        inner,
        grid_spec=pltpu.PrefetchScalarGridSpec(
            num_scalar_prefetch=1,
            grid=(grid,),
            in_specs=specs,
            out_specs=[spec(b, i) for _, _, b, i in outs],
            scratch_shapes=list(scratch),
        ),
        out_shape=[jax.ShapeDtypeStruct(s, t) for s, t, _, _ in outs],
        compiler_params=pltpu.CompilerParams(
            dimension_semantics=("arbitrary",), vmem_limit_bytes=vmem * 2**20
        ),
        name=name,
        cost_estimate=NO_COST,
    )(scalars, *arrays)
    CHAIN.note(got)
    return got


def whole(a):
    return (a, a.shape, lambda g, i, n=a.ndim: (0,) * n)


def step_from(first, count, lead=0, tail=1):
    def index(g, info):
        return (0,) * lead + (jnp.clip(g - first, 0, count - 1),) + (0,) * tail

    return index


class Copies:
    def __init__(self, sem):
        self.sem, self.count, self.out = sem, 0, []

    def load(self, src, dst):
        copy = pltpu.make_async_copy(src, dst, self.sem.at[self.count])
        self.count += 1
        copy.start()
        return copy

    def store(self, src, dst):
        self.out.append(self.load(src, dst))

    def finish(self):
        for copy in self.out:
            copy.wait()


def wait(*copies):
    for copy in copies:
        copy.wait()


def straight(body, name, scalars, rows_in, ins, outs, scratch, n_copies, vmem=60):
    return CHAIN(
        body,
        1,
        in_specs=[pl.BlockSpec(memory_space=pltpu.SMEM)]
        + [pl.BlockSpec(memory_space=pltpu.VMEM)] * len(rows_in)
        + [ANY] * len(ins),
        out_specs=[ANY] * len(outs),
        out_shape=[jax.ShapeDtypeStruct(s, t) for s, t in outs],
        scratch_shapes=[pltpu.VMEM(s, t) for s, t in scratch] + [pltpu.SemaphoreType.DMA((n_copies,))],
        compiler_params=pltpu.CompilerParams(vmem_limit_bytes=vmem * 2**20),
        name=name,
    )(scalars, *rows_in, *ins)


def part_of(ref, axis, start, size):
    span = pl.ds(pl.multiple_of(start, 128), size)
    return ref.at[span, :] if axis == 0 else ref.at[:, span]


def front(info, x_own, x_other, gain, bias, mixer_in, wave, spec, back, mixer_out):
    width = mixer_in.shape[0]
    half = width // 2
    rows = wave.shape[1]

    def body(info, gain, bias, x_own, x_other, w_in, wave, spec, back, w_mo,
             normed_o, value_o, gate_a_o, gate_b_o, zf_o, mixed_o, gated_out_o, part_o,
             xo, xt, w3, wv, sp, bk, wm, normed, value, gate_a, gate_b, gated, prod, zf, mixed, gated_out, part, sem):
        c, length = info[0], info[1]
        io = Copies(sem)
        x_in = [(io.load(x_own.at[pl.ds(2 * q, 2)], xo.at[pl.ds(2 * q, 2)]),
                 io.load(x_other.at[pl.ds(2 * q, 2)], xt.at[pl.ds(2 * q, 2)])) for q in range(4)]
        w_got = [io.load(part_of(w_in, 1, n * width + c * half, half), w3.at[n]) for n in range(3)]
        f_got = []
        for q in range(2):
            span = pl.ds(512 * q, 512)
            f_got.append((io.load(wave.at[:, span], wv.at[:, span]), io.load(spec.at[:, span], sp.at[:, span])))
        b_got = [io.load(back.at[pl.ds(512 * q, 512)], bk.at[pl.ds(512 * q, 512)]) for q in range(2)]
        m_got = io.load(part_of(w_mo, 0, c * half, half), wm)
        for q, span in enumerate(CHUNKS):
            wait(*x_in[q])
            hat, _ = stats(tokens(c, xo, xt, q))
            normed[span, :] = (hat * gain[...] + bias[...]).astype(BF16)
        io.store(normed, normed_o)
        wait(w_got[0])
        v = nn(normed[...], w3[0])
        value[...] = v.astype(BF16)
        io.store(value, value_o)
        wait(w_got[1])
        a = nn(normed[...], w3[1])
        gate_a[...] = a.astype(BF16)
        io.store(gate_a, gate_a_o)
        at_row = lax.broadcasted_iota(jnp.int32, a.shape, 0)
        gated[...] = jnp.where(at_row < length, v * a, 0.0).astype(BF16)
        wait(w_got[2])
        gate_b[...] = nn(normed[...], w3[2]).astype(BF16)
        io.store(gate_b, gate_b_o)
        for q in range(2):
            span, low = slice(512 * q, 512 * q + 512), slice(rows + 512 * q, rows + 512 * q + 512)
            wait(*f_got[q])
            re = nn(wv[0, span], gated[...])
            im = nn(wv[1, span], gated[...])
            zf[0, span] = re.astype(BF16)
            zf[1, span] = im.astype(BF16)
            kr, ki = sp[0, span], sp[1, span]
            prod[span, :] = (kr * re - ki * im).astype(BF16)
            prod[low, :] = (kr * im + ki * re).astype(BF16)
        io.store(zf, zf_o)
        for q in range(2):
            span = slice(512 * q, 512 * q + 512)
            wait(b_got[q])
            m = nn(bk[span, :], prod[...])
            mixed[span, :] = m.astype(BF16)
            out = (gate_b[span, :].astype(F32) * m).astype(BF16)
            gated_out[span, :] = out
            if q == 0:
                wait(m_got)
            part[span, :] = nn(out, wm[...]).astype(BF16)
            here = pl.ds(512 * q, 512)
            io.store(part.at[here], part_o.at[here])
        io.store(mixed, mixed_o)
        io.store(gated_out, gated_out_o)
        io.finish()

    thin, wide = ((rows, half), BF16), ((rows, width), BF16)
    tok = ((8, 64, width), BF16)
    return straight(
        body, "front", info, [gain, bias], [x_own, x_other, mixer_in, wave, spec, back, mixer_out],
        [wide, thin, thin, thin, ((2, rows, half), BF16), thin, thin, wide],
        [tok, tok, ((3, width, half), BF16), (wave.shape, BF16), (spec.shape, F32), (back.shape, BF16),
         ((half, width), BF16), wide, thin, thin, thin, thin, ((2 * rows, half), BF16), ((2, rows, half), BF16), thin,
         thin, wide],
        8 + 3 + 4 + 2 + 1 + 9,
    )


def grad_shapes(rows, width):
    one = ((rows, width), BF16)
    return [one, one, ((2, rows, width), BF16)]


def make_grads(io, info, left, right, grad, send_a_o, send_b_o, keeps_o):
    for g, out in enumerate((send_a_o, send_b_o, keeps_o.at[0], keeps_o.at[1])):
        n = info[2 + g]
        grad[g] = tn(left(n), right(n)).astype(BF16)
        io.store(grad.at[g], out)


def up_grads(info, d_pre, normed):
    rows, ff = d_pre.shape
    width = normed.shape[1]

    def body(info, d_pre, normed, send_a_o, send_b_o, keeps_o, left, right, grad, sem):
        io = Copies(sem)
        l_in = []
        for g in range(4):
            l_in.append(io.load(part_of(d_pre, 1, info[2 + g] * (ff // 4), ff // 4), left.at[g]))
            if g == 0:
                r_in = io.load(normed, right)
        wait(r_in)
        for g, out in enumerate((send_a_o, send_b_o, keeps_o.at[0], keeps_o.at[1])):
            wait(l_in[g])
            grad[g] = tn(left[g], right[...]).astype(BF16)
            io.store(grad.at[g], out)
        io.finish()

    return straight(
        body, "up_grads", info, [], [d_pre, normed], grad_shapes(ff // 4, width),
        [((4, rows, ff // 4), BF16), ((rows, width), BF16), ((4, ff // 4, width), BF16)], 9,
    )


def set_sums(sums, gains, biases):
    sums[...] = jnp.zeros_like(sums)
    sums[0:1, :] = gains
    sums[1:2, :] = biases


def block_of(ref, n, size):
    return ref[:, pl.ds(pl.multiple_of(n * size, 128), size)]


def feed_forward(info, x_own, x_other, cot_own, cot_other, part, got, gain, bias, up_weight, down_weight):
    rows, width = part.shape
    ff = up_weight.shape[1] // 2
    cols = ff // 3

    def body(info, gain, bias, x_own, x_other, cot_own, cot_other, part, got, w_up, w_dn,
             middle_o, normed_o, d_pre_o, cot_o, d_sec_o, sums_o, send_a_o, send_b_o, keeps_o, keep_o, give_o,
             xo, xt, co, ct, pt, gt, up, dn, middle, normed, cot, act, d_pre, d_sec, acc, sums, grad, out, keep, give, sem):
        c = info[0]
        io = Copies(sem)
        x_in, c_in = [], []
        for q, span in enumerate(CHUNKS):
            two, here = pl.ds(2 * q, 2), pl.ds(256 * q, 256)
            x_in.append([io.load(x_own.at[two], xo.at[two]), io.load(x_other.at[two], xt.at[two]),
                         io.load(part.at[here], pt.at[here]), io.load(got.at[here], gt.at[here])])
        u_in = [io.load(part_of(w_up, 1, c * ff, cols), up.at[0])]
        c_in = [io.load(cot_own, co), io.load(cot_other, ct)]
        d_in = [io.load(part_of(w_dn, 0, c * ff, cols), dn.at[0])]
        for n in range(1, 3):
            u_in.append(io.load(part_of(w_up, 1, c * ff + n * cols, cols), up.at[n]))
            d_in.append(io.load(part_of(w_dn, 0, c * ff + n * cols, cols), dn.at[n]))
        for q, span in enumerate(CHUNKS):
            wait(*x_in[q])
            mid = tokens(c, xo, xt, q) + pt[span, :].astype(F32) + gt[span, :].astype(F32)
            middle[span, :] = mid
            hat, _ = stats(mid)
            normed[span, :] = (hat * gain[...] + bias[...]).astype(BF16)
        io.store(middle, middle_o)
        io.store(normed, normed_o)
        wait(*c_in)
        for q, span in enumerate(CHUNKS):
            cot[span, :] = tokens(c, co, ct, q).astype(BF16)
        io.store(cot, cot_o)
        for n in range(3):
            wait(u_in[n], d_in[n])
            v, slope = gelu_pair(nn(normed[...], up[n]))
            here = pl.ds(n * cols, cols)
            act[:, n * cols : (n + 1) * cols] = v.astype(BF16)
            d_pre[n] = (nt(cot[...], dn[n]) * slope).astype(BF16)
            io.store(d_pre.at[n], d_pre_o.at[:, here])
            more = nt(d_pre[n], up[n])
            if n == 0:
                acc[...] = more
            else:
                acc[...] += more
            more = nn(act[:, n * cols : (n + 1) * cols], dn[n])
            if n == 0:
                out[...] = more
            else:
                out[...] += more
        gains, biases = 0.0, 0.0
        for q, span in enumerate(CHUNKS):
            ds = acc[span, :]
            d_sec[span, :] = ds.astype(BF16)
            here = pl.ds(256 * q, 256)
            io.store(d_sec.at[here], d_sec_o.at[here])
            hat, _ = stats(middle[span, :])
            gains += jnp.sum(ds * hat, axis=0, keepdims=True)
            biases += jnp.sum(ds, axis=0, keepdims=True)
            set_own(keep, q, c, out[span, :] + middle[span, :])
            set_own(give, q, c, out[span, :], False)
        set_sums(sums, gains, biases)
        io.store(sums, sums_o)
        io.store(give, give_o)
        io.store(keep, keep_o)
        make_grads(io, info, lambda n: block_of(act, n, ff // 4), lambda n: cot[...], grad, send_a_o, send_b_o, keeps_o)
        io.finish()

    tok, wide, long = ((8, 64, width), BF16), ((rows, width), BF16), ((rows, ff), BF16)
    full = ((rows, width), F32)
    slab = ((3, rows, cols), BF16)
    return straight(
        body, "feed_forward", info, [gain, bias],
        [x_own, x_other, cot_own, cot_other, part, got, up_weight, down_weight],
        [full, wide, long, wide, wide, ((8, width), F32)] + grad_shapes(ff // 4, width) + [((8, 64, width), F32), tok],
        [tok, tok, tok, tok, wide, wide, ((3, width, cols), BF16), ((3, cols, width), BF16), full, wide, wide, long, slab,
         wide, full, ((8, width), F32), ((4, ff // 4, width), BF16), full, ((8, 64, width), F32), tok],
        16 + 2 + 6 + 3 + 3 + 5 + 2 + 4,
    )


def backward(
    info, d_sec, got, middle, cot, gain, mixer_out, mixed, gate_b, value, gate_a, wave, spec, zf, back, normed, gated_out
):
    rows, width = middle.shape
    half = width // 2

    def body(info, gain, d_sec, got, middle, cot, w_mo, mixed, gate_b, value, gate_a, wave, spec, zf, back,
             normed, gated_out, d_own_o, tf_o, d_proj_o, send_a_o, send_b_o, keeps_o,
             ds, gt, md, cs, wm, mx, gb, vl, ga, wv, sp, zs, bk, right, d_own, d_gb, d_mixed, prod, tf, left, grad, sem):
        c, length = info[0], info[1]
        io = Copies(sem)
        first = []
        for q in range(4):
            here = pl.ds(256 * q, 256)
            first.append([io.load(s.at[here], t.at[here]) for s, t in ((middle, md), (d_sec, ds), (got, gt), (cot, cs))])
        go_in = [io.load(part_of(w_mo, 0, c * half, half), wm), io.load(mixed, mx), io.load(gate_b, gb)]
        f_in = []
        for q in range(2):
            span = pl.ds(512 * q, 512)
            f_in.append([io.load(s.at[:, span], t.at[:, span]) for s, t in ((wave, wv), (spec, sp), (zf, zs))])
        b_in = [io.load(back.at[pl.ds(512 * q, 512)], bk.at[pl.ds(512 * q, 512)]) for q in range(2)]
        v_in = [io.load(value, vl), io.load(gate_a, ga)]
        g_in = [io.load(normed, right.at[0]), io.load(gated_out, left.at[:, pl.ds(3 * half, half)])]
        d_mid = right.at[1]
        for q, span in enumerate(CHUNKS):
            wait(*first[q])
            hat, inv = stats(md[span, :])
            t = (ds[span, :].astype(F32) + gt[span, :].astype(F32)) * gain[...]
            v = cs[span, :].astype(F32) + norm_back(t, hat, inv)
            d_mid[span, :] = v.astype(BF16)
            set_own(d_own, q, c, v)
        io.store(d_own, d_own_o)
        wait(*go_in)
        d_go = nt(d_mid[...], wm[...])
        d_gb[...] = (d_go * mx[...].astype(F32)).astype(BF16)
        d_mixed[...] = (d_go * gb[...].astype(F32)).astype(BF16)
        for q in range(2):
            span, low = slice(512 * q, 512 * q + 512), slice(rows + 512 * q, rows + 512 * q + 512)
            wait(*f_in[q])
            re = nn(wv[0, span], d_mixed[...])
            im = nn(wv[1, span], d_mixed[...])
            kr, ki = sp[0, span], sp[1, span]
            prod[span, :] = (kr * re + ki * im).astype(BF16)
            prod[low, :] = (kr * im - ki * re).astype(BF16)
            zr, zi = zs[0, span].astype(F32), zs[1, span].astype(F32)
            tf[0, span] = ((zr * re + zi * im) * (1.0 / rows)).astype(BF16)
            tf[1, span] = ((zr * im - zi * re) * (1.0 / rows)).astype(BF16)
        io.store(tf, tf_o)
        wait(*v_in)
        for q in range(2):
            span = slice(512 * q, 512 * q + 512)
            wait(b_in[q])
            m = nn(bk[span, :], prod[...])
            at_row = 512 * q + lax.broadcasted_iota(jnp.int32, m.shape, 0)
            m = jnp.where(at_row < length, m, 0.0)
            left[span, 0:half] = (m * ga[span, :].astype(F32)).astype(BF16)
            left[span, half : 2 * half] = (m * vl[span, :].astype(F32)).astype(BF16)
            left[span, 2 * half : 3 * half] = d_gb[span, :]
            here = pl.ds(512 * q, 512)
            io.store(left.at[here, pl.ds(0, 3 * half)], d_proj_o.at[here])
        wait(*g_in)
        make_grads(
            io, info, lambda n: block_of(left, n, half), lambda n: right[n // 3], grad, send_a_o, send_b_o, keeps_o
        )
        io.finish()

    wide, thin, full = ((rows, width), BF16), ((rows, half), BF16), ((rows, width), F32)
    own, freq, proj = ((8, 64, width), F32), ((2, rows, half), BF16), ((rows, 3 * half), BF16)
    return straight(
        body, "backward", info, [gain],
        [d_sec, got, middle, cot, mixer_out, mixed, gate_b, value, gate_a, wave, spec, zf, back, normed, gated_out],
        [own, freq, proj] + grad_shapes(half, width),
        [wide, wide, full, wide, ((half, width), BF16), thin, thin, thin, thin, (wave.shape, BF16), (spec.shape, F32),
         freq, (back.shape, BF16), ((2, rows, width), BF16), own, thin, thin, ((2 * rows, half), BF16), freq,
         ((rows, 4 * half), BF16), ((4, half, width), BF16)],
        16 + 3 + 6 + 2 + 2 + 2 + 4 + 4,
    )


def norm_in_back(info, d_proj, mixer_in, x_own, x_other):
    rows = d_proj.shape[0]
    width = mixer_in.shape[0]
    half = width // 2

    def body(info, d_proj, w_in, x_own, x_other, keep_o, give_o, sums_o,
             dp, w3, xo, xt, acc, keep, give, sums, sem):
        c = info[0]
        io = Copies(sem)
        got = []
        for n in range(3):
            got.append([io.load(d_proj.at[:, pl.ds(n * half, half)], dp.at[n]),
                        io.load(part_of(w_in, 1, n * width + c * half, half), w3.at[n])])
        x_in = [io.load(x_own, xo), io.load(x_other, xt)]
        for n in range(3):
            wait(*got[n])
            more = nt(dp[n], w3[n])
            if n == 0:
                acc[...] = more
            else:
                acc[...] += more
        wait(*x_in)
        gains, biases = 0.0, 0.0
        for q, span in enumerate(CHUNKS):
            dn = acc[span, :]
            hat, _ = stats(tokens(c, xo, xt, q))
            gains += jnp.sum(dn * hat, axis=0, keepdims=True)
            biases += jnp.sum(dn, axis=0, keepdims=True)
            set_own(keep, q, c, dn)
            set_own(give, q, c, dn, False)
        io.store(give, give_o)
        io.store(keep, keep_o)
        set_sums(sums, gains, biases)
        io.store(sums, sums_o)
        io.finish()

    tok = ((8, 64, width), BF16)
    own = ((8, 64, width), F32)
    return straight(
        body, "norm_in_back", info, [], [d_proj, mixer_in, x_own, x_other], [own, tok, ((8, width), F32)],
        [((3, rows, half), BF16), ((3, width, half), BF16), tok, tok, ((rows, width), F32), own, tok,
         ((8, width), F32)],
        11,
        vmem=28,
    )


def filter_back(info, tf, spread, f_out, slope2, slope1, turn, sides, back, norm_sums, second_sums):
    rows, half = tf.shape[1:]
    width = 2 * half

    def body(info, spread, f_out, slope2, slope1, turn, sides, norm_s, second_s, tf, back, out_o,
             tv, bk, out, sem):
        io = Copies(sem)
        t_in = [io.load(tf.at[n], tv.at[pl.ds(n * rows, rows)]) for n in range(2)]
        b_in = [io.load(back.at[pl.ds(512 * q, 512)], bk.at[pl.ds(512 * q, 512)]) for q in range(2)]
        wait(*t_in)
        g_fo = tn(spread[...], tv[...])[0:64] * float(rows)
        kf = nt(tv[...], f_out[...]).astype(BF16)
        wait(*b_in)
        d_s = slope2[...] * nn(bk[...], kf)
        high = lax.Precision.HIGHEST
        both = d_s + slope1[...] * jnp.dot(d_s, turn[...], precision=high, preferred_element_type=F32)
        g = tn(sides[...].astype(BF16), both.astype(BF16))
        lane = lax.broadcasted_iota(jnp.int32, (64, 128), 1)
        g = jnp.where(lane < 64, g[0:64], g[64:128])
        out[...] = jnp.zeros_like(out)
        out[0:32, 0:half] = g_fo[0:32].astype(BF16)
        out[0:32, half:] = g_fo[32:64].astype(BF16)
        for n in range(6):
            pair = [g[8 * n : 8 * n + 8]]
            if n < 2:
                pair.append(g[48 + 8 * n : 56 + 8 * n])
            elif n == 2:
                pair.append(jnp.broadcast_to(jnp.sum(both, axis=0, keepdims=True), (8, 128)))
            else:
                pair.append(jnp.zeros((8, 128), F32))
            out[32:48, 128 * n : 128 * n + 128] = jnp.concatenate(pair, axis=0).astype(BF16)
        out[48:64, :] = jnp.concatenate([norm_s[...], second_s[...]], axis=0).astype(BF16)
        io.store(out, out_o)
        io.finish()

    return straight(
        body, "filter_back", info, [spread, f_out, slope2, slope1, turn, sides, norm_sums, second_sums], [tf, back],
        [((64, width), BF16)],
        [((2 * rows, half), BF16), (back.shape, BF16), ((64, width), BF16)], 5, vmem=22,
    )[0]


def unpack_small(info, own, got):
    width = own.shape[1]
    half = width // 2

    def body(info, own, got, g_fo, g_fm, g_fi, b_m, b_f, norms, seconds):
        a, b = own[0:64, :].astype(F32), got[0:64, :].astype(F32)
        lo = jnp.where(info[0] == 0, a[0:32], b[0:32])
        hi = jnp.where(info[0] == 0, b[0:32], a[0:32])
        g_fo[0:32, 0:half], g_fo[32:64, 0:half] = lo[:, 0:half], lo[:, half:]
        g_fo[0:32, half:], g_fo[32:64, half:] = hi[:, 0:half], hi[:, half:]
        s = a[32:64] + b[32:64]
        tiles = [s[0:8, 128 * n : 128 * n + 128] for n in range(6)] + [s[8:16, 128 * n : 128 * n + 128] for n in range(3)]
        g = jnp.concatenate(tiles[:8], axis=0)
        g_fm[...] = g[:, 0:64]
        g_fi[...] = g[0:33, 64:128]
        b_m[...] = tiles[8][0:1, 0:64]
        b_f[...] = tiles[8][0:1, 64:128]
        norms[...] = s[16:24]
        seconds[...] = s[24:32]

    shapes = [(64, width), (64, 64), (33, 64), (1, 64), (1, 64), (8, width), (8, width)]
    return CHAIN(
        body,
        1,
        in_specs=[pl.BlockSpec(memory_space=pltpu.SMEM)] + [pl.BlockSpec(memory_space=pltpu.VMEM)] * 2,
        out_specs=[pl.BlockSpec(memory_space=pltpu.VMEM)] * len(shapes),
        out_shape=[jax.ShapeDtypeStruct(s, F32) for s in shapes],
        compiler_params=pltpu.CompilerParams(vmem_limit_bytes=16 * 2**20),
        name="unpack_small",
    )(info, own, got)


def finish_output(out_keep, out_got):
    def body(out_keep, out_got, out):
        out[...] = (out_keep[...] + out_got[...].astype(F32)).astype(BF16)

    return CHAIN(
        body,
        0,
        in_specs=[pl.BlockSpec(memory_space=pltpu.VMEM)] * 2,
        out_specs=pl.BlockSpec(memory_space=pltpu.VMEM),
        out_shape=jax.ShapeDtypeStruct(out_keep.shape, BF16),
        compiler_params=pltpu.CompilerParams(vmem_limit_bytes=16 * 2**20),
        name="finish_output",
    )(out_keep, out_got)


def finish_inputs(gain, d_norm_keep, d_norm_got, d_mid_own, x_half):
    def body(gain, d_norm_keep, d_norm_got, d_mid_own, x_half, out):
        for p in range(x_half.shape[0]):
            hat, inv = stats(x_half[p].astype(F32))
            q = (d_norm_keep[p] + d_norm_got[p].astype(F32)) * gain[...]
            out[p] = (d_mid_own[p] + norm_back(q, hat, inv)).astype(BF16)

    return CHAIN(
        body,
        0,
        in_specs=[pl.BlockSpec(memory_space=pltpu.VMEM)] * 5,
        out_specs=pl.BlockSpec(memory_space=pltpu.VMEM),
        out_shape=jax.ShapeDtypeStruct(x_half.shape, BF16),
        compiler_params=pltpu.CompilerParams(vmem_limit_bytes=24 * 2**20),
        name="finish_inputs",
    )(gain, d_norm_keep, d_norm_got, d_mid_own, x_half)


def split_back(info, got):
    _, n, width = got.shape

    def body(info, got, keep, give):
        keep[...] = got[pl.ds(4 * info[0], 4)]
        give[...] = got[pl.ds(4 - 4 * info[0], 4)]

    return small(body, "split_back", [((4, n, width), BF16)] * 2, info, got)


def join_back(info, keep, got, dtype):
    _, n, width = keep.shape

    def body(info, keep, got, out):
        a, b = keep[...].astype(F32), got[...].astype(F32)
        out[:, 0:n, :] = jnp.where(info[0] == 0, a, b).astype(dtype)
        out[:, n:, :] = jnp.where(info[0] == 0, b, a).astype(dtype)

    return small(body, "join_back", [((4, 2 * n, width), dtype)], info, keep, got)[0]


def small(body, name, outs, *ins):
    return CHAIN(
        body,
        1,
        in_specs=[pl.BlockSpec(memory_space=pltpu.SMEM)] + [pl.BlockSpec(memory_space=pltpu.VMEM)] * (len(ins) - 1),
        out_specs=[pl.BlockSpec(memory_space=pltpu.VMEM)] * len(outs),
        out_shape=[jax.ShapeDtypeStruct(s, t) for s, t in outs],
        compiler_params=pltpu.CompilerParams(vmem_limit_bytes=16 * 2**20),
        name=name,
    )(*ins)


def plus(a, b):
    return (a.astype(F32) + b.astype(F32)).astype(BF16)


class Reducer:
    def __init__(self, pos, send_a, send_b, keeps):
        self.pos, self.keeps = pos, keeps
        self.rows, self.cols = send_a.shape
        self.got = (send(send_a, PX), send(send_b, PY))

    def step2(self):
        n = self.rows // 2

        def body(pos, keeps, got_a, got_b, out_a, out_b, keep):
            for k, (got, out) in enumerate(((got_a, out_a), (got_b, out_b))):
                p = pos[1 - k]
                mine, others = at(p, n), at(1 - p, n)
                out[...] = plus(keeps[k, others, :], got[others, :])
                keep[k] = plus(keeps[k, mine, :], got[mine, :])

        a, b, self.keeps = small(
            body, "step2", [((n, self.cols), BF16)] * 2 + [((2, n, self.cols), BF16)], self.pos, self.keeps, *self.got
        )
        self.got = (send(a, PY), send(b, PX))

    def step3(self):
        n = self.rows // 4

        def body(pos, keeps, got_a, got_b, out, keep):
            mine, others = at(pos[2], n, 32), at(1 - pos[2], n, 32)
            for k, got in enumerate((got_a, got_b)):
                out[k] = plus(keeps[k, others, :], got[others, :])
                keep[k] = plus(keeps[k, mine, :], got[mine, :])

        shape = (2, n, self.cols)
        out, self.keeps = small(body, "step3", [(shape, BF16), (shape, BF16)], self.pos, self.keeps, *self.got)
        self.got = (send(out, PZ[1]),)

    def step4(self, extra=None):
        n = self.rows // 2
        self.extra = 0 if extra is None else extra.shape[0]

        def body(pos, keeps, got, *refs):
            out = refs[-1]
            for k in range(2):
                out[k * n // 2 : (k + 1) * n // 2, :] = plus(keeps[k], got[k])
            if extra is not None:
                out[n:, :] = refs[0][...]

        ins = [self.keeps, *self.got] + ([] if extra is None else [extra])
        (self.total,) = small(body, "step4", [((n + self.extra, self.cols), BF16)], self.pos, *ins)
        self.got = (send(self.total, PZ[2]),)

    def step5(self):
        def body(pos, total, got, out):
            out[...] = plus(total[...], got[...])

        (self.total,) = small(body, "step5", [(self.total.shape, BF16)], self.pos, self.total, *self.got)
        self.got = (send(self.total, PZ[1]),)

    def step6(self):
        n, more = self.rows // 4, self.extra

        def body(pos, total, got, out_a, out_b):
            mine, others = at(pos[2], n, 32), at(1 - pos[2], n, 32)
            for k, out in enumerate((out_a, out_b)):
                out[mine, :] = total[k * n : (k + 1) * n, :]
                out[others, :] = got[k * n : (k + 1) * n, :]
            if more:
                out_a[2 * n :, :] = plus(total[2 * n :, :], got[2 * n :, :])

        shapes = [((2 * n + more, self.cols), BF16), ((2 * n, self.cols), BF16)]
        self.own = small(body, "step6", shapes, self.pos, self.total, *self.got)
        self.got = (send(self.own[0], PY), send(self.own[1], PX))

    def step7(self):
        n, more = self.rows // 2, self.extra

        def body(pos, own_a, own_b, got_a, got_b, out_a, out_b):
            for k, (own, got, out) in enumerate(((own_a, got_a, out_a), (own_b, got_b, out_b))):
                p = pos[1 - k]
                out[at(p, n), :] = own[0:n, :]
                out[at(1 - p, n), :] = got[0:n, :]
            if more:
                out_a[2 * n :, :] = plus(own_a[n:, :], got_a[n:, :])

        shapes = [((2 * n + more, self.cols), BF16), ((2 * n, self.cols), BF16)]
        self.near = small(body, "step7", shapes, self.pos, *self.own, *self.got)
        self.got = (send(self.near[0], PX), send(self.near[1], PY))
        self.pair_near = [send(v, PC) for v in self.near]

    def step8(self):
        n, more = self.rows, self.extra

        def body(pos, near, far_a, far_b, out_a, out_b, *sums):
            out_a[...] = far_a[0:n, :]
            out_b[...] = far_b[...]
            if more:
                sums[0][...] = plus(near[n:, :], far_a[n:, :])

        shapes = [((n, self.cols), BF16)] * 2 + ([((more, self.cols), BF16)] if more else [])
        *self.far, = small(body, "step8", shapes, self.pos, self.near[0], *self.got)
        if more:
            self.sum = self.far.pop()
        self.pair_far = [send(v, PC) for v in self.far]


def write(bufs, sources, spots, moves):
    n, m = len(sources), len(bufs)
    rows, cols = sources[1].shape
    turned = any(t for _, _, _, _, t in moves([0, 0, 0]))
    straight_ones = any(not t for _, _, _, _, t in moves([0, 0, 0]))

    def body(*refs):
        spot = refs[0]
        src, out = refs[1 : 1 + n], refs[1 + n + m : 1 + n + 2 * m]
        mark, wide, tall, sem = refs[1 + n + 2 * m :]
        mark[...] = jnp.zeros_like(mark)

        def each(act):
            for k in range(n):
                for when, b, i, j, t in moves([spot[k, e] for e in range(3)]):
                    size = (cols, rows) if t else (rows, cols)
                    src_ref = tall.at[k] if t else wide.at[k]
                    copy = pltpu.make_async_copy(
                        src_ref,
                        out[b].at[pl.ds(pl.multiple_of(i, 128), size[0]), pl.ds(pl.multiple_of(j, 128), size[1])],
                        sem.at[k],
                    )
                    act(k, when, t, copy)

        def begin(k, when, t, copy):
            @pl.when(when)
            def _():
                if t:
                    tall[k] = src[k][0:rows, :].astype(F32).T
                else:
                    wide[k] = src[k][0:rows, :].astype(F32)
                copy.start()

        def finish(k, when, t, copy):
            @pl.when(when)
            def _():
                copy.wait()

        each(begin)
        each(finish)

    return CHAIN(
        body,
        1,
        in_specs=[pl.BlockSpec(memory_space=pltpu.SMEM)] + [pl.BlockSpec(memory_space=pltpu.VMEM)] * n + [ANY] * m,
        out_specs=[ANY] * m + [pl.BlockSpec(memory_space=pltpu.VMEM)],
        out_shape=[jax.ShapeDtypeStruct(b.shape, F32) for b in bufs] + [jax.ShapeDtypeStruct((8, 128), F32)],
        input_output_aliases={1 + n + b: b for b in range(m)},
        scratch_shapes=[
            pltpu.VMEM((n, rows, cols) if straight_ones else (n, 8, 128), F32),
            pltpu.VMEM((n, cols, rows) if turned else (n, 8, 128), F32),
            pltpu.SemaphoreType.DMA((n,)),
        ],
        compiler_params=pltpu.CompilerParams(vmem_limit_bytes=20 * 2**20),
        name="write",
    )(spots, *sources, *bufs)[:-1]


def fresh(*shapes):
    def body(*refs):
        pass

    return pl.pallas_call(
        body, out_specs=[ANY] * len(shapes), out_shape=[jax.ShapeDtypeStruct(s, F32) for s in shapes], name="fresh"
    )()


def write_down(s):
    return [(s[0] >= 0, 0, s[0] * 1536 + s[1] * 768 + s[2] * 384, 0, False)]


def write_up(s):
    return [(s[0] >= 0, 0, 0, s[0] * 1536 + s[1] * 768 + s[2] * 384, True)]


def write_mix(s):
    n = s[1] * 2 + s[2]
    return [(n < 3, 0, 0, n * 768 + s[0] * 384, True), (n == 3, 1, s[0] * 384, 0, False)]


def chip_local(
    inputs, lengths, norm_gain, norm_bias, mixer_in, filter_in, filter_in_bias, filter_mid, filter_mid_bias,
    filter_out, mixer_out, second_gain, second_bias, up_weight, down_weight, cotangent,
):
    CHAIN.last = None
    s = lax.axis_index("seq")
    d = lax.axis_index("dp")
    z, x, y, c = s // 2, s % 2, d // 2, d % 2
    width = inputs.shape[-1]
    rows = 8 * inputs.shape[1]
    half = width // 2
    x_swapped = swap_in(inputs, c)
    cot_half = swap_in(cotangent, c)
    x_half = exchange_seq(x_swapped)
    other_len = send(lengths, PC)
    length = pick(jnp.where(c == (z >> 1), lengths, other_len), (z & 1) * 2 + x)
    tab = [1 - x, 3 - y, x, 2 + y]
    info = jnp.stack([c, length, *tab])
    zero = 0 * c
    pos = jnp.stack([x, y, z & 1, z >> 1])
    near = jnp.stack([jnp.stack(v) for v in ((c, zero, x), (c, zero + 1, y), (1 - c, zero, x), (1 - c, zero + 1, y))])
    far = jnp.stack(
        [jnp.stack(v) for v in ((c, zero, 1 - x), (c, zero + 1, 1 - y), (1 - c, zero, 1 - x), (1 - c, zero + 1, 1 - y))]
    )
    norm_gain, norm_bias = norm_gain[None], norm_bias[None]
    second_gain, second_bias = second_gain[None], second_bias[None]
    filter_in, filter_out, x_swapped = tie(filter_in, filter_out, x_swapped)
    f_out = lanes(filter_out, c * half, half)
    waves = dft_table(rows)
    table = jnp.asarray(waves, BF16)
    wave = table.reshape(2, rows, rows)
    back = jnp.asarray(waves.T, BF16)
    feats = jnp.asarray(feature_table(rows))
    first_act = jnp.dot(feats, filter_in, precision=HIGH) + filter_in_bias
    h1 = jnp.sin(first_act)
    second_act = jnp.dot(h1, filter_mid, precision=HIGH) + filter_mid_bias
    h2 = jnp.sin(second_act)
    h2_hi = h2.astype(BF16)
    h2_lo = (h2 - h2_hi.astype(F32)).astype(BF16)
    hf = mm(table, jnp.concatenate([h2_hi, h2_lo], axis=1))
    hf = (hf[:, :64] + hf[:, 64:]) * (1.0 / rows)
    spec = jnp.dot(hf, f_out, precision=lax.Precision.HIGH).reshape(2, rows, half)
    spread = jnp.pad(hf, ((0, 0), (0, 64))).astype(BF16)
    f_low = jnp.pad(f_out, ((0, 64), (0, 0))).astype(BF16)
    slope2 = jnp.pad(jnp.cos(second_act), ((0, 0), (0, 64)))
    slope1 = jnp.pad(jnp.cos(first_act), ((0, 0), (64, 0)))
    turn = jnp.pad(filter_mid.T, ((0, 64), (64, 0)))
    sides = jnp.concatenate([h1, jnp.pad(feats, ((0, 0), (0, 31)))], axis=1)
    x_half, spec, cot_half, info, near, far, pos, spread, f_low, slope2, slope1, turn, sides = tie(
        x_half, spec, cot_half, info, near, far, pos, spread, f_low, slope2, slope1, turn, sides
    )
    cot_half = exchange_seq(cot_half)
    x_pair = send(x_half, PC)
    normed, value, gate_a, gate_b, zf, mixed, gated_out, part = front(
        info, x_half, x_pair, norm_gain, norm_bias, mixer_in, wave, spec, back, mixer_out
    )
    cot_pair = send(cot_half, PC)
    middle, second_normed, d_pre, cot, d_second, second_sums, *more = feed_forward(
        info, x_half, x_pair, cot_half, cot_pair, part, send(part, PC), second_gain, second_bias, up_weight, down_weight
    )
    out_keep, out_give = more[3:]
    d_second_pair = send(d_second, PC)
    out_got = send(out_give, PC)
    down = Reducer(pos, *more[:3])
    up = Reducer(pos, *up_grads(info, d_pre, second_normed))
    out_back = exchange_seq(finish_output(out_keep, out_got))
    d_mid_own, tf, d_proj, *g_mix = backward(
        info, d_second, d_second_pair, middle, cot, second_gain, mixer_out, mixed, gate_b, value, gate_a, wave,
        spec, zf, back, normed, gated_out,
    )
    mix = Reducer(pos, *g_mix)
    down.step2()
    d_norm_keep, d_norm_give, norm_sums = norm_in_back(info, d_proj, mixer_in, x_half, x_pair)
    d_norm_got = send(d_norm_give, PC)
    up.step2()
    down.step3()
    mix.step2()
    up.step3()
    down.step4()
    tiny = filter_back(
        info, tf, spread, f_low, slope2, slope1, turn, sides, back, norm_sums, second_sums
    )
    mix.step3()
    up.step4(tiny)
    out_keep, out_give = split_back(info, out_back)
    out_got = send(out_give, PC)
    down.step5()
    mix.step4()
    up.step5()
    dx_back = exchange_seq(finish_inputs(norm_gain, d_norm_keep, d_norm_got, d_mid_own, x_half))
    down.step6()
    mix.step5()
    output = join_back(info, out_keep, out_got, BF16)
    down.step7()
    up.step6()
    mix.step6()
    bufs = fresh(down_weight.shape, up_weight.shape, mixer_in.shape, mixer_out.shape)
    down.step8()
    grad_down = write(bufs[:1], [*down.near, *down.pair_near], near, write_down)
    up.step7()
    mix.step7()
    (grad_down,) = write(grad_down, [*down.far, *down.pair_far], far, write_down)
    grad_up = write(bufs[1:2], [*up.near, *up.pair_near], near, write_up)
    grads_two = write(bufs[2:], [*mix.near, *mix.pair_near], near, write_mix)
    dx_keep, dx_give = split_back(info, dx_back)
    dx_got = send(dx_give, PC)
    up.step8()
    tiny_got = send(up.sum, PC)
    grad_inputs = join_back(info, dx_keep, dx_got, F32)
    mix.step8()
    (grad_up,) = write(grad_up, [*up.far, *up.pair_far], far, write_up)
    g_fo, g_fm, g_fi, b_m, b_f, norms, seconds = unpack_small(info, up.sum, tiny_got)
    grad_in, grad_mo = write(grads_two, [*mix.far, *mix.pair_far], far, write_mix)
    return (
        output, grad_inputs, norms[0], norms[1], grad_in, g_fi, b_f[0], g_fm, b_m[0],
        g_fo, grad_mo, seconds[0], seconds[1], grad_up, grad_down,
    )


LAGS = 16


def shifted(value, axis, by):
    devices = lax.axis_size(axis)
    pairs = [(i, i + by) for i in range(devices) if 0 <= i + by < devices]
    return lax.ppermute(value, axis, pairs)


def plain_norm(values, gain, shift):
    center = values - jnp.mean(values, axis=-1, keepdims=True)
    spread = jnp.mean(center * center, axis=-1, keepdims=True)
    return center * lax.rsqrt(spread + EPSILON) * gain + shift


def features_of(taps, bands):
    steps = jnp.arange(taps, dtype=jnp.float32) / taps
    freqs = jnp.arange(1, bands + 1, dtype=jnp.float32)
    phase = 2.0 * math.pi * steps[:, None] * freqs[None, :]
    return jnp.concatenate([steps[:, None], jnp.cos(phase), jnp.sin(phase)], axis=1)


def taps_of(filter_in, filter_in_bias, filter_mid, filter_mid_bias, filter_out):
    table = features_of(KL, BANDS)
    first = jnp.sin(jnp.dot(table, filter_in, precision=HIGH) + filter_in_bias)
    second = jnp.sin(jnp.dot(first, filter_mid, precision=HIGH) + filter_mid_bias)
    return jnp.dot(second, filter_out, precision=HIGH)


def wave_tables(block_len):
    length = 2 * block_len
    index = jnp.arange(length, dtype=jnp.int32)
    angle = (index[:, None] * index[None, :] % length).astype(jnp.float32) * (
        2.0 * math.pi / length
    )
    return (jnp.cos(angle), jnp.sin(angle))


def split_table(table):
    leading = table.astype(jnp.bfloat16)
    remainder = (table - leading.astype(jnp.float32)).astype(jnp.bfloat16)
    return (leading, remainder)


def low_tables(cos_t, sin_t):
    length = cos_t.shape[0]
    half = length // 2
    return (
        split_table(cos_t[:, :half]),
        split_table(sin_t[:, :half]),
        split_table(cos_t[half:] / length),
        split_table(sin_t[half:] / length),
    )


def apply_split(pattern, halves, values):
    first = jnp.einsum(pattern, halves[0], values, preferred_element_type=jnp.float32)
    second = jnp.einsum(pattern, halves[1], values, preferred_element_type=jnp.float32)
    return first + second


def kernel_freq(kernel, cos_t, sin_t):
    block_len = cos_t.shape[0] // 2
    width = kernel.shape[1]
    count = kernel.shape[0] // block_len
    padded = jnp.concatenate(
        [
            jnp.zeros((block_len, width), jnp.float32),
            kernel,
            jnp.zeros((2 * block_len, width), jnp.float32),
        ],
        axis=0,
    )
    pieces = padded.reshape(count + 3, block_len, width)
    segments = jnp.concatenate([pieces[: count + 1], pieces[1 : count + 2]], axis=1)
    real = jnp.einsum("fn,mnd->mfd", cos_t, segments, precision=HIGH)
    imag = -jnp.einsum("fn,mnd->mfd", sin_t, segments, precision=HIGH)
    return (real, imag)


def to_freq(values, tables):
    real = apply_split("fc,scd->sfd", tables[0], values)
    imag = -apply_split("fc,scd->sfd", tables[1], values)
    return (real, imag)


def from_freq(real, imag, cos_t, sin_t):
    length = cos_t.shape[0]
    half = length // 2
    first = jnp.einsum("nf,sfd->snd", cos_t[half:], real, precision=HIGH)
    second = jnp.einsum("nf,sfd->snd", sin_t[half:], imag, precision=HIGH)
    return (first - second) / length


def grad_freq(values, tables):
    real = apply_split("nf,snd->sfd", tables[2], values)
    imag = -apply_split("nf,snd->sfd", tables[3], values)
    return (real, imag)


def grad_time(real, imag, cos_t, sin_t):
    half = cos_t.shape[0] // 2
    first = jnp.einsum("fc,sfd->scd", cos_t[:, :half], real, precision=HIGH)
    second = jnp.einsum("fc,sfd->scd", sin_t[:, :half], imag, precision=HIGH)
    return first - second


def add_forward(acc, k_real, k_imag, values, tables):
    z_real, z_imag = to_freq(values, tables)
    return (acc[0] + k_real * z_real - k_imag * z_imag, acc[1] + k_real * z_imag + k_imag * z_real)


def add_backward(acc, k_real, k_imag, grads, own_real, own_imag, tables):
    d_real, d_imag = grad_freq(grads, tables)
    new_real = acc[0] + k_real * d_real + k_imag * d_imag
    new_imag = acc[1] - k_imag * d_real + k_real * d_imag
    term_real = jnp.sum(own_real * d_real + own_imag * d_imag, axis=0)
    term_imag = jnp.sum(own_real * d_imag - own_imag * d_real, axis=0)
    return ((new_real, new_imag), (term_real, term_imag))


def forward_stack(stack, k_real, k_imag, acc, tables):

    def forward_step(carry, item):
        return (add_forward(carry, item[1], item[2], item[0], tables), None)

    result, _ = lax.scan(forward_step, acc, (stack, k_real, k_imag))
    return result


def backward_stack(stack, k_real, k_imag, acc, own_real, own_imag, tables):

    def backward_step(carry, item):
        return add_backward(carry, item[1], item[2], item[0], own_real, own_imag, tables)

    return lax.scan(backward_step, acc, (stack, k_real, k_imag))


def sum_everywhere(parts):
    flat_grads = jnp.concatenate([piece.reshape(-1) for piece in parts])
    portion = lax.psum_scatter(flat_grads, ("seq", "dp"), scatter_dimension=0, tiled=True)
    summed = lax.all_gather(portion.astype(jnp.bfloat16), ("seq", "dp"), axis=0, tiled=True).astype(
        portion.dtype
    )
    results = []
    offset = 0
    for piece in parts:
        results.append(summed[offset : offset + piece.size].reshape(piece.shape))
        offset = offset + piece.size
    return results


def block_local(
    inputs,
    lengths,
    norm_gain,
    norm_bias,
    mixer_in,
    filter_in,
    filter_in_bias,
    filter_mid,
    filter_mid_bias,
    filter_out,
    mixer_out,
    second_gain,
    second_bias,
    up_weight,
    down_weight,
    cotangent,
):
    seqs, block_len, width = inputs.shape
    row_count = seqs * block_len
    reach = min(LAGS, lax.axis_size("seq") - 1)
    rank = lax.axis_index("seq")
    position = rank * block_len + jnp.arange(block_len, dtype=jnp.int32)
    valid = (position[None, :] < lengths[:, None]).astype(jnp.float32)[:, :, None]
    cos_t, sin_t = wave_tables(block_len)
    tables = low_tables(cos_t, sin_t)
    kernel, filter_back = jax.vjp(
        taps_of, filter_in, filter_in_bias, filter_mid, filter_mid_bias, filter_out
    )
    k_real, k_imag = kernel_freq(kernel, cos_t, sin_t)
    x_full = inputs.astype(jnp.float32).reshape(row_count, width)
    normed = plain_norm(x_full, norm_gain, norm_bias).astype(jnp.bfloat16)
    projected = jnp.dot(normed, mixer_in, preferred_element_type=jnp.float32)
    value = projected[:, :width]
    gate_a = projected[:, width : 2 * width]
    gate_b = projected[:, 2 * width :]
    gated = (value * gate_a).astype(jnp.bfloat16).reshape(seqs, block_len, width) * valid.astype(
        jnp.bfloat16
    )
    own_real, own_imag = to_freq(gated, tables)
    initial = (
        k_real[0] * own_real - k_imag[0] * own_imag,
        k_real[0] * own_imag + k_imag[0] * own_real,
    )
    earlier = []
    for lag in range(1, reach + 1):
        earlier.append(shifted(gated, "seq", lag))
    y_real, y_imag = forward_stack(
        jnp.stack(earlier), k_real[1 : reach + 1], k_imag[1 : reach + 1], initial, tables
    )
    mixed = from_freq(y_real, y_imag, cos_t, sin_t).reshape(row_count, width)
    gated_out = (gate_b * mixed).astype(jnp.bfloat16)
    middle = x_full + jnp.dot(gated_out, mixer_out, preferred_element_type=jnp.float32)
    second_normed = plain_norm(middle, second_gain, second_bias).astype(jnp.bfloat16)
    pre = jnp.dot(second_normed, up_weight, preferred_element_type=jnp.float32)
    activated = jax.nn.gelu(pre, approximate=True).astype(jnp.bfloat16)
    result = middle + jnp.dot(activated, down_weight, preferred_element_type=jnp.float32)
    output = result.astype(jnp.bfloat16).reshape(seqs, block_len, width)
    upstream_low = cotangent.reshape(row_count, width)
    upstream = upstream_low.astype(jnp.float32)
    grad_down = jnp.einsum("rk,rd->kd", activated, upstream_low, preferred_element_type=jnp.float32)
    d_act = jnp.einsum("rd,kd->rk", upstream_low, down_weight, preferred_element_type=jnp.float32)
    _, gelu_back = jax.vjp(lambda arg: jax.nn.gelu(arg, approximate=True), pre)
    d_pre = gelu_back(d_act)[0].astype(jnp.bfloat16)
    grad_up = jnp.einsum("rd,rk->dk", second_normed, d_pre, preferred_element_type=jnp.float32)
    d_second = jnp.einsum("rk,dk->rd", d_pre, up_weight, preferred_element_type=jnp.float32)
    _, second_back = jax.vjp(plain_norm, middle, second_gain, second_bias)
    d_middle_norm, grad_second_gain, grad_second_bias = second_back(d_second)
    d_middle = upstream + d_middle_norm
    d_middle_low = d_middle.astype(jnp.bfloat16)
    grad_mixer_out = jnp.einsum(
        "rk,rd->kd", gated_out, d_middle_low, preferred_element_type=jnp.float32
    )
    d_gated_out = jnp.einsum(
        "rd,kd->rk", d_middle_low, mixer_out, preferred_element_type=jnp.float32
    )
    d_gate_b = d_gated_out * mixed
    d_mixed = (d_gated_out * gate_b).astype(jnp.bfloat16).reshape(seqs, block_len, width)
    empty_freq = jnp.zeros((seqs, 2 * block_len, width), jnp.float32)
    start_acc, own_terms = add_backward(
        (empty_freq, empty_freq), k_real[0], k_imag[0], d_mixed, own_real, own_imag, tables
    )
    unused = jnp.zeros((LAGS - reach, 2 * block_len, width), jnp.float32)
    later = []
    for lead in range(1, reach + 1):
        later.append(shifted(d_mixed, "seq", -lead))
    (z_real, z_imag), terms = backward_stack(
        jnp.stack(later),
        k_real[1 : reach + 1],
        k_imag[1 : reach + 1],
        start_acc,
        own_real,
        own_imag,
        tables,
    )
    dk_real = jnp.concatenate([own_terms[0][None], terms[0], unused], axis=0)
    dk_imag = jnp.concatenate([own_terms[1][None], terms[1], unused], axis=0)
    d_gated = (grad_time(z_real, z_imag, cos_t, sin_t) * valid).reshape(row_count, width)
    d_projected = jnp.concatenate([d_gated * gate_a, d_gated * value, d_gate_b], axis=1).astype(
        jnp.bfloat16
    )
    grad_mixer_in = jnp.einsum("rd,rk->dk", normed, d_projected, preferred_element_type=jnp.float32)
    d_normed = jnp.einsum("rk,dk->rd", d_projected, mixer_in, preferred_element_type=jnp.float32)
    _, first_back = jax.vjp(plain_norm, x_full, norm_gain, norm_bias)
    d_x_norm, grad_norm_gain, grad_norm_bias = first_back(d_normed)
    grad_inputs = (d_middle + d_x_norm).reshape(seqs, block_len, width)
    _, kernel_back = jax.vjp(lambda kern: kernel_freq(kern, cos_t, sin_t), kernel)
    d_kernel = kernel_back((dk_real, dk_imag))[0]
    dense = [
        grad_norm_gain,
        grad_norm_bias,
        grad_mixer_in,
        grad_mixer_out,
        grad_second_gain,
        grad_second_bias,
        grad_up,
        grad_down,
    ]
    summed = sum_everywhere([d_kernel] + dense)
    filter_grads = filter_back(summed[0])
    dense_sums = summed[1:]
    return (
        output,
        grad_inputs,
        dense_sums[0],
        dense_sums[1],
        dense_sums[2],
        filter_grads[0],
        filter_grads[1],
        filter_grads[2],
        filter_grads[3],
        filter_grads[4],
        dense_sums[3],
        dense_sums[4],
        dense_sums[5],
        dense_sums[6],
        dense_sums[7],
    )


SPECS_IN = (P("dp", "seq", None), P("dp")) + (P(),) * 13 + (P("dp", "seq", None),)
SPECS_OUT = (P("dp", "seq", None), P("dp", "seq", None)) + (P(),) * 13


def solution(mesh):
    local = chip_local if (mesh.shape["seq"], mesh.shape["dp"]) == (8, 4) else block_local
    return jax.shard_map(local, mesh=mesh, in_specs=SPECS_IN, out_specs=SPECS_OUT, check_vma=False)
```

```python
import math

import jax
import jax.numpy as jnp
import numpy as np
from jax import lax
from jax.experimental import pallas as pl
from jax.experimental.pallas import tpu as pltpu
from jax.sharding import PartitionSpec as P

AX = ("seq", "dp")
HIGH = lax.Precision.HIGHEST
EPSILON = 1e-05
BANDS = 16
KL = 2048
F32 = jnp.float32
BF16 = jnp.bfloat16


def mm(a, b, ca=1, cb=0):
    return lax.dot_general(a, b, (((ca,), (cb,)), ((), ())), preferred_element_type=F32)


def perm_of(f):
    pairs = []
    for z in range(4):
        for x in range(2):
            for y in range(2):
                for c in range(2):
                    a, b, d, e = f(z, x, y, c)
                    pairs.append(((z * 2 + x) * 4 + y * 2 + c, (a * 2 + b) * 4 + d * 2 + e))
    return pairs


PC = perm_of(lambda z, x, y, c: (z, x, y, 1 - c))
PX = perm_of(lambda z, x, y, c: (z, 1 - x, y, c))
PY = perm_of(lambda z, x, y, c: (z, x, 1 - y, c))
PZ = [perm_of(lambda z, x, y, c, k=k: (z ^ k, x, y, c)) for k in range(4)]


def send(v, perm):
    return lax.ppermute(v, AX, perm)


def tie(*vals):
    return lax.optimization_barrier(tuple(vals))


def swap_in(v, c):
    v = v.reshape(4, 2, 64, v.shape[-1])
    keep = pick(v, c, 1)
    got = send(pick(v, 1 - c, 1), PC)
    return jnp.where(c == 0, jnp.concatenate([keep, got]), jnp.concatenate([got, keep]))


def exchange_seq(v):
    return lax.all_to_all(v, "seq", 0, 0)


def swap_out(v, c):
    v = v.reshape(2, 4, 64, v.shape[-1])
    keep = pick(v, c)
    got = send(pick(v, 1 - c), PC)
    m = jnp.stack([jnp.where(c == 0, keep, got), jnp.where(c == 0, got, keep)], axis=1)
    return m.reshape(4, 128, v.shape[-1])


def both(own, c):
    other = send(own, PC)
    return jnp.stack([jnp.where(c == 0, own, other), jnp.where(c == 0, other, own)], axis=1)


def feature_table(taps):
    steps = np.arange(taps, dtype=np.float64) / KL
    freqs = np.arange(1, BANDS + 1, dtype=np.float64)
    phase = 2.0 * math.pi * steps[:, None] * freqs[None, :]
    return np.concatenate([steps[:, None], np.cos(phase), np.sin(phase)], axis=1).astype(np.float32)


def dft_table(length):
    f = 2 * np.arange(length, dtype=np.int64)[:, None] + 1
    n = np.arange(length, dtype=np.int64)[None, :]
    angle = (f * n % (4 * length)) * (2.0 * math.pi / (4 * length))
    return np.concatenate([np.cos(angle), -np.sin(angle)], axis=0).astype(np.float32)


def norm_parts(v):
    center = v - jnp.mean(v, axis=-1, keepdims=True)
    spread_ = jnp.mean(center * center, axis=-1, keepdims=True)
    inv = lax.rsqrt(spread_ + EPSILON)
    return center * inv, inv


def norm_back(q, hat, inv):
    return (q - jnp.mean(q, -1, keepdims=True) - hat * jnp.mean(q * hat, -1, keepdims=True)) * inv


def lanes(a, at, size):
    return lax.dynamic_slice_in_dim(a, at, size, axis=1)


def in_order(bit, own, other, axis=0):
    first = jnp.where(bit == 0, own, other)
    second = jnp.where(bit == 0, other, own)
    return jnp.concatenate([first, second], axis=axis)


def pick(a, i, axis=0):
    return lax.dynamic_index_in_dim(a, i, axis, keepdims=False)


GELU_A = math.sqrt(2.0 / math.pi)
GELU_B = 0.044715


def gelu_pair(v):
    sq = v * v
    t = jnp.tanh(GELU_A * v * (1.0 + GELU_B * sq))
    up = 0.5 * (1.0 + t)
    return v * up, up + 0.5 * v * (1.0 - t * t) * (GELU_A * (1.0 + 3.0 * GELU_B * sq))


def nn(a, b):
    return jnp.dot(a, b, preferred_element_type=F32)


def nt(a, b):
    return lax.dot_general(a, b, (((1,), (1,)), ((), ())), preferred_element_type=F32)


def tn(a, b):
    return lax.dot_general(a, b, (((0,), (0,)), ((), ())), preferred_element_type=F32)


def stats(v):
    center = v - jnp.mean(v, axis=-1, keepdims=True)
    inv = lax.rsqrt(jnp.mean(center * center, axis=-1, keepdims=True) + EPSILON)
    return center * inv, inv


def loop(n, body):
    def step(i, carry):
        body(i)
        return carry

    lax.fori_loop(0, n, step, 0)


def at(i, size, least=64):
    return pl.ds(pl.multiple_of(i * size, least), size)


CHUNKS = tuple(slice(256 * q, 256 * (q + 1)) for q in range(4))


def tokens(c, own, other, q):
    parts = []
    for p in (2 * q, 2 * q + 1):
        a, b = own[p].astype(F32), other[p].astype(F32)
        parts += [jnp.where(c == 0, a, b), jnp.where(c == 0, b, a)]
    return jnp.concatenate(parts, axis=0)


def set_own(ref, q, c, tile, mine=True):
    for n in range(2):
        first, second = tile[128 * n : 128 * n + 64], tile[128 * n + 64 : 128 * n + 128]
        ref[2 * q + n] = jnp.where((c == 0) == mine, first, second).astype(ref.dtype)


ANY = pl.BlockSpec(memory_space=pl.ANY)


NO_COST = pl.CostEstimate(flops=3 * 10**8, bytes_accessed=0, transcendentals=0)


class Chain:
    last = None

    def note(self, outs):
        self.last = min(jax.tree_util.tree_leaves(outs), key=lambda v: v.size * v.dtype.itemsize)

    def __call__(self, body, at, **kwargs):
        def run(*args):
            if self.last is not None:
                inner = body
                kwargs["in_specs"] = kwargs["in_specs"][:at] + [ANY] + kwargs["in_specs"][at:]
                alias = kwargs.get("input_output_aliases", {})
                kwargs["input_output_aliases"] = {i + (i >= at): o for i, o in alias.items()}

                def outer(*refs):
                    inner(*refs[:at], *refs[at + 1 :])

                args = args[:at] + (self.last,) + args[at:]
            else:
                outer = body
            outs = pl.pallas_call(outer, cost_estimate=NO_COST, **kwargs)(*args)
            self.note(outs)
            return outs

        return run


CHAIN = Chain()


def call(body, name, grid, scalars, ins, outs, scratch=(), vmem=60):
    def spec(block, index):
        return ANY if block is None else pl.BlockSpec(block, index)

    specs = [spec(b, i) for _, b, i in ins]
    arrays = [a for a, _, _ in ins]
    inner = body
    if CHAIN.last is not None:
        specs, arrays = [ANY] + specs, [CHAIN.last] + arrays

        def inner(scalar, extra, *refs):
            body(scalar, *refs)

    got = pl.pallas_call(
        inner,
        grid_spec=pltpu.PrefetchScalarGridSpec(
            num_scalar_prefetch=1,
            grid=(grid,),
            in_specs=specs,
            out_specs=[spec(b, i) for _, _, b, i in outs],
            scratch_shapes=list(scratch),
        ),
        out_shape=[jax.ShapeDtypeStruct(s, t) for s, t, _, _ in outs],
        compiler_params=pltpu.CompilerParams(
            dimension_semantics=("arbitrary",), vmem_limit_bytes=vmem * 2**20
        ),
        name=name,
        cost_estimate=NO_COST,
    )(scalars, *arrays)
    CHAIN.note(got)
    return got


def whole(a):
    return (a, a.shape, lambda g, i, n=a.ndim: (0,) * n)


def step_from(first, count, lead=0, tail=1):
    def index(g, info):
        return (0,) * lead + (jnp.clip(g - first, 0, count - 1),) + (0,) * tail

    return index


class Copies:
    def __init__(self, sem):
        self.sem, self.count, self.out = sem, 0, []

    def load(self, src, dst):
        copy = pltpu.make_async_copy(src, dst, self.sem.at[self.count])
        self.count += 1
        copy.start()
        return copy

    def store(self, src, dst):
        self.out.append(self.load(src, dst))

    def finish(self):
        for copy in self.out:
            copy.wait()


def wait(*copies):
    for copy in copies:
        copy.wait()


def straight(body, name, scalars, rows_in, ins, outs, scratch, n_copies, vmem=60):
    return CHAIN(
        body,
        1,
        in_specs=[pl.BlockSpec(memory_space=pltpu.SMEM)]
        + [pl.BlockSpec(memory_space=pltpu.VMEM)] * len(rows_in)
        + [ANY] * len(ins),
        out_specs=[ANY] * len(outs),
        out_shape=[jax.ShapeDtypeStruct(s, t) for s, t in outs],
        scratch_shapes=[pltpu.VMEM(s, t) for s, t in scratch] + [pltpu.SemaphoreType.DMA((n_copies,))],
        compiler_params=pltpu.CompilerParams(vmem_limit_bytes=vmem * 2**20),
        name=name,
    )(scalars, *rows_in, *ins)


def part_of(ref, axis, start, size):
    span = pl.ds(pl.multiple_of(start, 128), size)
    return ref.at[span, :] if axis == 0 else ref.at[:, span]


def front(info, x_own, x_other, gain, bias, mixer_in, wave, spec, back, mixer_out):
    width = mixer_in.shape[0]
    half = width // 2
    rows = wave.shape[1]

    def body(info, gain, bias, x_own, x_other, w_in, wave, spec, back, w_mo,
             normed_o, value_o, gate_a_o, gate_b_o, zf_o, mixed_o, gated_out_o, part_o,
             xo, xt, w3, wv, sp, bk, wm, normed, value, gate_a, gate_b, gated, prod, zf, mixed, gated_out, part, sem):
        c, length = info[0], info[1]
        io = Copies(sem)
        x_in = [(io.load(x_own.at[pl.ds(2 * q, 2)], xo.at[pl.ds(2 * q, 2)]),
                 io.load(x_other.at[pl.ds(2 * q, 2)], xt.at[pl.ds(2 * q, 2)])) for q in range(4)]
        w_got = [io.load(part_of(w_in, 1, n * width + c * half, half), w3.at[n]) for n in range(3)]
        f_got = []
        for q in range(2):
            span = pl.ds(512 * q, 512)
            f_got.append((io.load(wave.at[:, span], wv.at[:, span]), io.load(spec.at[:, span], sp.at[:, span])))
        b_got = [io.load(back.at[pl.ds(512 * q, 512)], bk.at[pl.ds(512 * q, 512)]) for q in range(2)]
        m_got = io.load(part_of(w_mo, 0, c * half, half), wm)
        for q, span in enumerate(CHUNKS):
            wait(*x_in[q])
            hat, _ = stats(tokens(c, xo, xt, q))
            normed[span, :] = (hat * gain[...] + bias[...]).astype(BF16)
        io.store(normed, normed_o)
        wait(w_got[0])
        v = nn(normed[...], w3[0])
        value[...] = v.astype(BF16)
        io.store(value, value_o)
        wait(w_got[1])
        a = nn(normed[...], w3[1])
        gate_a[...] = a.astype(BF16)
        io.store(gate_a, gate_a_o)
        at_row = lax.broadcasted_iota(jnp.int32, a.shape, 0)
        gated[...] = jnp.where(at_row < length, v * a, 0.0).astype(BF16)
        wait(w_got[2])
        gate_b[...] = nn(normed[...], w3[2]).astype(BF16)
        io.store(gate_b, gate_b_o)
        for q in range(2):
            span, low = slice(512 * q, 512 * q + 512), slice(rows + 512 * q, rows + 512 * q + 512)
            wait(*f_got[q])
            re = nn(wv[0, span], gated[...])
            im = nn(wv[1, span], gated[...])
            zf[0, span] = re.astype(BF16)
            zf[1, span] = im.astype(BF16)
            kr, ki = sp[0, span], sp[1, span]
            prod[span, :] = (kr * re - ki * im).astype(BF16)
            prod[low, :] = (kr * im + ki * re).astype(BF16)
        io.store(zf, zf_o)
        for q in range(2):
            span = slice(512 * q, 512 * q + 512)
            wait(b_got[q])
            m = nn(bk[span, :], prod[...])
            mixed[span, :] = m.astype(BF16)
            out = (gate_b[span, :].astype(F32) * m).astype(BF16)
            gated_out[span, :] = out
            if q == 0:
                wait(m_got)
            part[span, :] = nn(out, wm[...]).astype(BF16)
            here = pl.ds(512 * q, 512)
            io.store(part.at[here], part_o.at[here])
        io.store(mixed, mixed_o)
        io.store(gated_out, gated_out_o)
        io.finish()

    thin, wide = ((rows, half), BF16), ((rows, width), BF16)
    tok = ((8, 64, width), BF16)
    return straight(
        body, "front", info, [gain, bias], [x_own, x_other, mixer_in, wave, spec, back, mixer_out],
        [wide, thin, thin, thin, ((2, rows, half), BF16), thin, thin, wide],
        [tok, tok, ((3, width, half), BF16), (wave.shape, BF16), (spec.shape, F32), (back.shape, BF16),
         ((half, width), BF16), wide, thin, thin, thin, thin, ((2 * rows, half), BF16), ((2, rows, half), BF16), thin,
         thin, wide],
        8 + 3 + 4 + 2 + 1 + 9,
    )


def grad_shapes(rows, width):
    one = ((rows, width), BF16)
    return [one, one, ((2, rows, width), BF16)]


def make_grads(io, info, left, right, grad, send_a_o, send_b_o, keeps_o):
    for g, out in enumerate((send_a_o, send_b_o, keeps_o.at[0], keeps_o.at[1])):
        n = info[2 + g]
        grad[g] = tn(left(n), right(n)).astype(BF16)
        io.store(grad.at[g], out)


def up_grads(info, d_pre, normed):
    rows, ff = d_pre.shape
    width = normed.shape[1]

    def body(info, d_pre, normed, send_a_o, send_b_o, keeps_o, left, right, grad, sem):
        io = Copies(sem)
        l_in = []
        for g in range(4):
            l_in.append(io.load(part_of(d_pre, 1, info[2 + g] * (ff // 4), ff // 4), left.at[g]))
            if g == 0:
                r_in = io.load(normed, right)
        wait(r_in)
        for g, out in enumerate((send_a_o, send_b_o, keeps_o.at[0], keeps_o.at[1])):
            wait(l_in[g])
            grad[g] = tn(left[g], right[...]).astype(BF16)
            io.store(grad.at[g], out)
        io.finish()

    return straight(
        body, "up_grads", info, [], [d_pre, normed], grad_shapes(ff // 4, width),
        [((4, rows, ff // 4), BF16), ((rows, width), BF16), ((4, ff // 4, width), BF16)], 9,
    )


def set_sums(sums, gains, biases):
    sums[...] = jnp.zeros_like(sums)
    sums[0:1, :] = gains
    sums[1:2, :] = biases


def block_of(ref, n, size):
    return ref[:, pl.ds(pl.multiple_of(n * size, 128), size)]


def feed_forward(info, x_own, x_other, cot_own, cot_other, part, got, gain, bias, up_weight, down_weight):
    rows, width = part.shape
    ff = up_weight.shape[1] // 2
    cols = ff // 3

    def body(info, gain, bias, x_own, x_other, cot_own, cot_other, part, got, w_up, w_dn,
             middle_o, normed_o, d_pre_o, cot_o, d_sec_o, sums_o, send_a_o, send_b_o, keeps_o, keep_o, give_o,
             xo, xt, co, ct, pt, gt, up, dn, middle, normed, cot, act, d_pre, d_sec, acc, sums, grad, out, keep, give, sem):
        c = info[0]
        io = Copies(sem)
        x_in, c_in = [], []
        for q, span in enumerate(CHUNKS):
            two, here = pl.ds(2 * q, 2), pl.ds(256 * q, 256)
            x_in.append([io.load(x_own.at[two], xo.at[two]), io.load(x_other.at[two], xt.at[two]),
                         io.load(part.at[here], pt.at[here]), io.load(got.at[here], gt.at[here])])
        u_in = [io.load(part_of(w_up, 1, c * ff, cols), up.at[0])]
        c_in = [io.load(cot_own, co), io.load(cot_other, ct)]
        d_in = [io.load(part_of(w_dn, 0, c * ff, cols), dn.at[0])]
        for n in range(1, 3):
            u_in.append(io.load(part_of(w_up, 1, c * ff + n * cols, cols), up.at[n]))
            d_in.append(io.load(part_of(w_dn, 0, c * ff + n * cols, cols), dn.at[n]))
        for q, span in enumerate(CHUNKS):
            wait(*x_in[q])
            mid = tokens(c, xo, xt, q) + pt[span, :].astype(F32) + gt[span, :].astype(F32)
            middle[span, :] = mid
            hat, _ = stats(mid)
            normed[span, :] = (hat * gain[...] + bias[...]).astype(BF16)
        io.store(middle, middle_o)
        io.store(normed, normed_o)
        wait(*c_in)
        for q, span in enumerate(CHUNKS):
            cot[span, :] = tokens(c, co, ct, q).astype(BF16)
        io.store(cot, cot_o)
        for n in range(3):
            wait(u_in[n], d_in[n])
            v, slope = gelu_pair(nn(normed[...], up[n]))
            here = pl.ds(n * cols, cols)
            act[:, n * cols : (n + 1) * cols] = v.astype(BF16)
            d_pre[n] = (nt(cot[...], dn[n]) * slope).astype(BF16)
            io.store(d_pre.at[n], d_pre_o.at[:, here])
            more = nt(d_pre[n], up[n])
            if n == 0:
                acc[...] = more
            else:
                acc[...] += more
            more = nn(act[:, n * cols : (n + 1) * cols], dn[n])
            if n == 0:
                out[...] = more
            else:
                out[...] += more
        gains, biases = 0.0, 0.0
        for q, span in enumerate(CHUNKS):
            ds = acc[span, :]
            d_sec[span, :] = ds.astype(BF16)
            here = pl.ds(256 * q, 256)
            io.store(d_sec.at[here], d_sec_o.at[here])
            hat, _ = stats(middle[span, :])
            gains += jnp.sum(ds * hat, axis=0, keepdims=True)
            biases += jnp.sum(ds, axis=0, keepdims=True)
            set_own(keep, q, c, out[span, :] + middle[span, :])
            set_own(give, q, c, out[span, :], False)
        set_sums(sums, gains, biases)
        io.store(sums, sums_o)
        io.store(give, give_o)
        io.store(keep, keep_o)
        make_grads(io, info, lambda n: block_of(act, n, ff // 4), lambda n: cot[...], grad, send_a_o, send_b_o, keeps_o)
        io.finish()

    tok, wide, long = ((8, 64, width), BF16), ((rows, width), BF16), ((rows, ff), BF16)
    full = ((rows, width), F32)
    slab = ((3, rows, cols), BF16)
    return straight(
        body, "feed_forward", info, [gain, bias],
        [x_own, x_other, cot_own, cot_other, part, got, up_weight, down_weight],
        [full, wide, long, wide, wide, ((8, width), F32)] + grad_shapes(ff // 4, width) + [((8, 64, width), F32), tok],
        [tok, tok, tok, tok, wide, wide, ((3, width, cols), BF16), ((3, cols, width), BF16), full, wide, wide, long, slab,
         wide, full, ((8, width), F32), ((4, ff // 4, width), BF16), full, ((8, 64, width), F32), tok],
        16 + 2 + 6 + 3 + 3 + 5 + 2 + 4,
    )


def backward(
    info, d_sec, got, middle, cot, gain, mixer_out, mixed, gate_b, value, gate_a, wave, spec, zf, back, normed, gated_out
):
    rows, width = middle.shape
    half = width // 2

    def body(info, gain, d_sec, got, middle, cot, w_mo, mixed, gate_b, value, gate_a, wave, spec, zf, back,
             normed, gated_out, d_own_o, tf_o, d_proj_o, send_a_o, send_b_o, keeps_o,
             ds, gt, md, cs, wm, mx, gb, vl, ga, wv, sp, zs, bk, right, d_own, d_gb, d_mixed, prod, tf, left, grad, sem):
        c, length = info[0], info[1]
        io = Copies(sem)
        first = []
        for q in range(4):
            here = pl.ds(256 * q, 256)
            first.append([io.load(s.at[here], t.at[here]) for s, t in ((middle, md), (d_sec, ds), (got, gt), (cot, cs))])
        go_in = [io.load(part_of(w_mo, 0, c * half, half), wm), io.load(mixed, mx), io.load(gate_b, gb)]
        f_in = []
        for q in range(2):
            span = pl.ds(512 * q, 512)
            f_in.append([io.load(s.at[:, span], t.at[:, span]) for s, t in ((wave, wv), (spec, sp), (zf, zs))])
        b_in = [io.load(back.at[pl.ds(512 * q, 512)], bk.at[pl.ds(512 * q, 512)]) for q in range(2)]
        v_in = [io.load(value, vl), io.load(gate_a, ga)]
        g_in = [io.load(normed, right.at[0]), io.load(gated_out, left.at[:, pl.ds(3 * half, half)])]
        d_mid = right.at[1]
        for q, span in enumerate(CHUNKS):
            wait(*first[q])
            hat, inv = stats(md[span, :])
            t = (ds[span, :].astype(F32) + gt[span, :].astype(F32)) * gain[...]
            v = cs[span, :].astype(F32) + norm_back(t, hat, inv)
            d_mid[span, :] = v.astype(BF16)
            set_own(d_own, q, c, v)
        io.store(d_own, d_own_o)
        wait(*go_in)
        d_go = nt(d_mid[...], wm[...])
        d_gb[...] = (d_go * mx[...].astype(F32)).astype(BF16)
        d_mixed[...] = (d_go * gb[...].astype(F32)).astype(BF16)
        for q in range(2):
            span, low = slice(512 * q, 512 * q + 512), slice(rows + 512 * q, rows + 512 * q + 512)
            wait(*f_in[q])
            re = nn(wv[0, span], d_mixed[...])
            im = nn(wv[1, span], d_mixed[...])
            kr, ki = sp[0, span], sp[1, span]
            prod[span, :] = (kr * re + ki * im).astype(BF16)
            prod[low, :] = (kr * im - ki * re).astype(BF16)
            zr, zi = zs[0, span].astype(F32), zs[1, span].astype(F32)
            tf[0, span] = ((zr * re + zi * im) * (1.0 / rows)).astype(BF16)
            tf[1, span] = ((zr * im - zi * re) * (1.0 / rows)).astype(BF16)
        io.store(tf, tf_o)
        wait(*v_in)
        for q in range(2):
            span = slice(512 * q, 512 * q + 512)
            wait(b_in[q])
            m = nn(bk[span, :], prod[...])
            at_row = 512 * q + lax.broadcasted_iota(jnp.int32, m.shape, 0)
            m = jnp.where(at_row < length, m, 0.0)
            left[span, 0:half] = (m * ga[span, :].astype(F32)).astype(BF16)
            left[span, half : 2 * half] = (m * vl[span, :].astype(F32)).astype(BF16)
            left[span, 2 * half : 3 * half] = d_gb[span, :]
            here = pl.ds(512 * q, 512)
            io.store(left.at[here, pl.ds(0, 3 * half)], d_proj_o.at[here])
        wait(*g_in)
        make_grads(
            io, info, lambda n: block_of(left, n, half), lambda n: right[n // 3], grad, send_a_o, send_b_o, keeps_o
        )
        io.finish()

    wide, thin, full = ((rows, width), BF16), ((rows, half), BF16), ((rows, width), F32)
    own, freq, proj = ((8, 64, width), F32), ((2, rows, half), BF16), ((rows, 3 * half), BF16)
    return straight(
        body, "backward", info, [gain],
        [d_sec, got, middle, cot, mixer_out, mixed, gate_b, value, gate_a, wave, spec, zf, back, normed, gated_out],
        [own, freq, proj] + grad_shapes(half, width),
        [wide, wide, full, wide, ((half, width), BF16), thin, thin, thin, thin, (wave.shape, BF16), (spec.shape, F32),
         freq, (back.shape, BF16), ((2, rows, width), BF16), own, thin, thin, ((2 * rows, half), BF16), freq,
         ((rows, 4 * half), BF16), ((4, half, width), BF16)],
        16 + 3 + 6 + 2 + 2 + 2 + 4 + 4,
    )


def norm_in_back(info, d_proj, mixer_in, x_own, x_other):
    rows = d_proj.shape[0]
    width = mixer_in.shape[0]
    half = width // 2

    def body(info, d_proj, w_in, x_own, x_other, keep_o, give_o, sums_o,
             dp, w3, xo, xt, acc, keep, give, sums, sem):
        c = info[0]
        io = Copies(sem)
        got = []
        for n in range(3):
            got.append([io.load(d_proj.at[:, pl.ds(n * half, half)], dp.at[n]),
                        io.load(part_of(w_in, 1, n * width + c * half, half), w3.at[n])])
        x_in = [io.load(x_own, xo), io.load(x_other, xt)]
        for n in range(3):
            wait(*got[n])
            more = nt(dp[n], w3[n])
            if n == 0:
                acc[...] = more
            else:
                acc[...] += more
        wait(*x_in)
        gains, biases = 0.0, 0.0
        for q, span in enumerate(CHUNKS):
            dn = acc[span, :]
            hat, _ = stats(tokens(c, xo, xt, q))
            gains += jnp.sum(dn * hat, axis=0, keepdims=True)
            biases += jnp.sum(dn, axis=0, keepdims=True)
            set_own(keep, q, c, dn)
            set_own(give, q, c, dn, False)
        io.store(give, give_o)
        io.store(keep, keep_o)
        set_sums(sums, gains, biases)
        io.store(sums, sums_o)
        io.finish()

    tok = ((8, 64, width), BF16)
    own = ((8, 64, width), F32)
    return straight(
        body, "norm_in_back", info, [], [d_proj, mixer_in, x_own, x_other], [own, tok, ((8, width), F32)],
        [((3, rows, half), BF16), ((3, width, half), BF16), tok, tok, ((rows, width), F32), own, tok,
         ((8, width), F32)],
        11,
        vmem=28,
    )


def filter_back(info, tf, spread, f_out, slope2, slope1, turn, sides, back, norm_sums, second_sums):
    rows, half = tf.shape[1:]
    width = 2 * half

    def body(info, spread, f_out, slope2, slope1, turn, sides, norm_s, second_s, tf, back, out_o,
             tv, bk, out, sem):
        io = Copies(sem)
        t_in = [io.load(tf.at[n], tv.at[pl.ds(n * rows, rows)]) for n in range(2)]
        b_in = [io.load(back.at[pl.ds(512 * q, 512)], bk.at[pl.ds(512 * q, 512)]) for q in range(2)]
        wait(*t_in)
        g_fo = tn(spread[...], tv[...])[0:64] * float(rows)
        kf = nt(tv[...], f_out[...]).astype(BF16)
        wait(*b_in)
        d_s = slope2[...] * nn(bk[...], kf)
        high = lax.Precision.HIGHEST
        both = d_s + slope1[...] * jnp.dot(d_s, turn[...], precision=high, preferred_element_type=F32)
        g = tn(sides[...].astype(BF16), both.astype(BF16))
        lane = lax.broadcasted_iota(jnp.int32, (64, 128), 1)
        g = jnp.where(lane < 64, g[0:64], g[64:128])
        out[...] = jnp.zeros_like(out)
        out[0:32, 0:half] = g_fo[0:32].astype(BF16)
        out[0:32, half:] = g_fo[32:64].astype(BF16)
        for n in range(6):
            pair = [g[8 * n : 8 * n + 8]]
            if n < 2:
                pair.append(g[48 + 8 * n : 56 + 8 * n])
            elif n == 2:
                pair.append(jnp.broadcast_to(jnp.sum(both, axis=0, keepdims=True), (8, 128)))
            else:
                pair.append(jnp.zeros((8, 128), F32))
            out[32:48, 128 * n : 128 * n + 128] = jnp.concatenate(pair, axis=0).astype(BF16)
        out[48:64, :] = jnp.concatenate([norm_s[...], second_s[...]], axis=0).astype(BF16)
        io.store(out, out_o)
        io.finish()

    return straight(
        body, "filter_back", info, [spread, f_out, slope2, slope1, turn, sides, norm_sums, second_sums], [tf, back],
        [((64, width), BF16)],
        [((2 * rows, half), BF16), (back.shape, BF16), ((64, width), BF16)], 5, vmem=22,
    )[0]


def unpack_small(info, own, got):
    width = own.shape[1]
    half = width // 2

    def body(info, own, got, g_fo, g_fm, g_fi, b_m, b_f, norms, seconds):
        a, b = own[0:64, :].astype(F32), got[0:64, :].astype(F32)
        lo = jnp.where(info[0] == 0, a[0:32], b[0:32])
        hi = jnp.where(info[0] == 0, b[0:32], a[0:32])
        g_fo[0:32, 0:half], g_fo[32:64, 0:half] = lo[:, 0:half], lo[:, half:]
        g_fo[0:32, half:], g_fo[32:64, half:] = hi[:, 0:half], hi[:, half:]
        s = a[32:64] + b[32:64]
        tiles = [s[0:8, 128 * n : 128 * n + 128] for n in range(6)] + [s[8:16, 128 * n : 128 * n + 128] for n in range(3)]
        g = jnp.concatenate(tiles[:8], axis=0)
        g_fm[...] = g[:, 0:64]
        g_fi[...] = g[0:33, 64:128]
        b_m[...] = tiles[8][0:1, 0:64]
        b_f[...] = tiles[8][0:1, 64:128]
        norms[...] = s[16:24]
        seconds[...] = s[24:32]

    shapes = [(64, width), (64, 64), (33, 64), (1, 64), (1, 64), (8, width), (8, width)]
    return CHAIN(
        body,
        1,
        in_specs=[pl.BlockSpec(memory_space=pltpu.SMEM)] + [pl.BlockSpec(memory_space=pltpu.VMEM)] * 2,
        out_specs=[pl.BlockSpec(memory_space=pltpu.VMEM)] * len(shapes),
        out_shape=[jax.ShapeDtypeStruct(s, F32) for s in shapes],
        compiler_params=pltpu.CompilerParams(vmem_limit_bytes=16 * 2**20),
        name="unpack_small",
    )(info, own, got)


def finish_output(out_keep, out_got):
    def body(out_keep, out_got, out):
        out[...] = (out_keep[...] + out_got[...].astype(F32)).astype(BF16)

    return CHAIN(
        body,
        0,
        in_specs=[pl.BlockSpec(memory_space=pltpu.VMEM)] * 2,
        out_specs=pl.BlockSpec(memory_space=pltpu.VMEM),
        out_shape=jax.ShapeDtypeStruct(out_keep.shape, BF16),
        compiler_params=pltpu.CompilerParams(vmem_limit_bytes=16 * 2**20),
        name="finish_output",
    )(out_keep, out_got)


def finish_inputs(gain, d_norm_keep, d_norm_got, d_mid_own, x_half):
    def body(gain, d_norm_keep, d_norm_got, d_mid_own, x_half, out):
        for p in range(x_half.shape[0]):
            hat, inv = stats(x_half[p].astype(F32))
            q = (d_norm_keep[p] + d_norm_got[p].astype(F32)) * gain[...]
            out[p] = (d_mid_own[p] + norm_back(q, hat, inv)).astype(BF16)

    return CHAIN(
        body,
        0,
        in_specs=[pl.BlockSpec(memory_space=pltpu.VMEM)] * 5,
        out_specs=pl.BlockSpec(memory_space=pltpu.VMEM),
        out_shape=jax.ShapeDtypeStruct(x_half.shape, BF16),
        compiler_params=pltpu.CompilerParams(vmem_limit_bytes=24 * 2**20),
        name="finish_inputs",
    )(gain, d_norm_keep, d_norm_got, d_mid_own, x_half)


def split_back(info, got):
    _, n, width = got.shape

    def body(info, got, keep, give):
        keep[...] = got[pl.ds(4 * info[0], 4)]
        give[...] = got[pl.ds(4 - 4 * info[0], 4)]

    return small(body, "split_back", [((4, n, width), BF16)] * 2, info, got)


def join_back(info, keep, got, dtype):
    _, n, width = keep.shape

    def body(info, keep, got, out):
        a, b = keep[...].astype(F32), got[...].astype(F32)
        out[:, 0:n, :] = jnp.where(info[0] == 0, a, b).astype(dtype)
        out[:, n:, :] = jnp.where(info[0] == 0, b, a).astype(dtype)

    return small(body, "join_back", [((4, 2 * n, width), dtype)], info, keep, got)[0]


def small(body, name, outs, *ins):
    return CHAIN(
        body,
        1,
        in_specs=[pl.BlockSpec(memory_space=pltpu.SMEM)] + [pl.BlockSpec(memory_space=pltpu.VMEM)] * (len(ins) - 1),
        out_specs=[pl.BlockSpec(memory_space=pltpu.VMEM)] * len(outs),
        out_shape=[jax.ShapeDtypeStruct(s, t) for s, t in outs],
        compiler_params=pltpu.CompilerParams(vmem_limit_bytes=16 * 2**20),
        name=name,
    )(*ins)


def plus(a, b):
    return (a.astype(F32) + b.astype(F32)).astype(BF16)


class Reducer:
    def __init__(self, pos, send_a, send_b, keeps):
        self.pos, self.keeps = pos, keeps
        self.rows, self.cols = send_a.shape
        self.got = (send(send_a, PX), send(send_b, PY))

    def step2(self):
        n = self.rows // 2

        def body(pos, keeps, got_a, got_b, out_a, out_b, keep):
            for k, (got, out) in enumerate(((got_a, out_a), (got_b, out_b))):
                p = pos[1 - k]
                mine, others = at(p, n), at(1 - p, n)
                out[...] = plus(keeps[k, others, :], got[others, :])
                keep[k] = plus(keeps[k, mine, :], got[mine, :])

        a, b, self.keeps = small(
            body, "step2", [((n, self.cols), BF16)] * 2 + [((2, n, self.cols), BF16)], self.pos, self.keeps, *self.got
        )
        self.got = (send(a, PY), send(b, PX))

    def step3(self):
        n = self.rows // 4

        def body(pos, keeps, got_a, got_b, out, keep):
            mine, others = at(pos[2], n, 32), at(1 - pos[2], n, 32)
            for k, got in enumerate((got_a, got_b)):
                out[k] = plus(keeps[k, others, :], got[others, :])
                keep[k] = plus(keeps[k, mine, :], got[mine, :])

        shape = (2, n, self.cols)
        out, self.keeps = small(body, "step3", [(shape, BF16), (shape, BF16)], self.pos, self.keeps, *self.got)
        self.got = (send(out, PZ[1]),)

    def step4(self, extra=None):
        n = self.rows // 2
        self.extra = 0 if extra is None else extra.shape[0]

        def body(pos, keeps, got, *refs):
            out = refs[-1]
            for k in range(2):
                out[k * n // 2 : (k + 1) * n // 2, :] = plus(keeps[k], got[k])
            if extra is not None:
                out[n:, :] = refs[0][...]

        ins = [self.keeps, *self.got] + ([] if extra is None else [extra])
        (self.total,) = small(body, "step4", [((n + self.extra, self.cols), BF16)], self.pos, *ins)
        self.got = (send(self.total, PZ[2]),)

    def step5(self):
        def body(pos, total, got, out):
            out[...] = plus(total[...], got[...])

        (self.total,) = small(body, "step5", [(self.total.shape, BF16)], self.pos, self.total, *self.got)
        self.got = (send(self.total, PZ[1]),)

    def step6(self):
        n, more = self.rows // 4, self.extra

        def body(pos, total, got, out_a, out_b):
            mine, others = at(pos[2], n, 32), at(1 - pos[2], n, 32)
            for k, out in enumerate((out_a, out_b)):
                out[mine, :] = total[k * n : (k + 1) * n, :]
                out[others, :] = got[k * n : (k + 1) * n, :]
            if more:
                out_a[2 * n :, :] = plus(total[2 * n :, :], got[2 * n :, :])

        shapes = [((2 * n + more, self.cols), BF16), ((2 * n, self.cols), BF16)]
        self.own = small(body, "step6", shapes, self.pos, self.total, *self.got)
        self.got = (send(self.own[0], PY), send(self.own[1], PX))

    def step7(self):
        n, more = self.rows // 2, self.extra

        def body(pos, own_a, own_b, got_a, got_b, out_a, out_b):
            for k, (own, got, out) in enumerate(((own_a, got_a, out_a), (own_b, got_b, out_b))):
                p = pos[1 - k]
                out[at(p, n), :] = own[0:n, :]
                out[at(1 - p, n), :] = got[0:n, :]
            if more:
                out_a[2 * n :, :] = plus(own_a[n:, :], got_a[n:, :])

        shapes = [((2 * n + more, self.cols), BF16), ((2 * n, self.cols), BF16)]
        self.near = small(body, "step7", shapes, self.pos, *self.own, *self.got)
        self.got = (send(self.near[0], PX), send(self.near[1], PY))
        self.pair_near = [send(v, PC) for v in self.near]

    def step8(self):
        n, more = self.rows, self.extra

        def body(pos, near, far_a, far_b, out_a, out_b, *sums):
            out_a[...] = far_a[0:n, :]
            out_b[...] = far_b[...]
            if more:
                sums[0][...] = plus(near[n:, :], far_a[n:, :])

        shapes = [((n, self.cols), BF16)] * 2 + ([((more, self.cols), BF16)] if more else [])
        *self.far, = small(body, "step8", shapes, self.pos, self.near[0], *self.got)
        if more:
            self.sum = self.far.pop()
        self.pair_far = [send(v, PC) for v in self.far]


def write(bufs, sources, spots, moves):
    n, m = len(sources), len(bufs)
    rows, cols = sources[1].shape
    turned = any(t for _, _, _, _, t in moves([0, 0, 0]))
    straight_ones = any(not t for _, _, _, _, t in moves([0, 0, 0]))

    def body(*refs):
        spot = refs[0]
        src, out = refs[1 : 1 + n], refs[1 + n + m : 1 + n + 2 * m]
        mark, wide, tall, sem = refs[1 + n + 2 * m :]
        mark[...] = jnp.zeros_like(mark)

        def each(act):
            for k in range(n):
                for when, b, i, j, t in moves([spot[k, e] for e in range(3)]):
                    size = (cols, rows) if t else (rows, cols)
                    src_ref = tall.at[k] if t else wide.at[k]
                    copy = pltpu.make_async_copy(
                        src_ref,
                        out[b].at[pl.ds(pl.multiple_of(i, 128), size[0]), pl.ds(pl.multiple_of(j, 128), size[1])],
                        sem.at[k],
                    )
                    act(k, when, t, copy)

        def begin(k, when, t, copy):
            @pl.when(when)
            def _():
                if t:
                    tall[k] = src[k][0:rows, :].astype(F32).T
                else:
                    wide[k] = src[k][0:rows, :].astype(F32)
                copy.start()

        def finish(k, when, t, copy):
            @pl.when(when)
            def _():
                copy.wait()

        each(begin)
        each(finish)

    return CHAIN(
        body,
        1,
        in_specs=[pl.BlockSpec(memory_space=pltpu.SMEM)] + [pl.BlockSpec(memory_space=pltpu.VMEM)] * n + [ANY] * m,
        out_specs=[ANY] * m + [pl.BlockSpec(memory_space=pltpu.VMEM)],
        out_shape=[jax.ShapeDtypeStruct(b.shape, F32) for b in bufs] + [jax.ShapeDtypeStruct((8, 128), F32)],
        input_output_aliases={1 + n + b: b for b in range(m)},
        scratch_shapes=[
            pltpu.VMEM((n, rows, cols) if straight_ones else (n, 8, 128), F32),
            pltpu.VMEM((n, cols, rows) if turned else (n, 8, 128), F32),
            pltpu.SemaphoreType.DMA((n,)),
        ],
        compiler_params=pltpu.CompilerParams(vmem_limit_bytes=20 * 2**20),
        name="write",
    )(spots, *sources, *bufs)[:-1]


def fresh(*shapes):
    def body(*refs):
        pass

    return pl.pallas_call(
        body, out_specs=[ANY] * len(shapes), out_shape=[jax.ShapeDtypeStruct(s, F32) for s in shapes], name="fresh"
    )()


def write_down(s):
    return [(s[0] >= 0, 0, s[0] * 1536 + s[1] * 768 + s[2] * 384, 0, False)]


def write_up(s):
    return [(s[0] >= 0, 0, 0, s[0] * 1536 + s[1] * 768 + s[2] * 384, True)]


def write_mix(s):
    n = s[1] * 2 + s[2]
    return [(n < 3, 0, 0, n * 768 + s[0] * 384, True), (n == 3, 1, s[0] * 384, 0, False)]


def chip_local(
    inputs, lengths, norm_gain, norm_bias, mixer_in, filter_in, filter_in_bias, filter_mid, filter_mid_bias,
    filter_out, mixer_out, second_gain, second_bias, up_weight, down_weight, cotangent,
):
    CHAIN.last = None
    s = lax.axis_index("seq")
    d = lax.axis_index("dp")
    z, x, y, c = s // 2, s % 2, d // 2, d % 2
    width = inputs.shape[-1]
    rows = 8 * inputs.shape[1]
    half = width // 2
    x_swapped = swap_in(inputs, c)
    filter_in, filter_out, filter_mid, cotangent, lengths, norm_gain, norm_bias, second_gain, second_bias, x_swapped = tie(
        filter_in, filter_out, filter_mid, cotangent, lengths, norm_gain, norm_bias, second_gain, second_bias, x_swapped
    )
    x_half = exchange_seq(x_swapped)
    cot_half = swap_in(cotangent, c)
    other_len = send(lengths, PC)
    length = pick(jnp.where(c == (z >> 1), lengths, other_len), (z & 1) * 2 + x)
    tab = [1 - x, 3 - y, x, 2 + y]
    info = jnp.stack([c, length, *tab])
    zero = 0 * c
    pos = jnp.stack([x, y, z & 1, z >> 1])
    near = jnp.stack([jnp.stack(v) for v in ((c, zero, x), (c, zero + 1, y), (1 - c, zero, x), (1 - c, zero + 1, y))])
    far = jnp.stack(
        [jnp.stack(v) for v in ((c, zero, 1 - x), (c, zero + 1, 1 - y), (1 - c, zero, 1 - x), (1 - c, zero + 1, 1 - y))]
    )
    norm_gain, norm_bias = norm_gain[None], norm_bias[None]
    second_gain, second_bias = second_gain[None], second_bias[None]
    f_out = lanes(filter_out, c * half, half)
    waves = dft_table(rows)
    table = jnp.asarray(waves, BF16)
    wave = table.reshape(2, rows, rows)
    back = jnp.asarray(waves.T, BF16)
    feats = jnp.asarray(feature_table(rows))
    first_act = jnp.dot(feats, filter_in, precision=HIGH) + filter_in_bias
    h1 = jnp.sin(first_act)
    second_act = jnp.dot(h1, filter_mid, precision=HIGH) + filter_mid_bias
    h2 = jnp.sin(second_act)
    h2_hi = h2.astype(BF16)
    h2_lo = (h2 - h2_hi.astype(F32)).astype(BF16)
    hf = mm(table, jnp.concatenate([h2_hi, h2_lo], axis=1))
    hf = (hf[:, :64] + hf[:, 64:]) * (1.0 / rows)
    spec = jnp.dot(hf, f_out, precision=lax.Precision.HIGH).reshape(2, rows, half)
    spread = jnp.pad(hf, ((0, 0), (0, 64))).astype(BF16)
    f_low = jnp.pad(f_out, ((0, 64), (0, 0))).astype(BF16)
    slope2 = jnp.pad(jnp.cos(second_act), ((0, 0), (0, 64)))
    slope1 = jnp.pad(jnp.cos(first_act), ((0, 0), (64, 0)))
    turn = jnp.pad(filter_mid.T, ((0, 64), (64, 0)))
    sides = jnp.concatenate([h1, jnp.pad(feats, ((0, 0), (0, 31)))], axis=1)
    x_half, spec, cot_half, info, norm_gain, norm_bias, second_gain, second_bias = tie(
        x_half, spec, cot_half, info, norm_gain, norm_bias, second_gain, second_bias
    )
    cot_half = exchange_seq(cot_half)
    x_pair = send(x_half, PC)
    normed, value, gate_a, gate_b, zf, mixed, gated_out, part = front(
        info, x_half, x_pair, norm_gain, norm_bias, mixer_in, wave, spec, back, mixer_out
    )
    cot_pair = send(cot_half, PC)
    part_pair, spread, f_low, slope2, slope1, turn, sides = tie(
        send(part, PC), spread, f_low, slope2, slope1, turn, sides
    )
    middle, second_normed, d_pre, cot, d_second, second_sums, *more = feed_forward(
        info, x_half, x_pair, cot_half, cot_pair, part, part_pair, second_gain, second_bias, up_weight, down_weight
    )
    out_keep, out_give = more[3:]
    d_second_pair = send(d_second, PC)
    out_got = send(out_give, PC)
    down = Reducer(pos, *more[:3])
    up = Reducer(pos, *up_grads(info, d_pre, second_normed))
    out_back = exchange_seq(finish_output(out_keep, out_got))
    d_mid_own, tf, d_proj, *g_mix = backward(
        info, d_second, d_second_pair, middle, cot, second_gain, mixer_out, mixed, gate_b, value, gate_a, wave,
        spec, zf, back, normed, gated_out,
    )
    mix = Reducer(pos, *g_mix)
    down.step2()
    d_norm_keep, d_norm_give, norm_sums = norm_in_back(info, d_proj, mixer_in, x_half, x_pair)
    d_norm_got = send(d_norm_give, PC)
    up.step2()
    down.step3()
    mix.step2()
    up.step3()
    down.step4()
    tiny = filter_back(
        info, tf, spread, f_low, slope2, slope1, turn, sides, back, norm_sums, second_sums
    )
    mix.step3()
    up.step4(tiny)
    out_keep, out_give = split_back(info, out_back)
    out_got = send(out_give, PC)
    down.step5()
    mix.step4()
    up.step5()
    dx_back = exchange_seq(finish_inputs(norm_gain, d_norm_keep, d_norm_got, d_mid_own, x_half))
    down.step6()
    mix.step5()
    output = join_back(info, out_keep, out_got, BF16)
    down.step7()
    up.step6()
    mix.step6()
    bufs = fresh(down_weight.shape, up_weight.shape, mixer_in.shape, mixer_out.shape)
    down.step8()
    grad_down = write(bufs[:1], [*down.near, *down.pair_near], near, write_down)
    up.step7()
    mix.step7()
    (grad_down,) = write(grad_down, [*down.far, *down.pair_far], far, write_down)
    grad_up = write(bufs[1:2], [*up.near, *up.pair_near], near, write_up)
    grads_two = write(bufs[2:], [*mix.near, *mix.pair_near], near, write_mix)
    dx_keep, dx_give = split_back(info, dx_back)
    dx_got = send(dx_give, PC)
    up.step8()
    tiny_got = send(up.sum, PC)
    grad_inputs = join_back(info, dx_keep, dx_got, F32)
    g_fo, g_fm, g_fi, b_m, b_f, norms, seconds = unpack_small(info, up.sum, tiny_got)
    mix.step8()
    (grad_up,) = write(grad_up, [*up.far, *up.pair_far], far, write_up)
    grad_in, grad_mo = write(grads_two, [*mix.far, *mix.pair_far], far, write_mix)
    return (
        output, grad_inputs, norms[0], norms[1], grad_in, g_fi, b_f[0], g_fm, b_m[0],
        g_fo, grad_mo, seconds[0], seconds[1], grad_up, grad_down,
    )


LAGS = 16


def shifted(value, axis, by):
    devices = lax.axis_size(axis)
    pairs = [(i, i + by) for i in range(devices) if 0 <= i + by < devices]
    return lax.ppermute(value, axis, pairs)


def plain_norm(values, gain, shift):
    center = values - jnp.mean(values, axis=-1, keepdims=True)
    spread = jnp.mean(center * center, axis=-1, keepdims=True)
    return center * lax.rsqrt(spread + EPSILON) * gain + shift


def features_of(taps, bands):
    steps = jnp.arange(taps, dtype=jnp.float32) / taps
    freqs = jnp.arange(1, bands + 1, dtype=jnp.float32)
    phase = 2.0 * math.pi * steps[:, None] * freqs[None, :]
    return jnp.concatenate([steps[:, None], jnp.cos(phase), jnp.sin(phase)], axis=1)


def taps_of(filter_in, filter_in_bias, filter_mid, filter_mid_bias, filter_out):
    table = features_of(KL, BANDS)
    first = jnp.sin(jnp.dot(table, filter_in, precision=HIGH) + filter_in_bias)
    second = jnp.sin(jnp.dot(first, filter_mid, precision=HIGH) + filter_mid_bias)
    return jnp.dot(second, filter_out, precision=HIGH)


def wave_tables(block_len):
    length = 2 * block_len
    index = jnp.arange(length, dtype=jnp.int32)
    angle = (index[:, None] * index[None, :] % length).astype(jnp.float32) * (
        2.0 * math.pi / length
    )
    return (jnp.cos(angle), jnp.sin(angle))


def split_table(table):
    leading = table.astype(jnp.bfloat16)
    remainder = (table - leading.astype(jnp.float32)).astype(jnp.bfloat16)
    return (leading, remainder)


def low_tables(cos_t, sin_t):
    length = cos_t.shape[0]
    half = length // 2
    return (
        split_table(cos_t[:, :half]),
        split_table(sin_t[:, :half]),
        split_table(cos_t[half:] / length),
        split_table(sin_t[half:] / length),
    )


def apply_split(pattern, halves, values):
    first = jnp.einsum(pattern, halves[0], values, preferred_element_type=jnp.float32)
    second = jnp.einsum(pattern, halves[1], values, preferred_element_type=jnp.float32)
    return first + second


def kernel_freq(kernel, cos_t, sin_t):
    block_len = cos_t.shape[0] // 2
    width = kernel.shape[1]
    count = kernel.shape[0] // block_len
    padded = jnp.concatenate(
        [
            jnp.zeros((block_len, width), jnp.float32),
            kernel,
            jnp.zeros((2 * block_len, width), jnp.float32),
        ],
        axis=0,
    )
    pieces = padded.reshape(count + 3, block_len, width)
    segments = jnp.concatenate([pieces[: count + 1], pieces[1 : count + 2]], axis=1)
    real = jnp.einsum("fn,mnd->mfd", cos_t, segments, precision=HIGH)
    imag = -jnp.einsum("fn,mnd->mfd", sin_t, segments, precision=HIGH)
    return (real, imag)


def to_freq(values, tables):
    real = apply_split("fc,scd->sfd", tables[0], values)
    imag = -apply_split("fc,scd->sfd", tables[1], values)
    return (real, imag)


def from_freq(real, imag, cos_t, sin_t):
    length = cos_t.shape[0]
    half = length // 2
    first = jnp.einsum("nf,sfd->snd", cos_t[half:], real, precision=HIGH)
    second = jnp.einsum("nf,sfd->snd", sin_t[half:], imag, precision=HIGH)
    return (first - second) / length


def grad_freq(values, tables):
    real = apply_split("nf,snd->sfd", tables[2], values)
    imag = -apply_split("nf,snd->sfd", tables[3], values)
    return (real, imag)


def grad_time(real, imag, cos_t, sin_t):
    half = cos_t.shape[0] // 2
    first = jnp.einsum("fc,sfd->scd", cos_t[:, :half], real, precision=HIGH)
    second = jnp.einsum("fc,sfd->scd", sin_t[:, :half], imag, precision=HIGH)
    return first - second


def add_forward(acc, k_real, k_imag, values, tables):
    z_real, z_imag = to_freq(values, tables)
    return (acc[0] + k_real * z_real - k_imag * z_imag, acc[1] + k_real * z_imag + k_imag * z_real)


def add_backward(acc, k_real, k_imag, grads, own_real, own_imag, tables):
    d_real, d_imag = grad_freq(grads, tables)
    new_real = acc[0] + k_real * d_real + k_imag * d_imag
    new_imag = acc[1] - k_imag * d_real + k_real * d_imag
    term_real = jnp.sum(own_real * d_real + own_imag * d_imag, axis=0)
    term_imag = jnp.sum(own_real * d_imag - own_imag * d_real, axis=0)
    return ((new_real, new_imag), (term_real, term_imag))


def forward_stack(stack, k_real, k_imag, acc, tables):

    def forward_step(carry, item):
        return (add_forward(carry, item[1], item[2], item[0], tables), None)

    result, _ = lax.scan(forward_step, acc, (stack, k_real, k_imag))
    return result


def backward_stack(stack, k_real, k_imag, acc, own_real, own_imag, tables):

    def backward_step(carry, item):
        return add_backward(carry, item[1], item[2], item[0], own_real, own_imag, tables)

    return lax.scan(backward_step, acc, (stack, k_real, k_imag))


def sum_everywhere(parts):
    flat_grads = jnp.concatenate([piece.reshape(-1) for piece in parts])
    portion = lax.psum_scatter(flat_grads, ("seq", "dp"), scatter_dimension=0, tiled=True)
    summed = lax.all_gather(portion.astype(jnp.bfloat16), ("seq", "dp"), axis=0, tiled=True).astype(
        portion.dtype
    )
    results = []
    offset = 0
    for piece in parts:
        results.append(summed[offset : offset + piece.size].reshape(piece.shape))
        offset = offset + piece.size
    return results


def block_local(
    inputs,
    lengths,
    norm_gain,
    norm_bias,
    mixer_in,
    filter_in,
    filter_in_bias,
    filter_mid,
    filter_mid_bias,
    filter_out,
    mixer_out,
    second_gain,
    second_bias,
    up_weight,
    down_weight,
    cotangent,
):
    seqs, block_len, width = inputs.shape
    row_count = seqs * block_len
    reach = min(LAGS, lax.axis_size("seq") - 1)
    rank = lax.axis_index("seq")
    position = rank * block_len + jnp.arange(block_len, dtype=jnp.int32)
    valid = (position[None, :] < lengths[:, None]).astype(jnp.float32)[:, :, None]
    cos_t, sin_t = wave_tables(block_len)
    tables = low_tables(cos_t, sin_t)
    kernel, filter_back = jax.vjp(
        taps_of, filter_in, filter_in_bias, filter_mid, filter_mid_bias, filter_out
    )
    k_real, k_imag = kernel_freq(kernel, cos_t, sin_t)
    x_full = inputs.astype(jnp.float32).reshape(row_count, width)
    normed = plain_norm(x_full, norm_gain, norm_bias).astype(jnp.bfloat16)
    projected = jnp.dot(normed, mixer_in, preferred_element_type=jnp.float32)
    value = projected[:, :width]
    gate_a = projected[:, width : 2 * width]
    gate_b = projected[:, 2 * width :]
    gated = (value * gate_a).astype(jnp.bfloat16).reshape(seqs, block_len, width) * valid.astype(
        jnp.bfloat16
    )
    own_real, own_imag = to_freq(gated, tables)
    initial = (
        k_real[0] * own_real - k_imag[0] * own_imag,
        k_real[0] * own_imag + k_imag[0] * own_real,
    )
    earlier = []
    for lag in range(1, reach + 1):
        earlier.append(shifted(gated, "seq", lag))
    y_real, y_imag = forward_stack(
        jnp.stack(earlier), k_real[1 : reach + 1], k_imag[1 : reach + 1], initial, tables
    )
    mixed = from_freq(y_real, y_imag, cos_t, sin_t).reshape(row_count, width)
    gated_out = (gate_b * mixed).astype(jnp.bfloat16)
    middle = x_full + jnp.dot(gated_out, mixer_out, preferred_element_type=jnp.float32)
    second_normed = plain_norm(middle, second_gain, second_bias).astype(jnp.bfloat16)
    pre = jnp.dot(second_normed, up_weight, preferred_element_type=jnp.float32)
    activated = jax.nn.gelu(pre, approximate=True).astype(jnp.bfloat16)
    result = middle + jnp.dot(activated, down_weight, preferred_element_type=jnp.float32)
    output = result.astype(jnp.bfloat16).reshape(seqs, block_len, width)
    upstream_low = cotangent.reshape(row_count, width)
    upstream = upstream_low.astype(jnp.float32)
    grad_down = jnp.einsum("rk,rd->kd", activated, upstream_low, preferred_element_type=jnp.float32)
    d_act = jnp.einsum("rd,kd->rk", upstream_low, down_weight, preferred_element_type=jnp.float32)
    _, gelu_back = jax.vjp(lambda arg: jax.nn.gelu(arg, approximate=True), pre)
    d_pre = gelu_back(d_act)[0].astype(jnp.bfloat16)
    grad_up = jnp.einsum("rd,rk->dk", second_normed, d_pre, preferred_element_type=jnp.float32)
    d_second = jnp.einsum("rk,dk->rd", d_pre, up_weight, preferred_element_type=jnp.float32)
    _, second_back = jax.vjp(plain_norm, middle, second_gain, second_bias)
    d_middle_norm, grad_second_gain, grad_second_bias = second_back(d_second)
    d_middle = upstream + d_middle_norm
    d_middle_low = d_middle.astype(jnp.bfloat16)
    grad_mixer_out = jnp.einsum(
        "rk,rd->kd", gated_out, d_middle_low, preferred_element_type=jnp.float32
    )
    d_gated_out = jnp.einsum(
        "rd,kd->rk", d_middle_low, mixer_out, preferred_element_type=jnp.float32
    )
    d_gate_b = d_gated_out * mixed
    d_mixed = (d_gated_out * gate_b).astype(jnp.bfloat16).reshape(seqs, block_len, width)
    empty_freq = jnp.zeros((seqs, 2 * block_len, width), jnp.float32)
    start_acc, own_terms = add_backward(
        (empty_freq, empty_freq), k_real[0], k_imag[0], d_mixed, own_real, own_imag, tables
    )
    unused = jnp.zeros((LAGS - reach, 2 * block_len, width), jnp.float32)
    later = []
    for lead in range(1, reach + 1):
        later.append(shifted(d_mixed, "seq", -lead))
    (z_real, z_imag), terms = backward_stack(
        jnp.stack(later),
        k_real[1 : reach + 1],
        k_imag[1 : reach + 1],
        start_acc,
        own_real,
        own_imag,
        tables,
    )
    dk_real = jnp.concatenate([own_terms[0][None], terms[0], unused], axis=0)
    dk_imag = jnp.concatenate([own_terms[1][None], terms[1], unused], axis=0)
    d_gated = (grad_time(z_real, z_imag, cos_t, sin_t) * valid).reshape(row_count, width)
    d_projected = jnp.concatenate([d_gated * gate_a, d_gated * value, d_gate_b], axis=1).astype(
        jnp.bfloat16
    )
    grad_mixer_in = jnp.einsum("rd,rk->dk", normed, d_projected, preferred_element_type=jnp.float32)
    d_normed = jnp.einsum("rk,dk->rd", d_projected, mixer_in, preferred_element_type=jnp.float32)
    _, first_back = jax.vjp(plain_norm, x_full, norm_gain, norm_bias)
    d_x_norm, grad_norm_gain, grad_norm_bias = first_back(d_normed)
    grad_inputs = (d_middle + d_x_norm).reshape(seqs, block_len, width)
    _, kernel_back = jax.vjp(lambda kern: kernel_freq(kern, cos_t, sin_t), kernel)
    d_kernel = kernel_back((dk_real, dk_imag))[0]
    dense = [
        grad_norm_gain,
        grad_norm_bias,
        grad_mixer_in,
        grad_mixer_out,
        grad_second_gain,
        grad_second_bias,
        grad_up,
        grad_down,
    ]
    summed = sum_everywhere([d_kernel] + dense)
    filter_grads = filter_back(summed[0])
    dense_sums = summed[1:]
    return (
        output,
        grad_inputs,
        dense_sums[0],
        dense_sums[1],
        dense_sums[2],
        filter_grads[0],
        filter_grads[1],
        filter_grads[2],
        filter_grads[3],
        filter_grads[4],
        dense_sums[3],
        dense_sums[4],
        dense_sums[5],
        dense_sums[6],
        dense_sums[7],
    )


SPECS_IN = (P("dp", "seq", None), P("dp")) + (P(),) * 13 + (P("dp", "seq", None),)
SPECS_OUT = (P("dp", "seq", None), P("dp", "seq", None)) + (P(),) * 13


def solution(mesh):
    local = chip_local if (mesh.shape["seq"], mesh.shape["dp"]) == (8, 4) else block_local
    return jax.shard_map(local, mesh=mesh, in_specs=SPECS_IN, out_specs=SPECS_OUT, check_vma=False)
```

```python
import math

import jax
import jax.numpy as jnp
import numpy as np
from jax import lax
from jax.experimental import pallas as pl
from jax.experimental.pallas import tpu as pltpu
from jax.sharding import PartitionSpec as P

AX = ("seq", "dp")
HIGH = lax.Precision.HIGHEST
EPSILON = 1e-05
BANDS = 16
KL = 2048
F32 = jnp.float32
BF16 = jnp.bfloat16


def mm(a, b, ca=1, cb=0):
    return lax.dot_general(a, b, (((ca,), (cb,)), ((), ())), preferred_element_type=F32)


def perm_of(f):
    pairs = []
    for z in range(4):
        for x in range(2):
            for y in range(2):
                for c in range(2):
                    a, b, d, e = f(z, x, y, c)
                    pairs.append(((z * 2 + x) * 4 + y * 2 + c, (a * 2 + b) * 4 + d * 2 + e))
    return pairs


PC = perm_of(lambda z, x, y, c: (z, x, y, 1 - c))
PX = perm_of(lambda z, x, y, c: (z, 1 - x, y, c))
PY = perm_of(lambda z, x, y, c: (z, x, 1 - y, c))
PZ = [perm_of(lambda z, x, y, c, k=k: (z ^ k, x, y, c)) for k in range(4)]


def send(v, perm):
    return lax.ppermute(v, AX, perm)


def tie(*vals):
    return lax.optimization_barrier(tuple(vals))


def swap_in(v, c):
    v = v.reshape(4, 2, 64, v.shape[-1])
    keep = pick(v, c, 1)
    got = send(pick(v, 1 - c, 1), PC)
    return jnp.where(c == 0, jnp.concatenate([keep, got]), jnp.concatenate([got, keep]))


def exchange_seq(v):
    return lax.all_to_all(v, "seq", 0, 0)


def swap_out(v, c):
    v = v.reshape(2, 4, 64, v.shape[-1])
    keep = pick(v, c)
    got = send(pick(v, 1 - c), PC)
    m = jnp.stack([jnp.where(c == 0, keep, got), jnp.where(c == 0, got, keep)], axis=1)
    return m.reshape(4, 128, v.shape[-1])


def both(own, c):
    other = send(own, PC)
    return jnp.stack([jnp.where(c == 0, own, other), jnp.where(c == 0, other, own)], axis=1)


def feature_table(taps):
    steps = np.arange(taps, dtype=np.float64) / KL
    freqs = np.arange(1, BANDS + 1, dtype=np.float64)
    phase = 2.0 * math.pi * steps[:, None] * freqs[None, :]
    return np.concatenate([steps[:, None], np.cos(phase), np.sin(phase)], axis=1).astype(np.float32)


def dft_table(length):
    f = 2 * np.arange(length, dtype=np.int64)[:, None] + 1
    n = np.arange(length, dtype=np.int64)[None, :]
    angle = (f * n % (4 * length)) * (2.0 * math.pi / (4 * length))
    return np.concatenate([np.cos(angle), -np.sin(angle)], axis=0).astype(np.float32)


def norm_parts(v):
    center = v - jnp.mean(v, axis=-1, keepdims=True)
    spread_ = jnp.mean(center * center, axis=-1, keepdims=True)
    inv = lax.rsqrt(spread_ + EPSILON)
    return center * inv, inv


def norm_back(q, hat, inv):
    return (q - jnp.mean(q, -1, keepdims=True) - hat * jnp.mean(q * hat, -1, keepdims=True)) * inv


def lanes(a, at, size):
    return lax.dynamic_slice_in_dim(a, at, size, axis=1)


def in_order(bit, own, other, axis=0):
    first = jnp.where(bit == 0, own, other)
    second = jnp.where(bit == 0, other, own)
    return jnp.concatenate([first, second], axis=axis)


def pick(a, i, axis=0):
    return lax.dynamic_index_in_dim(a, i, axis, keepdims=False)


GELU_A = math.sqrt(2.0 / math.pi)
GELU_B = 0.044715


def gelu_pair(v):
    sq = v * v
    t = jnp.tanh(GELU_A * v * (1.0 + GELU_B * sq))
    up = 0.5 * (1.0 + t)
    return v * up, up + 0.5 * v * (1.0 - t * t) * (GELU_A * (1.0 + 3.0 * GELU_B * sq))


def nn(a, b):
    return jnp.dot(a, b, preferred_element_type=F32)


def nt(a, b):
    return lax.dot_general(a, b, (((1,), (1,)), ((), ())), preferred_element_type=F32)


def tn(a, b):
    return lax.dot_general(a, b, (((0,), (0,)), ((), ())), preferred_element_type=F32)


def stats(v):
    center = v - jnp.mean(v, axis=-1, keepdims=True)
    inv = lax.rsqrt(jnp.mean(center * center, axis=-1, keepdims=True) + EPSILON)
    return center * inv, inv


def loop(n, body):
    def step(i, carry):
        body(i)
        return carry

    lax.fori_loop(0, n, step, 0)


def at(i, size, least=64):
    return pl.ds(pl.multiple_of(i * size, least), size)


CHUNKS = tuple(slice(256 * q, 256 * (q + 1)) for q in range(4))


def tokens(c, own, other, q):
    parts = []
    for p in (2 * q, 2 * q + 1):
        a, b = own[p].astype(F32), other[p].astype(F32)
        parts += [jnp.where(c == 0, a, b), jnp.where(c == 0, b, a)]
    return jnp.concatenate(parts, axis=0)


def set_own(ref, q, c, tile, mine=True):
    for n in range(2):
        first, second = tile[128 * n : 128 * n + 64], tile[128 * n + 64 : 128 * n + 128]
        ref[2 * q + n] = jnp.where((c == 0) == mine, first, second).astype(ref.dtype)


ANY = pl.BlockSpec(memory_space=pl.ANY)


NO_COST = pl.CostEstimate(flops=3 * 10**8, bytes_accessed=0, transcendentals=0)


class Chain:
    last = None

    def note(self, outs):
        self.last = min(jax.tree_util.tree_leaves(outs), key=lambda v: v.size * v.dtype.itemsize)

    def __call__(self, body, at, **kwargs):
        def run(*args):
            if self.last is not None:
                inner = body
                kwargs["in_specs"] = kwargs["in_specs"][:at] + [ANY] + kwargs["in_specs"][at:]
                alias = kwargs.get("input_output_aliases", {})
                kwargs["input_output_aliases"] = {i + (i >= at): o for i, o in alias.items()}

                def outer(*refs):
                    inner(*refs[:at], *refs[at + 1 :])

                args = args[:at] + (self.last,) + args[at:]
            else:
                outer = body
            outs = pl.pallas_call(outer, cost_estimate=NO_COST, **kwargs)(*args)
            self.note(outs)
            return outs

        return run


CHAIN = Chain()


def call(body, name, grid, scalars, ins, outs, scratch=(), vmem=60):
    def spec(block, index):
        return ANY if block is None else pl.BlockSpec(block, index)

    specs = [spec(b, i) for _, b, i in ins]
    arrays = [a for a, _, _ in ins]
    inner = body
    if CHAIN.last is not None:
        specs, arrays = [ANY] + specs, [CHAIN.last] + arrays

        def inner(scalar, extra, *refs):
            body(scalar, *refs)

    got = pl.pallas_call(
        inner,
        grid_spec=pltpu.PrefetchScalarGridSpec(
            num_scalar_prefetch=1,
            grid=(grid,),
            in_specs=specs,
            out_specs=[spec(b, i) for _, _, b, i in outs],
            scratch_shapes=list(scratch),
        ),
        out_shape=[jax.ShapeDtypeStruct(s, t) for s, t, _, _ in outs],
        compiler_params=pltpu.CompilerParams(
            dimension_semantics=("arbitrary",), vmem_limit_bytes=vmem * 2**20
        ),
        name=name,
        cost_estimate=NO_COST,
    )(scalars, *arrays)
    CHAIN.note(got)
    return got


def whole(a):
    return (a, a.shape, lambda g, i, n=a.ndim: (0,) * n)


def step_from(first, count, lead=0, tail=1):
    def index(g, info):
        return (0,) * lead + (jnp.clip(g - first, 0, count - 1),) + (0,) * tail

    return index


class Copies:
    def __init__(self, sem):
        self.sem, self.count, self.out = sem, 0, []

    def load(self, src, dst):
        copy = pltpu.make_async_copy(src, dst, self.sem.at[self.count])
        self.count += 1
        copy.start()
        return copy

    def store(self, src, dst):
        self.out.append(self.load(src, dst))

    def finish(self):
        for copy in self.out:
            copy.wait()


def wait(*copies):
    for copy in copies:
        copy.wait()


def straight(body, name, scalars, rows_in, ins, outs, scratch, n_copies, vmem=60):
    return CHAIN(
        body,
        1,
        in_specs=[pl.BlockSpec(memory_space=pltpu.SMEM)]
        + [pl.BlockSpec(memory_space=pltpu.VMEM)] * len(rows_in)
        + [ANY] * len(ins),
        out_specs=[ANY] * len(outs),
        out_shape=[jax.ShapeDtypeStruct(s, t) for s, t in outs],
        scratch_shapes=[pltpu.VMEM(s, t) for s, t in scratch] + [pltpu.SemaphoreType.DMA((n_copies,))],
        compiler_params=pltpu.CompilerParams(vmem_limit_bytes=vmem * 2**20),
        name=name,
    )(scalars, *rows_in, *ins)


def part_of(ref, axis, start, size):
    span = pl.ds(pl.multiple_of(start, 128), size)
    return ref.at[span, :] if axis == 0 else ref.at[:, span]


def front(info, x_own, x_other, gain, bias, mixer_in, wave, spec, back, mixer_out):
    width = mixer_in.shape[0]
    half = width // 2
    rows = wave.shape[1]

    def body(info, gain, bias, x_own, x_other, w_in, wave, spec, back, w_mo,
             normed_o, value_o, gate_a_o, gate_b_o, zf_o, mixed_o, gated_out_o, part_o,
             xo, xt, w3, wv, sp, bk, wm, normed, value, gate_a, gate_b, gated, prod, zf, mixed, gated_out, part, sem):
        c, length = info[0], info[1]
        io = Copies(sem)
        x_in = [(io.load(x_own.at[pl.ds(2 * q, 2)], xo.at[pl.ds(2 * q, 2)]),
                 io.load(x_other.at[pl.ds(2 * q, 2)], xt.at[pl.ds(2 * q, 2)])) for q in range(4)]
        w_got = [io.load(part_of(w_in, 1, n * width + c * half, half), w3.at[n]) for n in range(3)]
        f_got = []
        for q in range(2):
            span = pl.ds(512 * q, 512)
            f_got.append((io.load(wave.at[:, span], wv.at[:, span]), io.load(spec.at[:, span], sp.at[:, span])))
        b_got = [io.load(back.at[pl.ds(512 * q, 512)], bk.at[pl.ds(512 * q, 512)]) for q in range(2)]
        m_got = io.load(part_of(w_mo, 0, c * half, half), wm)
        for q, span in enumerate(CHUNKS):
            wait(*x_in[q])
            hat, _ = stats(tokens(c, xo, xt, q))
            normed[span, :] = (hat * gain[...] + bias[...]).astype(BF16)
        io.store(normed, normed_o)
        wait(w_got[0])
        v = nn(normed[...], w3[0])
        value[...] = v.astype(BF16)
        io.store(value, value_o)
        wait(w_got[1])
        a = nn(normed[...], w3[1])
        gate_a[...] = a.astype(BF16)
        io.store(gate_a, gate_a_o)
        at_row = lax.broadcasted_iota(jnp.int32, a.shape, 0)
        gated[...] = jnp.where(at_row < length, v * a, 0.0).astype(BF16)
        wait(w_got[2])
        gate_b[...] = nn(normed[...], w3[2]).astype(BF16)
        io.store(gate_b, gate_b_o)
        for q in range(2):
            span, low = slice(512 * q, 512 * q + 512), slice(rows + 512 * q, rows + 512 * q + 512)
            wait(*f_got[q])
            re = nn(wv[0, span], gated[...])
            im = nn(wv[1, span], gated[...])
            zf[0, span] = re.astype(BF16)
            zf[1, span] = im.astype(BF16)
            kr, ki = sp[0, span], sp[1, span]
            prod[span, :] = (kr * re - ki * im).astype(BF16)
            prod[low, :] = (kr * im + ki * re).astype(BF16)
        io.store(zf, zf_o)
        for q in range(2):
            span = slice(512 * q, 512 * q + 512)
            wait(b_got[q])
            m = nn(bk[span, :], prod[...])
            mixed[span, :] = m.astype(BF16)
            out = (gate_b[span, :].astype(F32) * m).astype(BF16)
            gated_out[span, :] = out
            if q == 0:
                wait(m_got)
            part[span, :] = nn(out, wm[...]).astype(BF16)
            here = pl.ds(512 * q, 512)
            io.store(part.at[here], part_o.at[here])
        io.store(mixed, mixed_o)
        io.store(gated_out, gated_out_o)
        io.finish()

    thin, wide = ((rows, half), BF16), ((rows, width), BF16)
    tok = ((8, 64, width), BF16)
    return straight(
        body, "front", info, [gain, bias], [x_own, x_other, mixer_in, wave, spec, back, mixer_out],
        [wide, thin, thin, thin, ((2, rows, half), BF16), thin, thin, wide],
        [tok, tok, ((3, width, half), BF16), (wave.shape, BF16), (spec.shape, F32), (back.shape, BF16),
         ((half, width), BF16), wide, thin, thin, thin, thin, ((2 * rows, half), BF16), ((2, rows, half), BF16), thin,
         thin, wide],
        8 + 3 + 4 + 2 + 1 + 9,
    )


def grad_shapes(rows, width):
    one = ((rows, width), BF16)
    return [one, one, ((2, rows, width), BF16)]


def make_grads(io, info, left, right, grad, send_a_o, send_b_o, keeps_o):
    for g, out in enumerate((send_a_o, send_b_o, keeps_o.at[0], keeps_o.at[1])):
        n = info[2 + g]
        grad[g] = tn(left(n), right(n)).astype(BF16)
        io.store(grad.at[g], out)


def up_grads(info, d_pre, normed):
    rows, ff = d_pre.shape
    width = normed.shape[1]

    def body(info, d_pre, normed, send_a_o, send_b_o, keeps_o, left, right, grad, sem):
        io = Copies(sem)
        l_in = []
        for g in range(4):
            l_in.append(io.load(part_of(d_pre, 1, info[2 + g] * (ff // 4), ff // 4), left.at[g]))
            if g == 0:
                r_in = io.load(normed, right)
        wait(r_in)
        for g, out in enumerate((send_a_o, send_b_o, keeps_o.at[0], keeps_o.at[1])):
            wait(l_in[g])
            grad[g] = tn(left[g], right[...]).astype(BF16)
            io.store(grad.at[g], out)
        io.finish()

    return straight(
        body, "up_grads", info, [], [d_pre, normed], grad_shapes(ff // 4, width),
        [((4, rows, ff // 4), BF16), ((rows, width), BF16), ((4, ff // 4, width), BF16)], 9,
    )


def set_sums(sums, gains, biases):
    sums[...] = jnp.zeros_like(sums)
    sums[0:1, :] = gains
    sums[1:2, :] = biases


def block_of(ref, n, size):
    return ref[:, pl.ds(pl.multiple_of(n * size, 128), size)]


def feed_forward(info, x_own, x_other, cot_own, cot_other, part, got, gain, bias, up_weight, down_weight):
    rows, width = part.shape
    ff = up_weight.shape[1] // 2
    cols = ff // 3

    def body(info, gain, bias, x_own, x_other, cot_own, cot_other, part, got, w_up, w_dn,
             middle_o, normed_o, d_pre_o, cot_o, d_sec_o, sums_o, send_a_o, send_b_o, keeps_o, keep_o, give_o,
             xo, xt, co, ct, pt, gt, up, dn, middle, normed, cot, act, d_pre, d_sec, acc, sums, grad, out, keep, give, sem):
        c = info[0]
        io = Copies(sem)
        x_in, c_in = [], []
        for q, span in enumerate(CHUNKS):
            two, here = pl.ds(2 * q, 2), pl.ds(256 * q, 256)
            x_in.append([io.load(x_own.at[two], xo.at[two]), io.load(x_other.at[two], xt.at[two]),
                         io.load(part.at[here], pt.at[here]), io.load(got.at[here], gt.at[here])])
        u_in = [io.load(part_of(w_up, 1, c * ff, cols), up.at[0])]
        c_in = [io.load(cot_own, co), io.load(cot_other, ct)]
        d_in = [io.load(part_of(w_dn, 0, c * ff, cols), dn.at[0])]
        for n in range(1, 3):
            u_in.append(io.load(part_of(w_up, 1, c * ff + n * cols, cols), up.at[n]))
            d_in.append(io.load(part_of(w_dn, 0, c * ff + n * cols, cols), dn.at[n]))
        for q, span in enumerate(CHUNKS):
            wait(*x_in[q])
            mid = tokens(c, xo, xt, q) + pt[span, :].astype(F32) + gt[span, :].astype(F32)
            middle[span, :] = mid
            hat, _ = stats(mid)
            normed[span, :] = (hat * gain[...] + bias[...]).astype(BF16)
        io.store(middle, middle_o)
        io.store(normed, normed_o)
        wait(*c_in)
        for q, span in enumerate(CHUNKS):
            cot[span, :] = tokens(c, co, ct, q).astype(BF16)
        io.store(cot, cot_o)
        for n in range(3):
            wait(u_in[n], d_in[n])
            v, slope = gelu_pair(nn(normed[...], up[n]))
            here = pl.ds(n * cols, cols)
            act[:, n * cols : (n + 1) * cols] = v.astype(BF16)
            d_pre[n] = (nt(cot[...], dn[n]) * slope).astype(BF16)
            io.store(d_pre.at[n], d_pre_o.at[:, here])
            more = nt(d_pre[n], up[n])
            if n == 0:
                acc[...] = more
            else:
                acc[...] += more
            more = nn(act[:, n * cols : (n + 1) * cols], dn[n])
            if n == 0:
                out[...] = more
            else:
                out[...] += more
        gains, biases = 0.0, 0.0
        for q, span in enumerate(CHUNKS):
            ds = acc[span, :]
            d_sec[span, :] = ds.astype(BF16)
            here = pl.ds(256 * q, 256)
            io.store(d_sec.at[here], d_sec_o.at[here])
            hat, _ = stats(middle[span, :])
            gains += jnp.sum(ds * hat, axis=0, keepdims=True)
            biases += jnp.sum(ds, axis=0, keepdims=True)
            set_own(keep, q, c, out[span, :] + middle[span, :])
            set_own(give, q, c, out[span, :], False)
        set_sums(sums, gains, biases)
        io.store(sums, sums_o)
        io.store(give, give_o)
        io.store(keep, keep_o)
        make_grads(io, info, lambda n: block_of(act, n, ff // 4), lambda n: cot[...], grad, send_a_o, send_b_o, keeps_o)
        io.finish()

    tok, wide, long = ((8, 64, width), BF16), ((rows, width), BF16), ((rows, ff), BF16)
    full = ((rows, width), F32)
    slab = ((3, rows, cols), BF16)
    return straight(
        body, "feed_forward", info, [gain, bias],
        [x_own, x_other, cot_own, cot_other, part, got, up_weight, down_weight],
        [full, wide, long, wide, wide, ((8, width), F32)] + grad_shapes(ff // 4, width) + [((8, 64, width), F32), tok],
        [tok, tok, tok, tok, wide, wide, ((3, width, cols), BF16), ((3, cols, width), BF16), full, wide, wide, long, slab,
         wide, full, ((8, width), F32), ((4, ff // 4, width), BF16), full, ((8, 64, width), F32), tok],
        16 + 2 + 6 + 3 + 3 + 5 + 2 + 4,
    )


def backward(
    info, d_sec, got, middle, cot, gain, mixer_out, mixed, gate_b, value, gate_a, wave, spec, zf, back, normed, gated_out
):
    rows, width = middle.shape
    half = width // 2

    def body(info, gain, d_sec, got, middle, cot, w_mo, mixed, gate_b, value, gate_a, wave, spec, zf, back,
             normed, gated_out, d_own_o, tf_o, d_proj_o, send_a_o, send_b_o, keeps_o,
             ds, gt, md, cs, wm, mx, gb, vl, ga, wv, sp, zs, bk, right, d_own, d_gb, d_mixed, prod, tf, left, grad, sem):
        c, length = info[0], info[1]
        io = Copies(sem)
        first = []
        for q in range(4):
            here = pl.ds(256 * q, 256)
            first.append([io.load(s.at[here], t.at[here]) for s, t in ((middle, md), (d_sec, ds), (got, gt), (cot, cs))])
        go_in = [io.load(part_of(w_mo, 0, c * half, half), wm), io.load(mixed, mx), io.load(gate_b, gb)]
        f_in = []
        for q in range(2):
            span = pl.ds(512 * q, 512)
            f_in.append([io.load(s.at[:, span], t.at[:, span]) for s, t in ((wave, wv), (spec, sp), (zf, zs))])
        b_in = [io.load(back.at[pl.ds(512 * q, 512)], bk.at[pl.ds(512 * q, 512)]) for q in range(2)]
        v_in = [io.load(value, vl), io.load(gate_a, ga)]
        g_in = [io.load(normed, right.at[0]), io.load(gated_out, left.at[:, pl.ds(3 * half, half)])]
        d_mid = right.at[1]
        for q, span in enumerate(CHUNKS):
            wait(*first[q])
            hat, inv = stats(md[span, :])
            t = (ds[span, :].astype(F32) + gt[span, :].astype(F32)) * gain[...]
            v = cs[span, :].astype(F32) + norm_back(t, hat, inv)
            d_mid[span, :] = v.astype(BF16)
            set_own(d_own, q, c, v)
        io.store(d_own, d_own_o)
        wait(*go_in)
        d_go = nt(d_mid[...], wm[...])
        d_gb[...] = (d_go * mx[...].astype(F32)).astype(BF16)
        d_mixed[...] = (d_go * gb[...].astype(F32)).astype(BF16)
        for q in range(2):
            span, low = slice(512 * q, 512 * q + 512), slice(rows + 512 * q, rows + 512 * q + 512)
            wait(*f_in[q])
            re = nn(wv[0, span], d_mixed[...])
            im = nn(wv[1, span], d_mixed[...])
            kr, ki = sp[0, span], sp[1, span]
            prod[span, :] = (kr * re + ki * im).astype(BF16)
            prod[low, :] = (kr * im - ki * re).astype(BF16)
            zr, zi = zs[0, span].astype(F32), zs[1, span].astype(F32)
            tf[0, span] = ((zr * re + zi * im) * (1.0 / rows)).astype(BF16)
            tf[1, span] = ((zr * im - zi * re) * (1.0 / rows)).astype(BF16)
        io.store(tf, tf_o)
        wait(*v_in)
        for q in range(2):
            span = slice(512 * q, 512 * q + 512)
            wait(b_in[q])
            m = nn(bk[span, :], prod[...])
            at_row = 512 * q + lax.broadcasted_iota(jnp.int32, m.shape, 0)
            m = jnp.where(at_row < length, m, 0.0)
            left[span, 0:half] = (m * ga[span, :].astype(F32)).astype(BF16)
            left[span, half : 2 * half] = (m * vl[span, :].astype(F32)).astype(BF16)
            left[span, 2 * half : 3 * half] = d_gb[span, :]
            here = pl.ds(512 * q, 512)
            io.store(left.at[here, pl.ds(0, 3 * half)], d_proj_o.at[here])
        wait(*g_in)
        make_grads(
            io, info, lambda n: block_of(left, n, half), lambda n: right[n // 3], grad, send_a_o, send_b_o, keeps_o
        )
        io.finish()

    wide, thin, full = ((rows, width), BF16), ((rows, half), BF16), ((rows, width), F32)
    own, freq, proj = ((8, 64, width), F32), ((2, rows, half), BF16), ((rows, 3 * half), BF16)
    return straight(
        body, "backward", info, [gain],
        [d_sec, got, middle, cot, mixer_out, mixed, gate_b, value, gate_a, wave, spec, zf, back, normed, gated_out],
        [own, freq, proj] + grad_shapes(half, width),
        [wide, wide, full, wide, ((half, width), BF16), thin, thin, thin, thin, (wave.shape, BF16), (spec.shape, F32),
         freq, (back.shape, BF16), ((2, rows, width), BF16), own, thin, thin, ((2 * rows, half), BF16), freq,
         ((rows, 4 * half), BF16), ((4, half, width), BF16)],
        16 + 3 + 6 + 2 + 2 + 2 + 4 + 4,
    )


def norm_in_back(info, d_proj, mixer_in, x_own, x_other):
    rows = d_proj.shape[0]
    width = mixer_in.shape[0]
    half = width // 2

    def body(info, d_proj, w_in, x_own, x_other, keep_o, give_o, sums_o,
             dp, w3, xo, xt, acc, keep, give, sums, sem):
        c = info[0]
        io = Copies(sem)
        got = []
        for n in range(3):
            got.append([io.load(d_proj.at[:, pl.ds(n * half, half)], dp.at[n]),
                        io.load(part_of(w_in, 1, n * width + c * half, half), w3.at[n])])
        x_in = [io.load(x_own, xo), io.load(x_other, xt)]
        for n in range(3):
            wait(*got[n])
            more = nt(dp[n], w3[n])
            if n == 0:
                acc[...] = more
            else:
                acc[...] += more
        wait(*x_in)
        gains, biases = 0.0, 0.0
        for q, span in enumerate(CHUNKS):
            dn = acc[span, :]
            hat, _ = stats(tokens(c, xo, xt, q))
            gains += jnp.sum(dn * hat, axis=0, keepdims=True)
            biases += jnp.sum(dn, axis=0, keepdims=True)
            set_own(keep, q, c, dn)
            set_own(give, q, c, dn, False)
        io.store(give, give_o)
        io.store(keep, keep_o)
        set_sums(sums, gains, biases)
        io.store(sums, sums_o)
        io.finish()

    tok = ((8, 64, width), BF16)
    own = ((8, 64, width), F32)
    return straight(
        body, "norm_in_back", info, [], [d_proj, mixer_in, x_own, x_other], [own, tok, ((8, width), F32)],
        [((3, rows, half), BF16), ((3, width, half), BF16), tok, tok, ((rows, width), F32), own, tok,
         ((8, width), F32)],
        11,
        vmem=28,
    )


def filter_back(info, tf, spread, f_out, slope2, slope1, turn, sides, back, norm_sums, second_sums):
    rows, half = tf.shape[1:]
    width = 2 * half

    def body(info, spread, f_out, slope2, slope1, turn, sides, norm_s, second_s, tf, back, out_o,
             tv, bk, out, sem):
        io = Copies(sem)
        t_in = [io.load(tf.at[n], tv.at[pl.ds(n * rows, rows)]) for n in range(2)]
        b_in = [io.load(back.at[pl.ds(512 * q, 512)], bk.at[pl.ds(512 * q, 512)]) for q in range(2)]
        wait(*t_in)
        g_fo = tn(spread[...], tv[...])[0:64] * float(rows)
        kf = nt(tv[...], f_out[...]).astype(BF16)
        wait(*b_in)
        d_s = slope2[...] * nn(bk[...], kf)
        high = lax.Precision.HIGHEST
        both = d_s + slope1[...] * jnp.dot(d_s, turn[...], precision=high, preferred_element_type=F32)
        g = tn(sides[...].astype(BF16), both.astype(BF16))
        lane = lax.broadcasted_iota(jnp.int32, (64, 128), 1)
        g = jnp.where(lane < 64, g[0:64], g[64:128])
        out[...] = jnp.zeros_like(out)
        out[0:32, 0:half] = g_fo[0:32].astype(BF16)
        out[0:32, half:] = g_fo[32:64].astype(BF16)
        for n in range(6):
            pair = [g[8 * n : 8 * n + 8]]
            if n < 2:
                pair.append(g[48 + 8 * n : 56 + 8 * n])
            elif n == 2:
                pair.append(jnp.broadcast_to(jnp.sum(both, axis=0, keepdims=True), (8, 128)))
            else:
                pair.append(jnp.zeros((8, 128), F32))
            out[32:48, 128 * n : 128 * n + 128] = jnp.concatenate(pair, axis=0).astype(BF16)
        out[48:64, :] = jnp.concatenate([norm_s[...], second_s[...]], axis=0).astype(BF16)
        io.store(out, out_o)
        io.finish()

    return straight(
        body, "filter_back", info, [spread, f_out, slope2, slope1, turn, sides, norm_sums, second_sums], [tf, back],
        [((64, width), BF16)],
        [((2 * rows, half), BF16), (back.shape, BF16), ((64, width), BF16)], 5, vmem=22,
    )[0]


def unpack_small(info, own, got):
    width = own.shape[1]
    half = width // 2

    def body(info, own, got, g_fo, g_fm, g_fi, b_m, b_f, norms, seconds):
        a, b = own[0:64, :].astype(F32), got[0:64, :].astype(F32)
        lo = jnp.where(info[0] == 0, a[0:32], b[0:32])
        hi = jnp.where(info[0] == 0, b[0:32], a[0:32])
        g_fo[0:32, 0:half], g_fo[32:64, 0:half] = lo[:, 0:half], lo[:, half:]
        g_fo[0:32, half:], g_fo[32:64, half:] = hi[:, 0:half], hi[:, half:]
        s = a[32:64] + b[32:64]
        tiles = [s[0:8, 128 * n : 128 * n + 128] for n in range(6)] + [s[8:16, 128 * n : 128 * n + 128] for n in range(3)]
        g = jnp.concatenate(tiles[:8], axis=0)
        g_fm[...] = g[:, 0:64]
        g_fi[...] = g[0:33, 64:128]
        b_m[...] = tiles[8][0:1, 0:64]
        b_f[...] = tiles[8][0:1, 64:128]
        norms[...] = s[16:24]
        seconds[...] = s[24:32]

    shapes = [(64, width), (64, 64), (33, 64), (1, 64), (1, 64), (8, width), (8, width)]
    return CHAIN(
        body,
        1,
        in_specs=[pl.BlockSpec(memory_space=pltpu.SMEM)] + [pl.BlockSpec(memory_space=pltpu.VMEM)] * 2,
        out_specs=[pl.BlockSpec(memory_space=pltpu.VMEM)] * len(shapes),
        out_shape=[jax.ShapeDtypeStruct(s, F32) for s in shapes],
        compiler_params=pltpu.CompilerParams(vmem_limit_bytes=16 * 2**20),
        name="unpack_small",
    )(info, own, got)


def finish_output(out_keep, out_got):
    def body(out_keep, out_got, out):
        out[...] = (out_keep[...] + out_got[...].astype(F32)).astype(BF16)

    return CHAIN(
        body,
        0,
        in_specs=[pl.BlockSpec(memory_space=pltpu.VMEM)] * 2,
        out_specs=pl.BlockSpec(memory_space=pltpu.VMEM),
        out_shape=jax.ShapeDtypeStruct(out_keep.shape, BF16),
        compiler_params=pltpu.CompilerParams(vmem_limit_bytes=16 * 2**20),
        name="finish_output",
    )(out_keep, out_got)


def finish_inputs(gain, d_norm_keep, d_norm_got, d_mid_own, x_half):
    def body(gain, d_norm_keep, d_norm_got, d_mid_own, x_half, out):
        for p in range(x_half.shape[0]):
            hat, inv = stats(x_half[p].astype(F32))
            q = (d_norm_keep[p] + d_norm_got[p].astype(F32)) * gain[...]
            out[p] = (d_mid_own[p] + norm_back(q, hat, inv)).astype(BF16)

    return CHAIN(
        body,
        0,
        in_specs=[pl.BlockSpec(memory_space=pltpu.VMEM)] * 5,
        out_specs=pl.BlockSpec(memory_space=pltpu.VMEM),
        out_shape=jax.ShapeDtypeStruct(x_half.shape, BF16),
        compiler_params=pltpu.CompilerParams(vmem_limit_bytes=24 * 2**20),
        name="finish_inputs",
    )(gain, d_norm_keep, d_norm_got, d_mid_own, x_half)


def split_back(info, got):
    _, n, width = got.shape

    def body(info, got, keep, give):
        keep[...] = got[pl.ds(4 * info[0], 4)]
        give[...] = got[pl.ds(4 - 4 * info[0], 4)]

    return small(body, "split_back", [((4, n, width), BF16)] * 2, info, got)


def join_back(info, keep, got, dtype):
    _, n, width = keep.shape

    def body(info, keep, got, out):
        a, b = keep[...].astype(F32), got[...].astype(F32)
        out[:, 0:n, :] = jnp.where(info[0] == 0, a, b).astype(dtype)
        out[:, n:, :] = jnp.where(info[0] == 0, b, a).astype(dtype)

    return small(body, "join_back", [((4, 2 * n, width), dtype)], info, keep, got)[0]


def small(body, name, outs, *ins):
    return CHAIN(
        body,
        1,
        in_specs=[pl.BlockSpec(memory_space=pltpu.SMEM)] + [pl.BlockSpec(memory_space=pltpu.VMEM)] * (len(ins) - 1),
        out_specs=[pl.BlockSpec(memory_space=pltpu.VMEM)] * len(outs),
        out_shape=[jax.ShapeDtypeStruct(s, t) for s, t in outs],
        compiler_params=pltpu.CompilerParams(vmem_limit_bytes=16 * 2**20),
        name=name,
    )(*ins)


def plus(a, b):
    return (a.astype(F32) + b.astype(F32)).astype(BF16)


class Reducer:
    def __init__(self, pos, send_a, send_b, keeps):
        self.pos, self.keeps = pos, keeps
        self.rows, self.cols = send_a.shape
        self.got = (send(send_a, PX), send(send_b, PY))

    def step2(self):
        n = self.rows // 2

        def body(pos, keeps, got_a, got_b, out_a, out_b, keep):
            for k, (got, out) in enumerate(((got_a, out_a), (got_b, out_b))):
                p = pos[1 - k]
                mine, others = at(p, n), at(1 - p, n)
                out[...] = plus(keeps[k, others, :], got[others, :])
                keep[k] = plus(keeps[k, mine, :], got[mine, :])

        a, b, self.keeps = small(
            body, "step2", [((n, self.cols), BF16)] * 2 + [((2, n, self.cols), BF16)], self.pos, self.keeps, *self.got
        )
        self.got = (send(a, PY), send(b, PX))

    def step3(self):
        n = self.rows // 4

        def body(pos, keeps, got_a, got_b, out, keep):
            mine, others = at(pos[2], n, 32), at(1 - pos[2], n, 32)
            for k, got in enumerate((got_a, got_b)):
                out[k] = plus(keeps[k, others, :], got[others, :])
                keep[k] = plus(keeps[k, mine, :], got[mine, :])

        shape = (2, n, self.cols)
        out, self.keeps = small(body, "step3", [(shape, BF16), (shape, BF16)], self.pos, self.keeps, *self.got)
        self.got = (send(out, PZ[1]),)

    def step4(self, extra=None):
        n = self.rows // 2
        self.extra = 0 if extra is None else extra.shape[0]

        def body(pos, keeps, got, *refs):
            out = refs[-1]
            for k in range(2):
                out[k * n // 2 : (k + 1) * n // 2, :] = plus(keeps[k], got[k])
            if extra is not None:
                out[n:, :] = refs[0][...]

        ins = [self.keeps, *self.got] + ([] if extra is None else [extra])
        (self.total,) = small(body, "step4", [((n + self.extra, self.cols), BF16)], self.pos, *ins)
        self.got = (send(self.total, PZ[2]),)

    def step5(self):
        def body(pos, total, got, out):
            out[...] = plus(total[...], got[...])

        (self.total,) = small(body, "step5", [(self.total.shape, BF16)], self.pos, self.total, *self.got)
        self.got = (send(self.total, PZ[1]),)

    def step6(self):
        n, more = self.rows // 4, self.extra

        def body(pos, total, got, out_a, out_b):
            mine, others = at(pos[2], n, 32), at(1 - pos[2], n, 32)
            for k, out in enumerate((out_a, out_b)):
                out[mine, :] = total[k * n : (k + 1) * n, :]
                out[others, :] = got[k * n : (k + 1) * n, :]
            if more:
                out_a[2 * n :, :] = plus(total[2 * n :, :], got[2 * n :, :])

        shapes = [((2 * n + more, self.cols), BF16), ((2 * n, self.cols), BF16)]
        self.own = small(body, "step6", shapes, self.pos, self.total, *self.got)
        self.got = (send(self.own[0], PY), send(self.own[1], PX))

    def step7(self):
        n, more = self.rows // 2, self.extra

        def body(pos, own_a, own_b, got_a, got_b, out_a, out_b):
            for k, (own, got, out) in enumerate(((own_a, got_a, out_a), (own_b, got_b, out_b))):
                p = pos[1 - k]
                out[at(p, n), :] = own[0:n, :]
                out[at(1 - p, n), :] = got[0:n, :]
            if more:
                out_a[2 * n :, :] = plus(own_a[n:, :], got_a[n:, :])

        shapes = [((2 * n + more, self.cols), BF16), ((2 * n, self.cols), BF16)]
        self.near = small(body, "step7", shapes, self.pos, *self.own, *self.got)
        self.got = (send(self.near[0], PX), send(self.near[1], PY))
        self.pair_near = [send(v, PC) for v in self.near]

    def step8(self):
        n, more = self.rows, self.extra

        def body(pos, near, far_a, far_b, out_a, out_b, *sums):
            out_a[...] = far_a[0:n, :]
            out_b[...] = far_b[...]
            if more:
                sums[0][...] = plus(near[n:, :], far_a[n:, :])

        shapes = [((n, self.cols), BF16)] * 2 + ([((more, self.cols), BF16)] if more else [])
        *self.far, = small(body, "step8", shapes, self.pos, self.near[0], *self.got)
        if more:
            self.sum = self.far.pop()
        self.pair_far = [send(v, PC) for v in self.far]


def write(bufs, sources, spots, moves):
    n, m = len(sources), len(bufs)
    rows, cols = sources[1].shape
    turned = any(t for _, _, _, _, t in moves([0, 0, 0]))
    straight_ones = any(not t for _, _, _, _, t in moves([0, 0, 0]))

    def body(*refs):
        spot = refs[0]
        src, out = refs[1 : 1 + n], refs[1 + n + m : 1 + n + 2 * m]
        mark, wide, tall, sem = refs[1 + n + 2 * m :]
        mark[...] = jnp.zeros_like(mark)

        def each(act):
            for k in range(n):
                for when, b, i, j, t in moves([spot[k, e] for e in range(3)]):
                    size = (cols, rows) if t else (rows, cols)
                    src_ref = tall.at[k] if t else wide.at[k]
                    copy = pltpu.make_async_copy(
                        src_ref,
                        out[b].at[pl.ds(pl.multiple_of(i, 128), size[0]), pl.ds(pl.multiple_of(j, 128), size[1])],
                        sem.at[k],
                    )
                    act(k, when, t, copy)

        def begin(k, when, t, copy):
            @pl.when(when)
            def _():
                if t:
                    tall[k] = src[k][0:rows, :].astype(F32).T
                else:
                    wide[k] = src[k][0:rows, :].astype(F32)
                copy.start()

        def finish(k, when, t, copy):
            @pl.when(when)
            def _():
                copy.wait()

        each(begin)
        each(finish)

    return CHAIN(
        body,
        1,
        in_specs=[pl.BlockSpec(memory_space=pltpu.SMEM)] + [pl.BlockSpec(memory_space=pltpu.VMEM)] * n + [ANY] * m,
        out_specs=[ANY] * m + [pl.BlockSpec(memory_space=pltpu.VMEM)],
        out_shape=[jax.ShapeDtypeStruct(b.shape, F32) for b in bufs] + [jax.ShapeDtypeStruct((8, 128), F32)],
        input_output_aliases={1 + n + b: b for b in range(m)},
        scratch_shapes=[
            pltpu.VMEM((n, rows, cols) if straight_ones else (n, 8, 128), F32),
            pltpu.VMEM((n, cols, rows) if turned else (n, 8, 128), F32),
            pltpu.SemaphoreType.DMA((n,)),
        ],
        compiler_params=pltpu.CompilerParams(vmem_limit_bytes=20 * 2**20),
        name="write",
    )(spots, *sources, *bufs)[:-1]


def fresh(*shapes):
    def body(*refs):
        pass

    return pl.pallas_call(
        body, out_specs=[ANY] * len(shapes), out_shape=[jax.ShapeDtypeStruct(s, F32) for s in shapes], name="fresh"
    )()


def write_down(s):
    return [(s[0] >= 0, 0, s[0] * 1536 + s[1] * 768 + s[2] * 384, 0, False)]


def write_up(s):
    return [(s[0] >= 0, 0, 0, s[0] * 1536 + s[1] * 768 + s[2] * 384, True)]


def write_mix(s):
    n = s[1] * 2 + s[2]
    return [(n < 3, 0, 0, n * 768 + s[0] * 384, True), (n == 3, 1, s[0] * 384, 0, False)]


def chip_local(
    inputs, lengths, norm_gain, norm_bias, mixer_in, filter_in, filter_in_bias, filter_mid, filter_mid_bias,
    filter_out, mixer_out, second_gain, second_bias, up_weight, down_weight, cotangent,
):
    CHAIN.last = None
    s = lax.axis_index("seq")
    d = lax.axis_index("dp")
    z, x, y, c = s // 2, s % 2, d // 2, d % 2
    width = inputs.shape[-1]
    rows = 8 * inputs.shape[1]
    half = width // 2
    x_swapped = swap_in(inputs, c)
    filter_in, filter_out, filter_mid, cotangent, lengths, norm_gain, norm_bias, second_gain, second_bias, x_swapped = tie(
        filter_in, filter_out, filter_mid, cotangent, lengths, norm_gain, norm_bias, second_gain, second_bias, x_swapped
    )
    x_half = exchange_seq(x_swapped)
    cot_half = swap_in(cotangent, c)
    other_len = send(lengths, PC)
    length = pick(jnp.where(c == (z >> 1), lengths, other_len), (z & 1) * 2 + x)
    tab = [1 - x, 3 - y, x, 2 + y]
    info = jnp.stack([c, length, *tab])
    zero = 0 * c
    pos = jnp.stack([x, y, z & 1, z >> 1])
    near = jnp.stack([jnp.stack(v) for v in ((c, zero, x), (c, zero + 1, y), (1 - c, zero, x), (1 - c, zero + 1, y))])
    far = jnp.stack(
        [jnp.stack(v) for v in ((c, zero, 1 - x), (c, zero + 1, 1 - y), (1 - c, zero, 1 - x), (1 - c, zero + 1, 1 - y))]
    )
    norm_gain, norm_bias = norm_gain[None], norm_bias[None]
    second_gain, second_bias = second_gain[None], second_bias[None]
    f_out = lanes(filter_out, c * half, half)
    waves = dft_table(rows)
    table = jnp.asarray(waves, BF16)
    wave = table.reshape(2, rows, rows)
    back = jnp.asarray(waves.T, BF16)
    feats = jnp.asarray(feature_table(rows))
    first_act = jnp.dot(feats, filter_in, precision=HIGH) + filter_in_bias
    h1 = jnp.sin(first_act)
    second_act = jnp.dot(h1, filter_mid, precision=HIGH) + filter_mid_bias
    h2 = jnp.sin(second_act)
    h2_hi = h2.astype(BF16)
    h2_lo = (h2 - h2_hi.astype(F32)).astype(BF16)
    hf = mm(table, jnp.concatenate([h2_hi, h2_lo], axis=1))
    hf = (hf[:, :64] + hf[:, 64:]) * (1.0 / rows)
    spec = jnp.dot(hf, f_out, precision=lax.Precision.HIGH).reshape(2, rows, half)
    spread = jnp.pad(hf, ((0, 0), (0, 64))).astype(BF16)
    f_low = jnp.pad(f_out, ((0, 64), (0, 0))).astype(BF16)
    slope2 = jnp.pad(jnp.cos(second_act), ((0, 0), (0, 64)))
    slope1 = jnp.pad(jnp.cos(first_act), ((0, 0), (64, 0)))
    turn = jnp.pad(filter_mid.T, ((0, 64), (64, 0)))
    sides = jnp.concatenate([h1, jnp.pad(feats, ((0, 0), (0, 31)))], axis=1)
    x_half, spec, cot_half, info, norm_gain, norm_bias, second_gain, second_bias = tie(
        x_half, spec, cot_half, info, norm_gain, norm_bias, second_gain, second_bias
    )
    cot_half = exchange_seq(cot_half)
    x_pair = send(x_half, PC)
    normed, value, gate_a, gate_b, zf, mixed, gated_out, part = front(
        info, x_half, x_pair, norm_gain, norm_bias, mixer_in, wave, spec, back, mixer_out
    )
    cot_pair = send(cot_half, PC)
    part_pair, spread, f_low, slope2, slope1, turn, sides = tie(
        send(part, PC), spread, f_low, slope2, slope1, turn, sides
    )
    middle, second_normed, d_pre, cot, d_second, second_sums, *more = feed_forward(
        info, x_half, x_pair, cot_half, cot_pair, part, part_pair, second_gain, second_bias, up_weight, down_weight
    )
    out_keep, out_give = more[3:]
    d_second_pair = send(d_second, PC)
    out_got = send(out_give, PC)
    down = Reducer(pos, *more[:3])
    up = Reducer(pos, *up_grads(info, d_pre, second_normed))
    out_back = exchange_seq(finish_output(out_keep, out_got))
    d_mid_own, tf, d_proj, *g_mix = backward(
        info, d_second, d_second_pair, middle, cot, second_gain, mixer_out, mixed, gate_b, value, gate_a, wave,
        spec, zf, back, normed, gated_out,
    )
    mix = Reducer(pos, *g_mix)
    down.step2()
    d_norm_keep, d_norm_give, norm_sums = norm_in_back(info, d_proj, mixer_in, x_half, x_pair)
    d_norm_got = send(d_norm_give, PC)
    up.step2()
    down.step3()
    mix.step2()
    up.step3()
    down.step4()
    tiny = filter_back(
        info, tf, spread, f_low, slope2, slope1, turn, sides, back, norm_sums, second_sums
    )
    mix.step3()
    up.step4(tiny)
    out_keep, out_give = split_back(info, out_back)
    out_got = send(out_give, PC)
    down.step5()
    mix.step4()
    up.step5()
    dx_back = exchange_seq(finish_inputs(norm_gain, d_norm_keep, d_norm_got, d_mid_own, x_half))
    down.step6()
    mix.step5()
    down.step7()
    up.step6()
    mix.step6()
    bufs = fresh(down_weight.shape, up_weight.shape, mixer_in.shape, mixer_out.shape)
    down.step8()
    grad_down = write(bufs[:1], [*down.near, *down.pair_near], near, write_down)
    up.step7()
    mix.step7()
    (grad_down,) = write(grad_down, [*down.far, *down.pair_far], far, write_down)
    grad_up = write(bufs[1:2], [*up.near, *up.pair_near], near, write_up)
    grads_two = write(bufs[2:], [*mix.near, *mix.pair_near], near, write_mix)
    dx_keep, dx_give = split_back(info, dx_back)
    dx_got = send(dx_give, PC)
    up.step8()
    tiny_got = send(up.sum, PC)
    output = join_back(info, out_keep, out_got, BF16)
    grad_inputs = join_back(info, dx_keep, dx_got, F32)
    g_fo, g_fm, g_fi, b_m, b_f, norms, seconds = unpack_small(info, up.sum, tiny_got)
    mix.step8()
    (grad_up,) = write(grad_up, [*up.far, *up.pair_far], far, write_up)
    grad_in, grad_mo = write(grads_two, [*mix.far, *mix.pair_far], far, write_mix)
    return (
        output, grad_inputs, norms[0], norms[1], grad_in, g_fi, b_f[0], g_fm, b_m[0],
        g_fo, grad_mo, seconds[0], seconds[1], grad_up, grad_down,
    )


LAGS = 16


def shifted(value, axis, by):
    devices = lax.axis_size(axis)
    pairs = [(i, i + by) for i in range(devices) if 0 <= i + by < devices]
    return lax.ppermute(value, axis, pairs)


def plain_norm(values, gain, shift):
    center = values - jnp.mean(values, axis=-1, keepdims=True)
    spread = jnp.mean(center * center, axis=-1, keepdims=True)
    return center * lax.rsqrt(spread + EPSILON) * gain + shift


def features_of(taps, bands):
    steps = jnp.arange(taps, dtype=jnp.float32) / taps
    freqs = jnp.arange(1, bands + 1, dtype=jnp.float32)
    phase = 2.0 * math.pi * steps[:, None] * freqs[None, :]
    return jnp.concatenate([steps[:, None], jnp.cos(phase), jnp.sin(phase)], axis=1)


def taps_of(filter_in, filter_in_bias, filter_mid, filter_mid_bias, filter_out):
    table = features_of(KL, BANDS)
    first = jnp.sin(jnp.dot(table, filter_in, precision=HIGH) + filter_in_bias)
    second = jnp.sin(jnp.dot(first, filter_mid, precision=HIGH) + filter_mid_bias)
    return jnp.dot(second, filter_out, precision=HIGH)


def wave_tables(block_len):
    length = 2 * block_len
    index = jnp.arange(length, dtype=jnp.int32)
    angle = (index[:, None] * index[None, :] % length).astype(jnp.float32) * (
        2.0 * math.pi / length
    )
    return (jnp.cos(angle), jnp.sin(angle))


def split_table(table):
    leading = table.astype(jnp.bfloat16)
    remainder = (table - leading.astype(jnp.float32)).astype(jnp.bfloat16)
    return (leading, remainder)


def low_tables(cos_t, sin_t):
    length = cos_t.shape[0]
    half = length // 2
    return (
        split_table(cos_t[:, :half]),
        split_table(sin_t[:, :half]),
        split_table(cos_t[half:] / length),
        split_table(sin_t[half:] / length),
    )


def apply_split(pattern, halves, values):
    first = jnp.einsum(pattern, halves[0], values, preferred_element_type=jnp.float32)
    second = jnp.einsum(pattern, halves[1], values, preferred_element_type=jnp.float32)
    return first + second


def kernel_freq(kernel, cos_t, sin_t):
    block_len = cos_t.shape[0] // 2
    width = kernel.shape[1]
    count = kernel.shape[0] // block_len
    padded = jnp.concatenate(
        [
            jnp.zeros((block_len, width), jnp.float32),
            kernel,
            jnp.zeros((2 * block_len, width), jnp.float32),
        ],
        axis=0,
    )
    pieces = padded.reshape(count + 3, block_len, width)
    segments = jnp.concatenate([pieces[: count + 1], pieces[1 : count + 2]], axis=1)
    real = jnp.einsum("fn,mnd->mfd", cos_t, segments, precision=HIGH)
    imag = -jnp.einsum("fn,mnd->mfd", sin_t, segments, precision=HIGH)
    return (real, imag)


def to_freq(values, tables):
    real = apply_split("fc,scd->sfd", tables[0], values)
    imag = -apply_split("fc,scd->sfd", tables[1], values)
    return (real, imag)


def from_freq(real, imag, cos_t, sin_t):
    length = cos_t.shape[0]
    half = length // 2
    first = jnp.einsum("nf,sfd->snd", cos_t[half:], real, precision=HIGH)
    second = jnp.einsum("nf,sfd->snd", sin_t[half:], imag, precision=HIGH)
    return (first - second) / length


def grad_freq(values, tables):
    real = apply_split("nf,snd->sfd", tables[2], values)
    imag = -apply_split("nf,snd->sfd", tables[3], values)
    return (real, imag)


def grad_time(real, imag, cos_t, sin_t):
    half = cos_t.shape[0] // 2
    first = jnp.einsum("fc,sfd->scd", cos_t[:, :half], real, precision=HIGH)
    second = jnp.einsum("fc,sfd->scd", sin_t[:, :half], imag, precision=HIGH)
    return first - second


def add_forward(acc, k_real, k_imag, values, tables):
    z_real, z_imag = to_freq(values, tables)
    return (acc[0] + k_real * z_real - k_imag * z_imag, acc[1] + k_real * z_imag + k_imag * z_real)


def add_backward(acc, k_real, k_imag, grads, own_real, own_imag, tables):
    d_real, d_imag = grad_freq(grads, tables)
    new_real = acc[0] + k_real * d_real + k_imag * d_imag
    new_imag = acc[1] - k_imag * d_real + k_real * d_imag
    term_real = jnp.sum(own_real * d_real + own_imag * d_imag, axis=0)
    term_imag = jnp.sum(own_real * d_imag - own_imag * d_real, axis=0)
    return ((new_real, new_imag), (term_real, term_imag))


def forward_stack(stack, k_real, k_imag, acc, tables):

    def forward_step(carry, item):
        return (add_forward(carry, item[1], item[2], item[0], tables), None)

    result, _ = lax.scan(forward_step, acc, (stack, k_real, k_imag))
    return result


def backward_stack(stack, k_real, k_imag, acc, own_real, own_imag, tables):

    def backward_step(carry, item):
        return add_backward(carry, item[1], item[2], item[0], own_real, own_imag, tables)

    return lax.scan(backward_step, acc, (stack, k_real, k_imag))


def sum_everywhere(parts):
    flat_grads = jnp.concatenate([piece.reshape(-1) for piece in parts])
    portion = lax.psum_scatter(flat_grads, ("seq", "dp"), scatter_dimension=0, tiled=True)
    summed = lax.all_gather(portion.astype(jnp.bfloat16), ("seq", "dp"), axis=0, tiled=True).astype(
        portion.dtype
    )
    results = []
    offset = 0
    for piece in parts:
        results.append(summed[offset : offset + piece.size].reshape(piece.shape))
        offset = offset + piece.size
    return results


def block_local(
    inputs,
    lengths,
    norm_gain,
    norm_bias,
    mixer_in,
    filter_in,
    filter_in_bias,
    filter_mid,
    filter_mid_bias,
    filter_out,
    mixer_out,
    second_gain,
    second_bias,
    up_weight,
    down_weight,
    cotangent,
):
    seqs, block_len, width = inputs.shape
    row_count = seqs * block_len
    reach = min(LAGS, lax.axis_size("seq") - 1)
    rank = lax.axis_index("seq")
    position = rank * block_len + jnp.arange(block_len, dtype=jnp.int32)
    valid = (position[None, :] < lengths[:, None]).astype(jnp.float32)[:, :, None]
    cos_t, sin_t = wave_tables(block_len)
    tables = low_tables(cos_t, sin_t)
    kernel, filter_back = jax.vjp(
        taps_of, filter_in, filter_in_bias, filter_mid, filter_mid_bias, filter_out
    )
    k_real, k_imag = kernel_freq(kernel, cos_t, sin_t)
    x_full = inputs.astype(jnp.float32).reshape(row_count, width)
    normed = plain_norm(x_full, norm_gain, norm_bias).astype(jnp.bfloat16)
    projected = jnp.dot(normed, mixer_in, preferred_element_type=jnp.float32)
    value = projected[:, :width]
    gate_a = projected[:, width : 2 * width]
    gate_b = projected[:, 2 * width :]
    gated = (value * gate_a).astype(jnp.bfloat16).reshape(seqs, block_len, width) * valid.astype(
        jnp.bfloat16
    )
    own_real, own_imag = to_freq(gated, tables)
    initial = (
        k_real[0] * own_real - k_imag[0] * own_imag,
        k_real[0] * own_imag + k_imag[0] * own_real,
    )
    earlier = []
    for lag in range(1, reach + 1):
        earlier.append(shifted(gated, "seq", lag))
    y_real, y_imag = forward_stack(
        jnp.stack(earlier), k_real[1 : reach + 1], k_imag[1 : reach + 1], initial, tables
    )
    mixed = from_freq(y_real, y_imag, cos_t, sin_t).reshape(row_count, width)
    gated_out = (gate_b * mixed).astype(jnp.bfloat16)
    middle = x_full + jnp.dot(gated_out, mixer_out, preferred_element_type=jnp.float32)
    second_normed = plain_norm(middle, second_gain, second_bias).astype(jnp.bfloat16)
    pre = jnp.dot(second_normed, up_weight, preferred_element_type=jnp.float32)
    activated = jax.nn.gelu(pre, approximate=True).astype(jnp.bfloat16)
    result = middle + jnp.dot(activated, down_weight, preferred_element_type=jnp.float32)
    output = result.astype(jnp.bfloat16).reshape(seqs, block_len, width)
    upstream_low = cotangent.reshape(row_count, width)
    upstream = upstream_low.astype(jnp.float32)
    grad_down = jnp.einsum("rk,rd->kd", activated, upstream_low, preferred_element_type=jnp.float32)
    d_act = jnp.einsum("rd,kd->rk", upstream_low, down_weight, preferred_element_type=jnp.float32)
    _, gelu_back = jax.vjp(lambda arg: jax.nn.gelu(arg, approximate=True), pre)
    d_pre = gelu_back(d_act)[0].astype(jnp.bfloat16)
    grad_up = jnp.einsum("rd,rk->dk", second_normed, d_pre, preferred_element_type=jnp.float32)
    d_second = jnp.einsum("rk,dk->rd", d_pre, up_weight, preferred_element_type=jnp.float32)
    _, second_back = jax.vjp(plain_norm, middle, second_gain, second_bias)
    d_middle_norm, grad_second_gain, grad_second_bias = second_back(d_second)
    d_middle = upstream + d_middle_norm
    d_middle_low = d_middle.astype(jnp.bfloat16)
    grad_mixer_out = jnp.einsum(
        "rk,rd->kd", gated_out, d_middle_low, preferred_element_type=jnp.float32
    )
    d_gated_out = jnp.einsum(
        "rd,kd->rk", d_middle_low, mixer_out, preferred_element_type=jnp.float32
    )
    d_gate_b = d_gated_out * mixed
    d_mixed = (d_gated_out * gate_b).astype(jnp.bfloat16).reshape(seqs, block_len, width)
    empty_freq = jnp.zeros((seqs, 2 * block_len, width), jnp.float32)
    start_acc, own_terms = add_backward(
        (empty_freq, empty_freq), k_real[0], k_imag[0], d_mixed, own_real, own_imag, tables
    )
    unused = jnp.zeros((LAGS - reach, 2 * block_len, width), jnp.float32)
    later = []
    for lead in range(1, reach + 1):
        later.append(shifted(d_mixed, "seq", -lead))
    (z_real, z_imag), terms = backward_stack(
        jnp.stack(later),
        k_real[1 : reach + 1],
        k_imag[1 : reach + 1],
        start_acc,
        own_real,
        own_imag,
        tables,
    )
    dk_real = jnp.concatenate([own_terms[0][None], terms[0], unused], axis=0)
    dk_imag = jnp.concatenate([own_terms[1][None], terms[1], unused], axis=0)
    d_gated = (grad_time(z_real, z_imag, cos_t, sin_t) * valid).reshape(row_count, width)
    d_projected = jnp.concatenate([d_gated * gate_a, d_gated * value, d_gate_b], axis=1).astype(
        jnp.bfloat16
    )
    grad_mixer_in = jnp.einsum("rd,rk->dk", normed, d_projected, preferred_element_type=jnp.float32)
    d_normed = jnp.einsum("rk,dk->rd", d_projected, mixer_in, preferred_element_type=jnp.float32)
    _, first_back = jax.vjp(plain_norm, x_full, norm_gain, norm_bias)
    d_x_norm, grad_norm_gain, grad_norm_bias = first_back(d_normed)
    grad_inputs = (d_middle + d_x_norm).reshape(seqs, block_len, width)
    _, kernel_back = jax.vjp(lambda kern: kernel_freq(kern, cos_t, sin_t), kernel)
    d_kernel = kernel_back((dk_real, dk_imag))[0]
    dense = [
        grad_norm_gain,
        grad_norm_bias,
        grad_mixer_in,
        grad_mixer_out,
        grad_second_gain,
        grad_second_bias,
        grad_up,
        grad_down,
    ]
    summed = sum_everywhere([d_kernel] + dense)
    filter_grads = filter_back(summed[0])
    dense_sums = summed[1:]
    return (
        output,
        grad_inputs,
        dense_sums[0],
        dense_sums[1],
        dense_sums[2],
        filter_grads[0],
        filter_grads[1],
        filter_grads[2],
        filter_grads[3],
        filter_grads[4],
        dense_sums[3],
        dense_sums[4],
        dense_sums[5],
        dense_sums[6],
        dense_sums[7],
    )


SPECS_IN = (P("dp", "seq", None), P("dp")) + (P(),) * 13 + (P("dp", "seq", None),)
SPECS_OUT = (P("dp", "seq", None), P("dp", "seq", None)) + (P(),) * 13


def solution(mesh):
    local = chip_local if (mesh.shape["seq"], mesh.shape["dp"]) == (8, 4) else block_local
    return jax.shard_map(local, mesh=mesh, in_specs=SPECS_IN, out_specs=SPECS_OUT, check_vma=False)
```
